32 devices in a mesh: wide: 8 (over z, x), narrow: 4 (over y, core).
Axes of the slice: x: 2, y: 2, z: 4, core: 2. Of those that a mesh axis runs over, the one named last changes fastest.
Arguments:
- target_in: bfloat16 [12288, 1024], P(('wide', 'narrow')), may hold values from -6 to 6
- memory: bfloat16 [32768, 1024], P(('wide', 'narrow')), may hold values from -6 to 6
- block_rows: int32 [32, 3], P(('wide', 'narrow')), may hold values from 1 to 640, 1024 in all within a row
- pad_rows: int32 [32, 3], P(('wide', 'narrow')), may hold values from 0 to 340
- seq_lengths: int32 [32, 3], P(('wide', 'narrow')), may hold values from 32 to 128
- self_qkv: bfloat16 [1024, 3072], P(('wide', 'narrow')), may hold values from -0.1875 to 0.1875
- self_out: bfloat16 [1024, 1024], P(('wide', 'narrow')), may hold values from -0.75 to 0.75
- cross_query: bfloat16 [1024, 1024], P(('wide', 'narrow')), may hold values from -0.1875 to 0.1875
- cross_kv: bfloat16 [1024, 2048], P(('wide', 'narrow')), may hold values from -0.1875 to 0.1875
- cross_out: bfloat16 [1024, 1024], P(('wide', 'narrow')), may hold values from -0.75 to 0.75
- ffn_in: bfloat16 [1024, 4096], P(('wide', 'narrow')), may hold values from -0.1875 to 0.1875
- ffn_out: bfloat16 [4096, 1024], P(('wide', 'narrow')), may hold values from -0.09375 to 0.09375
- norm_scale: bfloat16 [3, 1024], P(None, ('wide', 'narrow')), may hold values from 0.5 to 1.5
- small_bias: bfloat16 [10, 1024], P(None, ('wide', 'narrow')), may hold values from -2 to 2
- ffn_bias: bfloat16 [4096], P(('wide', 'narrow')), may hold values from -2 to 2
- cotangent: bfloat16 [12288, 1024], P(('wide', 'narrow')), may hold values from -6 to 6
Outputs:
- block_out: bfloat16 [12288, 1024], P(('wide', 'narrow'))
- target_grad: float32 [12288, 1024], P(('wide', 'narrow'))
- memory_grad: float32 [32768, 1024], P(('wide', 'narrow'))
- self_qkv_grad: float32 [1024, 3072], P(('wide', 'narrow'))
- self_out_grad: float32 [1024, 1024], P(('wide', 'narrow'))
- cross_query_grad: float32 [1024, 1024], P(('wide', 'narrow'))
- cross_kv_grad: float32 [1024, 2048], P(('wide', 'narrow'))
- cross_out_grad: float32 [1024, 1024], P(('wide', 'narrow'))
- ffn_in_grad: float32 [1024, 4096], P(('wide', 'narrow'))
- ffn_out_grad: float32 [4096, 1024], P(('wide', 'narrow'))
- norm_scale_grad: float32 [3, 1024], P(None, ('wide', 'narrow'))
- small_bias_grad: float32 [10, 1024], P(None, ('wide', 'narrow'))
- ffn_bias_grad: float32 [4096], P(('wide', 'narrow'))
The draws below stay inside these ranges and needn't reach their ends.
Inputs may be any that keep to these rules, and one draw needn't show every extreme that they name: `block_rows`: each row's 3 blocks together hold its 1024 memory rows.
All inputs are finite; a program needn't handle non-finite values.
Results may differ from the reference program's by a relative error of at most 0.018.
Values may be sent and summed in bfloat16 or wider, within the bound.
No kernel may reach another device: no remote copies, remote signals or barrier semaphores. Data moves between devices by JAX's collectives and lax.ppermute only.
A program may use at most 256 MiB of HBM per device.

```python
import math
import jax
import jax.numpy as jnp
import numpy as np
from jax import lax

D = 1024
FF = 4096
HEADS = 16
HEAD_DIM = 64
SEQ_LEN = 128
SEQ_DEV = 3
MEM_DEV = 1024
TOK_DEV = 384
TOKENS = 12288
MEMS = 32768
BLOCK_MOST = 640
DEVICES = 32


def plant(drawn, key, smallest, high):
    extent = drawn.shape
    place = [jax.random.randint(jax.random.fold_in(key, axis), (), 0, extent[axis]) for axis in range(len(extent))]
    drawn = drawn.at[tuple(place)].set(smallest)
    longest = extent.index(max(extent))
    place[longest] = (place[longest] + 1) % extent[longest]
    return drawn.at[tuple(place)].set(high)


def levels(key, shape, cuts, smallest, top_value):
    def one(dim, shards_of):
        steps = jax.random.uniform(jax.random.fold_in(jax.random.fold_in(key, 6), dim), (shards_of,), jnp.float32, smallest / len(cuts), top_value / len(cuts))
        return jnp.repeat(jnp.exp(steps), shape[dim] // shards_of).reshape((-1,) + (1,) * (len(shape) - dim - 1))

    factor_of = one(*cuts[0])
    for cut in cuts[1:]:
        factor_of = factor_of * one(*cut)
    return factor_of


def length_profile(count, total, limit, slope):
    portions = [(1 << 20) // math.isqrt(standing ** slope) + 1 for standing in range(2, count + 1)]
    spare, counts = total - limit - (count - 1), [1] * (count - 1)
    while spare > 0:
        free = [i for i in range(count - 1) if counts[i] < limit]
        whole, remaining = sum([portions[i] for i in free]), spare
        for i in free:
            addition = min(limit - counts[i], max(1, remaining * portions[i] // whole), spare)
            counts[i] = counts[i] + addition
            spare = spare - addition
    return np.array([limit] + counts)


def uneven(key, number_of, total, reach, skew):
    if number_of == 2:
        one = jax.random.randint(key, (), max(1, total - reach), min(reach, total - 1) + 1)
        return jnp.stack([one, total - one])
    sizes = jnp.asarray(length_profile(number_of, total, reach, skew), jnp.int32)
    twos = (number_of - 1) // 2
    giver, receiver = sizes[1:1 + 2 * twos:2], sizes[2:2 + 2 * twos:2]
    slack = jnp.minimum(giver - 1, reach - receiver)
    moved = jax.random.randint(jax.random.fold_in(key, 1), (twos,), 0, 1 << 20) % (slack + 1)
    sizes = sizes.at[1:1 + 2 * twos:2].set(giver - moved).at[2:2 + 2 * twos:2].set(receiver + moved)
    return sizes[jax.random.permutation(jax.random.fold_in(key, 2), number_of)]


def gaussian(rng, dims, scale, limit, cuts=(), held_as=jnp.bfloat16):
    entries = jax.random.normal(rng, dims, jnp.float32) * scale
    if len(cuts) > 0:
        entries = levels(rng, dims, cuts, -0.22, 0.18) * entries
    return jnp.clip(entries, min=-limit, max=limit).astype(held_as)


def setup_inputs(seed: int = 0) -> dict:
    keys = jax.random.split(jax.random.key(seed), 17)
    return {
        "target_in": gaussian(keys[0], (TOKENS, D), 1.0, 6.0, ((0, 32),)),
        "memory": gaussian(keys[1], (MEMS, D), 1.0, 6.0, ((0, 32),)),
        "block_rows": jax.vmap(lambda own: uneven(own, SEQ_DEV, MEM_DEV, BLOCK_MOST, 1))(jax.random.split(keys[2], DEVICES)).reshape((DEVICES, SEQ_DEV)).astype(jnp.int32),
        "pad_rows": plant(jax.random.randint(keys[3], (DEVICES, SEQ_DEV), 0, MEM_DEV // SEQ_DEV), jax.random.fold_in(keys[3], 1), 0, (MEM_DEV // SEQ_DEV) - 1).astype(jnp.int32),
        "seq_lengths": plant(jax.random.randint(keys[4], (DEVICES, SEQ_DEV), SEQ_LEN // 4, SEQ_LEN + 1), jax.random.fold_in(keys[4], 1), SEQ_LEN // 4, SEQ_LEN).astype(jnp.int32),
        "self_qkv": gaussian(keys[5], (D, 3 * D), D ** -0.5, 0.1875, ((0, 32),)),
        "self_out": gaussian(keys[6], (D, D), (D // 16) ** -0.5, 0.75, ((0, 32),)),
        "cross_query": gaussian(keys[7], (D, D), D ** -0.5, 0.1875, ((0, 32),)),
        "cross_kv": gaussian(keys[8], (D, 2 * D), D ** -0.5, 0.1875, ((0, 32),)),
        "cross_out": gaussian(keys[9], (D, D), (D // 16) ** -0.5, 0.75, ((0, 32),)),
        "ffn_in": gaussian(keys[10], (D, FF), D ** -0.5, 0.1875, ((0, 32),)),
        "ffn_out": gaussian(keys[11], (FF, D), FF ** -0.5, 0.09375, ((0, 32),)),
        "norm_scale": jnp.clip(1.0 + 0.1 * jax.random.normal(keys[12], (3, D), jnp.float32), 0.5, 1.5).astype(jnp.bfloat16),
        "small_bias": gaussian(keys[13], (10, D), 0.3, 2.0, ((1, 32),)),
        "ffn_bias": gaussian(keys[14], (FF,), 0.3, 2.0, ((0, 32),)),
        "cotangent": gaussian(keys[15], (TOKENS, D), 1.0, 6.0, ((0, 32),)),
    }


norm_eps = 1e-05
neg_fill = -1e+30

@jax.custom_vjp
def low(v):
    return lax.optimization_barrier(v.astype(jnp.bfloat16)).astype(jnp.float32)

@jax.custom_vjp
def low_back(v):
    return v

def low_keep(v):
    return (low(v), None)

def low_pass(kept, grad):
    return (grad,)

def back_keep(v):
    return (v, None)

def back_low(kept, grad):
    return (low(grad),)
low.defvjp(low_keep, low_pass)
low_back.defvjp(back_keep, back_low)

def matmul(first, second):
    return jnp.dot(first, second, precision=lax.Precision.HIGHEST, preferred_element_type=jnp.float32)

def build_masks(block_rows, pad_rows, seq_lengths, seq_len, mem_rows):
    block_rows = block_rows.astype(jnp.int32)
    starts = (jnp.cumsum(block_rows) - block_rows).astype(jnp.int32)
    valid = jnp.maximum(block_rows - pad_rows, (block_rows + 1) // 2).astype(jnp.int32)
    places = jnp.arange(mem_rows, dtype=jnp.int32)
    memory_ok = (places[None, :] >= starts[:, None]) & (places[None, :] < (starts + valid)[:, None])
    cross_mask = jnp.repeat(memory_ok, seq_len, axis=0)
    slots = jnp.arange(seq_len, dtype=jnp.int32)
    causal = slots[None, :] <= slots[:, None]
    self_mask = causal[None] & (slots[None, None, :] < seq_lengths.astype(jnp.int32)[:, None, None])
    return (self_mask, cross_mask)

def normalize(values, gain, shift):
    centered = values - lax.optimization_barrier(jnp.mean(values, axis=-1, keepdims=True))
    inverse = lax.rsqrt(lax.optimization_barrier(jnp.mean(centered * centered, axis=-1, keepdims=True)) + norm_eps)
    return centered * inverse * gain + shift

def group_forward(weights, target, memory, block_rows, pad_rows, seq_lengths):
    w_qkv, w_self, w_query, w_pairs, w_cross, w_in, w_out, gains, biases, b_in = weights
    self_mask, cross_mask = build_masks(block_rows, pad_rows, seq_lengths, SEQ_LEN, MEM_DEV)
    width = target.shape[1]
    zeros = jnp.zeros((width,), jnp.float32)
    scale = HEAD_DIM ** (-0.5)
    highest = lax.Precision.HIGHEST
    qkv = low(low_back(matmul(target, w_qkv) + jnp.concatenate([biases[0], zeros, biases[1]])))
    parts = qkv.reshape(-1, SEQ_LEN, 3, HEADS, HEAD_DIM)
    raw = low_back(jnp.einsum('sqhe,skhe->shqk', parts[:, :, 0], parts[:, :, 1], precision=highest) * scale)
    probs = low(jax.nn.softmax(jnp.where(self_mask[:, None], raw, neg_fill), axis=-1))
    context = jnp.einsum('shqk,skhe->sqhe', probs, parts[:, :, 2], precision=highest).reshape(-1, width)
    context = low(low_back(context))
    first = normalize(target + low_back(matmul(context, w_self) + biases[2]), gains[0], biases[7])
    cross_q = low(low_back(matmul(low(first), w_query) + biases[3])).reshape(-1, HEADS, HEAD_DIM)
    pairs = low(low_back(matmul(memory, w_pairs) + jnp.concatenate([zeros, biases[4]]))).reshape(-1, 2, HEADS, HEAD_DIM)
    raw = low_back(jnp.einsum('qhe,khe->hqk', cross_q, pairs[:, 0], precision=highest) * scale)
    probs = low(jax.nn.softmax(jnp.where(cross_mask[None], raw, neg_fill), axis=-1))
    context = jnp.einsum('hqk,khe->qhe', probs, pairs[:, 1], precision=highest).reshape(-1, width)
    context = low(low_back(context))
    second = normalize(first + low_back(matmul(context, w_cross) + biases[5]), gains[1], biases[8])
    hidden = low(jax.nn.gelu(low_back(matmul(low(second), w_in) + b_in), approximate=False))
    return normalize(second + low_back(matmul(hidden, w_out) + biases[6]), gains[2], biases[9])

def reference(target_in, memory, block_rows, pad_rows, seq_lengths, self_qkv, self_out, cross_query, cross_kv, cross_out, ffn_in, ffn_out, norm_scale, small_bias, ffn_bias, cotangent):
    width = target_in.shape[1]
    params = tuple((weight.astype(jnp.float32) for weight in (self_qkv, self_out, cross_query, cross_kv, cross_out, ffn_in, ffn_out, norm_scale, small_bias, ffn_bias)))
    targets = target_in.astype(jnp.float32).reshape(-1, TOK_DEV, width)
    memories = memory.astype(jnp.float32).reshape(-1, MEM_DEV, width)

    def forward(weights, target_all, memory_all):

        def one_group(item):
            target, mem, rows, pads, lengths = item
            return group_forward(weights, target, mem, rows, pads, lengths)
        return lax.map(jax.checkpoint(one_group), (target_all, memory_all, block_rows, pad_rows, seq_lengths))
    outputs, pullback = jax.vjp(forward, params, targets, memories)
    weight_grads, target_grad, memory_grad = pullback(cotangent.astype(jnp.float32).reshape(outputs.shape))
    return (outputs.reshape(-1, width).astype(jnp.bfloat16), target_grad.reshape(-1, width), memory_grad.reshape(-1, width), weight_grads[0], weight_grads[1], weight_grads[2], weight_grads[3], weight_grads[4], weight_grads[5], weight_grads[6], weight_grads[7], weight_grads[8], weight_grads[9])
```

```python
import jax
import jax.numpy as jnp
from jax import lax
from jax.sharding import PartitionSpec as P

HEADS = 16
HEAD_DIM = 64
SEQ_LEN = 128


norm_eps = 1e-05
neg_fill = -1e30


def matmul(first, second):
    return jnp.dot(first, second, preferred_element_type=jnp.float32)


def inner_rows(first, second):
    return lax.dot_general(
        first, second, (((0,), (0,)), ((), ())), preferred_element_type=jnp.float32
    )


def inner_cols(first, second):
    return lax.dot_general(
        first, second, (((1,), (1,)), ((), ())), preferred_element_type=jnp.float32
    )


def column_sums(values):
    return jnp.sum(values.astype(jnp.float32), axis=0)


def exact_gelu(values):
    return jax.nn.gelu(values, approximate=False)


def build_masks(block_rows, pad_rows, seq_lengths, seq_len, mem_rows):
    count = block_rows.shape[0]
    before = jnp.arange(count)[None, :] < jnp.arange(count)[:, None]
    starts = jnp.sum(jnp.where(before, block_rows[None, :], 0), axis=1)
    valid = jnp.maximum(block_rows - pad_rows, (block_rows + 1) // 2)
    places = jnp.arange(mem_rows, dtype=jnp.int32)
    memory_ok = (places[None, :] >= starts[:, None]) & (places[None, :] < (starts + valid)[:, None])
    cross_mask = jnp.repeat(memory_ok, seq_len, axis=0)
    slots = jnp.arange(seq_len, dtype=jnp.int32)
    causal = slots[None, :] <= slots[:, None]
    self_mask = causal[None] & (slots[None, None, :] < seq_lengths[:, None, None])
    return (self_mask, cross_mask)


def normalize(values, gain, shift):
    centered = values - jnp.mean(values, axis=-1, keepdims=True)
    inverse = lax.rsqrt(jnp.mean(centered * centered, axis=-1, keepdims=True) + norm_eps)
    unit = centered * inverse
    return (unit * gain + shift, unit, inverse)


def normalize_back(grad, unit, inverse, gain):
    scaled = grad * gain
    inner = (
        scaled
        - jnp.mean(scaled, axis=-1, keepdims=True)
        - unit * jnp.mean(scaled * unit, axis=-1, keepdims=True)
    )
    return (inverse * inner, jnp.sum(grad * unit, axis=0), jnp.sum(grad, axis=0))


def softmax_rows(scores):
    top = jnp.max(scores, axis=-1, keepdims=True)
    shifted = jnp.exp(scores - top)
    total = jnp.sum(shifted, axis=-1, keepdims=True)
    return (shifted / total, top + jnp.log(total))


def self_split(qkv):
    tokens = qkv.shape[0]
    parts = qkv.reshape(tokens // SEQ_LEN, SEQ_LEN, 3, HEADS, HEAD_DIM)
    return (parts[:, :, 0], parts[:, :, 1], parts[:, :, 2])


def self_scores(queries, keys, mask):
    raw = jnp.einsum(
        "sqhe,skhe->shqk", queries, keys, preferred_element_type=jnp.float32
    ) * HEAD_DIM ** (-0.5)
    return jnp.where(mask[:, None], raw, neg_fill)


def self_forward(qkv, mask):
    queries, keys, values = self_split(qkv)
    probs, summary = softmax_rows(self_scores(queries, keys, mask))
    context = jnp.einsum(
        "shqk,skhe->sqhe", probs.astype(jnp.bfloat16), values, preferred_element_type=jnp.float32
    )
    return (context.reshape(qkv.shape[0], -1).astype(jnp.bfloat16), summary)


def self_backward(qkv, context_grad, summary, mask):
    queries, keys, values = self_split(qkv)
    scale = HEAD_DIM ** (-0.5)
    tokens = qkv.shape[0]
    probs = jnp.exp(self_scores(queries, keys, mask) - summary)
    grad_heads = context_grad.reshape(queries.shape)
    value_grad = jnp.einsum(
        "shqk,sqhe->skhe",
        probs.astype(jnp.bfloat16),
        grad_heads,
        preferred_element_type=jnp.float32,
    )
    prob_grad = jnp.einsum(
        "sqhe,skhe->shqk", grad_heads, values, preferred_element_type=jnp.float32
    )
    score_grad = (probs * (prob_grad - jnp.sum(probs * prob_grad, axis=-1, keepdims=True))).astype(
        jnp.bfloat16
    )
    query_grad = (
        jnp.einsum("shqk,skhe->sqhe", score_grad, keys, preferred_element_type=jnp.float32) * scale
    )
    key_grad = (
        jnp.einsum("shqk,sqhe->skhe", score_grad, queries, preferred_element_type=jnp.float32)
        * scale
    )
    joined = [
        query_grad.reshape(tokens, -1),
        key_grad.reshape(tokens, -1),
        value_grad.reshape(tokens, -1),
    ]
    return jnp.concatenate(joined, axis=1).astype(jnp.bfloat16)


def head_groups(matrix, parts):
    rows = matrix.shape[0]
    groups = HEADS // min(HEADS, 4)
    shaped = matrix.reshape(rows, parts, groups, HEADS // groups, HEAD_DIM)
    return jnp.transpose(shaped, (1, 2, 0, 3, 4))


def from_groups(stacked):
    rows = stacked.shape[1]
    return jnp.transpose(stacked, (1, 0, 2, 3)).reshape(rows, -1)


def cross_scores(queries, keys, mask):
    raw = jnp.einsum(
        "qhe,khe->hqk", queries, keys, preferred_element_type=jnp.float32
    ) * HEAD_DIM ** (-0.5)
    return jnp.where(mask[None], raw, neg_fill)


def cross_forward(cross_q, cross_pairs, mask):
    queries = head_groups(cross_q, 1)[0]
    pairs = head_groups(cross_pairs, 2)

    def one_group(item):
        group_q, group_k, group_v = item
        probs, summary = softmax_rows(cross_scores(group_q, group_k, mask))
        context = jnp.einsum(
            "hqk,khe->qhe", probs.astype(jnp.bfloat16), group_v, preferred_element_type=jnp.float32
        )
        return (context.astype(jnp.bfloat16), summary)

    context, summary = lax.map(one_group, (queries, pairs[0], pairs[1]))
    return (from_groups(context), summary)


def cross_backward(cross_q, cross_pairs, context_grad, summary, mask):
    queries = head_groups(cross_q, 1)[0]
    pairs = head_groups(cross_pairs, 2)
    grads = head_groups(context_grad, 1)[0]
    scale = HEAD_DIM ** (-0.5)

    def one_group(item):
        group_q, group_k, group_v, grad_heads, group_summary = item
        probs = jnp.exp(cross_scores(group_q, group_k, mask) - group_summary)
        value_grad = jnp.einsum(
            "hqk,qhe->khe",
            probs.astype(jnp.bfloat16),
            grad_heads,
            preferred_element_type=jnp.float32,
        )
        prob_grad = jnp.einsum(
            "qhe,khe->hqk", grad_heads, group_v, preferred_element_type=jnp.float32
        )
        score_grad = (
            probs * (prob_grad - jnp.sum(probs * prob_grad, axis=-1, keepdims=True))
        ).astype(jnp.bfloat16)
        query_grad = (
            jnp.einsum("hqk,khe->qhe", score_grad, group_k, preferred_element_type=jnp.float32)
            * scale
        )
        key_grad = (
            jnp.einsum("hqk,qhe->khe", score_grad, group_q, preferred_element_type=jnp.float32)
            * scale
        )
        return (
            query_grad.astype(jnp.bfloat16),
            key_grad.astype(jnp.bfloat16),
            value_grad.astype(jnp.bfloat16),
        )

    query_grad, key_grad, value_grad = lax.map(
        one_group, (queries, pairs[0], pairs[1], grads, summary)
    )
    return (
        from_groups(query_grad),
        jnp.concatenate([from_groups(key_grad), from_groups(value_grad)], axis=1),
    )


def attention_back(saved, weights, second_total, third_norm):
    (
        target_in,
        memory,
        qkv,
        self_context,
        self_summary,
        self_mask,
        first_low,
        first_unit,
        first_inverse,
        cross_q,
        cross_pairs,
        cross_context,
        cross_summary,
        cross_mask,
        second_unit,
        second_inverse,
    ) = saved
    w_qkv, w_self, w_query, w_pairs, w_cross, gains, biases = weights
    width = target_in.shape[1]
    second_grad, scale_two, shift_two = normalize_back(
        second_total, second_unit, second_inverse, gains[1]
    )
    cross_branch = second_grad.astype(jnp.bfloat16)
    cross_out_grad = inner_rows(cross_context, cross_branch)
    context_grad = inner_cols(cross_branch, w_cross).astype(jnp.bfloat16)
    query_delta, pair_delta = cross_backward(
        cross_q, cross_pairs, context_grad, cross_summary, cross_mask
    )
    cross_query_grad = inner_rows(first_low, query_delta)
    cross_kv_grad = inner_rows(memory, pair_delta)
    memory_grad = inner_cols(pair_delta, w_pairs)
    first_total = second_grad + inner_cols(query_delta, w_query)
    first_grad, scale_one, shift_one = normalize_back(
        first_total, first_unit, first_inverse, gains[0]
    )
    self_branch = first_grad.astype(jnp.bfloat16)
    self_out_grad = inner_rows(self_context, self_branch)
    self_context_grad = inner_cols(self_branch, w_self).astype(jnp.bfloat16)
    qkv_delta = self_backward(qkv, self_context_grad, self_summary, self_mask)
    self_qkv_grad = inner_rows(target_in, qkv_delta)
    target_grad = first_grad + inner_cols(qkv_delta, w_qkv)
    scale_three, shift_three, out_bias = third_norm
    norm_grad = jnp.stack([scale_one, scale_two, scale_three])
    bias_grad = jnp.stack(
        [
            column_sums(qkv_delta[:, :width]),
            column_sums(qkv_delta[:, 2 * width :]),
            column_sums(self_branch),
            column_sums(query_delta),
            column_sums(pair_delta[:, width:]),
            column_sums(cross_branch),
            out_bias,
            shift_one,
            shift_two,
            shift_three,
        ]
    )
    return (
        target_grad,
        memory_grad,
        (
            self_qkv_grad,
            self_out_grad,
            cross_query_grad,
            cross_kv_grad,
            cross_out_grad,
            norm_grad,
            bias_grad,
        ),
    )


def exchange(values, bit):
    count = lax.axis_size(("wide", "narrow"))
    return lax.ppermute(
        values, ("wide", "narrow"), [(i, i ^ (1 << bit)) for i in range(count)]
    )


class Scatter:
    def __init__(self, values, bits):
        self.values = values
        self.bits = bits

    def pick(self, bit, other):
        me = lax.axis_index(("wide", "narrow"))
        mine = (me >> bit) & 1
        axis = self.bits.index(bit)
        return lax.dynamic_index_in_dim(
            self.values, 1 - mine if other else mine, axis, keepdims=False
        )

    def step(self, bit):
        arrived = exchange(self.pick(bit, True), bit)
        kept = self.pick(bit, False)
        total = kept.astype(jnp.float32) + arrived.astype(jnp.float32)
        return Scatter(total.astype(jnp.bfloat16), [b for b in self.bits if b != bit])


def scatter_sum(parts):
    count = lax.axis_size(("wide", "narrow"))
    bits = list(range(count.bit_length() - 1))[::-1]
    split = (2,) * len(bits)
    joined = jnp.concatenate([p.astype(jnp.bfloat16) for p in parts], axis=-1)
    first = Scatter(joined.reshape(split + joined.shape[1:]), bits).step(0)
    half = joined.shape[-1] // 256 * 128
    left = Scatter(first.values[..., :half], first.bits)
    right = Scatter(first.values[..., half:], first.bits)
    left = left.step(2).step(1)
    right = right.step(1).step(2)
    rest = Scatter(jnp.concatenate([left.values, right.values], axis=-1), left.bits)
    for bit in rest.bits[::-1]:
        rest = rest.step(bit)
    return rest.values.astype(jnp.float32)


def body(
    target_in,
    memory,
    block_rows,
    pad_rows,
    seq_lengths,
    self_qkv,
    self_out,
    cross_query,
    cross_kv,
    cross_out,
    ffn_in,
    ffn_out,
    norm_scale,
    small_bias,
    ffn_bias,
    cotangent,
):
    axes = ("wide", "narrow")
    width = target_in.shape[1]
    owned = self_qkv.shape[0]
    pack = jnp.concatenate([norm_scale.T, small_bias.T, ffn_bias.reshape(owned, -1)], axis=1)
    small_cols = pack.shape[1]
    pack = jnp.pad(pack, ((0, 0), (0, -small_cols % 128)))
    attn = lax.all_gather(
        jnp.concatenate([self_qkv, self_out, cross_query, cross_kv, cross_out, pack], axis=1),
        axes,
        axis=0,
        tiled=True,
    )
    attn_full = (
        attn[:, : 3 * width],
        attn[:, 3 * width : 4 * width],
        attn[:, 4 * width : 5 * width],
        attn[:, 5 * width : 7 * width],
        attn[:, 7 * width : 8 * width],
    )
    small = attn[:, 8 * width : 8 * width + small_cols].astype(jnp.float32)
    gains = small[:, :3].T
    biases = small[:, 3:13].T
    in_bias = small[:, 13:].reshape(-1)
    w_in = lax.all_gather(ffn_in, axes, axis=0, tiled=True)
    w_out = lax.all_gather(ffn_out, axes, axis=0, tiled=True)
    self_mask, cross_mask = build_masks(
        block_rows[0], pad_rows[0], seq_lengths[0], SEQ_LEN, memory.shape[0]
    )
    zeros = jnp.zeros((width,), jnp.float32)
    w_qkv, w_self, w_query, w_pairs, w_cross = attn_full
    qkv = (matmul(target_in, w_qkv) + jnp.concatenate([biases[0], zeros, biases[1]])).astype(
        jnp.bfloat16
    )
    self_context, self_summary = self_forward(qkv, self_mask)
    first, first_unit, first_inverse = normalize(
        target_in.astype(jnp.float32) + matmul(self_context, w_self) + biases[2],
        gains[0],
        biases[7],
    )
    first_low = first.astype(jnp.bfloat16)
    cross_q = (matmul(first_low, w_query) + biases[3]).astype(jnp.bfloat16)
    cross_pairs = (matmul(memory, w_pairs) + jnp.concatenate([zeros, biases[4]])).astype(
        jnp.bfloat16
    )
    cross_context, cross_summary = cross_forward(cross_q, cross_pairs, cross_mask)
    second, second_unit, second_inverse = normalize(
        first + matmul(cross_context, w_cross) + biases[5], gains[1], biases[8]
    )
    second_low = second.astype(jnp.bfloat16)
    activation, gelu_back = jax.vjp(exact_gelu, matmul(second_low, w_in) + in_bias)
    hidden = activation.astype(jnp.bfloat16)
    third, third_unit, third_inverse = normalize(
        second + matmul(hidden, w_out) + biases[6], gains[2], biases[9]
    )
    block_out = third.astype(jnp.bfloat16)
    back_weights = attn_full + (gains, biases)
    third_grad, scale_three, shift_three = normalize_back(
        cotangent.astype(jnp.float32), third_unit, third_inverse, gains[2]
    )
    out_grad = third_grad.astype(jnp.bfloat16)
    ffn_out_grad = inner_rows(hidden, out_grad)
    pre_grad = gelu_back(inner_cols(out_grad, w_out))[0].astype(jnp.bfloat16)
    ffn_in_grad = inner_rows(second_low, pre_grad)
    ffn_bias_grad = column_sums(pre_grad)
    second_total = third_grad + inner_cols(pre_grad, w_in)
    third_norm = (scale_three, shift_three, column_sums(out_grad))
    saved = (
        target_in,
        memory,
        qkv,
        self_context,
        self_summary,
        self_mask,
        first_low,
        first_unit,
        first_inverse,
        cross_q,
        cross_pairs,
        cross_context,
        cross_summary,
        cross_mask,
        second_unit,
        second_inverse,
    )
    target_grad, memory_grad, attn_grads = attention_back(
        saved, back_weights, second_total, third_norm
    )
    (
        self_qkv_grad,
        self_out_grad,
        cross_query_grad,
        cross_kv_grad,
        cross_out_grad,
        norm_grad,
        bias_grad,
    ) = attn_grads
    small_grad = jnp.concatenate(
        [norm_grad.T, bias_grad.T, ffn_bias_grad.reshape(width, -1)], axis=1
    )
    small_grad = jnp.pad(small_grad, ((0, 0), (0, -small_cols % 128)))
    n = lax.axis_size(axes)
    ffn_shard = scatter_sum([ffn_in_grad.reshape(n, owned, -1), ffn_out_grad.reshape(n, owned, -1)])
    cross_shard = scatter_sum(
        [x.reshape(n, owned, -1) for x in (cross_query_grad, cross_kv_grad, cross_out_grad)]
    )
    self_shard = scatter_sum(
        [x.reshape(n, owned, -1) for x in (self_qkv_grad, self_out_grad, small_grad)]
    )
    hidden_cols = ffn_in.shape[1]
    small_shard = self_shard[:, 4 * width : 4 * width + small_cols]
    return (
        block_out,
        target_grad,
        memory_grad,
        self_shard[:, : 3 * width],
        self_shard[:, 3 * width : 4 * width],
        cross_shard[:, :width],
        cross_shard[:, width : 3 * width],
        cross_shard[:, 3 * width :],
        ffn_shard[:, :hidden_cols],
        ffn_shard[:, hidden_cols:].reshape(ffn_out.shape),
        small_shard[:, :3].T,
        small_shard[:, 3:13].T,
        small_shard[:, 13:].reshape(-1),
    )


def solution(mesh):
    in_specs = (
        P(("wide", "narrow"), None),
        P(("wide", "narrow"), None),
        P(("wide", "narrow"), None),
        P(("wide", "narrow"), None),
        P(("wide", "narrow"), None),
        P(("wide", "narrow"), None),
        P(("wide", "narrow"), None),
        P(("wide", "narrow"), None),
        P(("wide", "narrow"), None),
        P(("wide", "narrow"), None),
        P(("wide", "narrow"), None),
        P(("wide", "narrow"), None),
        P(None, ("wide", "narrow")),
        P(None, ("wide", "narrow")),
        P(("wide", "narrow")),
        P(("wide", "narrow"), None),
    )
    out_specs = (
        P(("wide", "narrow"), None),
        P(("wide", "narrow"), None),
        P(("wide", "narrow"), None),
        P(("wide", "narrow"), None),
        P(("wide", "narrow"), None),
        P(("wide", "narrow"), None),
        P(("wide", "narrow"), None),
        P(("wide", "narrow"), None),
        P(("wide", "narrow"), None),
        P(("wide", "narrow"), None),
        P(None, ("wide", "narrow")),
        P(None, ("wide", "narrow")),
        P(("wide", "narrow")),
    )
    return jax.shard_map(body, mesh=mesh, in_specs=in_specs, out_specs=out_specs, check_vma=False)
```

```python
import functools

import jax
import jax.numpy as jnp
from jax import lax
from jax.experimental import pallas as pl
from jax.experimental.pallas import tpu as pltpu
from jax.sharding import PartitionSpec as P

HEADS = 16
HEAD_DIM = 64
SEQ_LEN = 128
PAIRS = HEADS // 2
neg_fill = -1e30
AXES = ("wide", "narrow")
vmem = pl.BlockSpec(memory_space=pltpu.VMEM)
smem = pl.BlockSpec(memory_space=pltpu.SMEM)
anywhere = pl.BlockSpec(memory_space=pl.ANY)
norm_eps = 1e-05


def kernel_params(megabytes):
    return pltpu.CompilerParams(vmem_limit_bytes=megabytes << 20)


def cost(flops, megabytes, transcendentals=0):
    return pl.CostEstimate(
        flops=int(flops), bytes_accessed=int(megabytes * 2**20), transcendentals=int(transcendentals)
    )


def matmul(first, second):
    return jnp.dot(first, second, preferred_element_type=jnp.float32)


def inner_cols(first, second):
    return lax.dot_general(
        first, second, (((1,), (1,)), ((), ())), preferred_element_type=jnp.float32
    )


def column_sums(values):
    return jnp.sum(values.astype(jnp.float32), axis=0)


def memory_bounds(block_rows, pad_rows):
    count = block_rows.shape[0]
    before = jnp.arange(count)[None, :] < jnp.arange(count)[:, None]
    starts = jnp.sum(jnp.where(before, block_rows[None, :], 0), axis=1)
    valid = jnp.maximum(block_rows - pad_rows, (block_rows + 1) // 2)
    return jnp.stack([starts, starts + valid])


def dot(first, second, contract):
    return lax.dot_general(
        first, second, ((contract[:1], contract[1:]), ((), ())), preferred_element_type=jnp.float32
    )


def cols(pair, base=0):
    return slice((base + pair) * 128, (base + pair + 1) * 128)


def split_heads(block):
    low = lax.broadcasted_iota(jnp.int32, block.shape, 1) < HEAD_DIM
    zero = jnp.zeros_like(block)
    return jnp.concatenate([jnp.where(low, block, zero), jnp.where(low, zero, block)], axis=0)


def join_heads(stacked):
    low = lax.broadcasted_iota(jnp.int32, (SEQ_LEN, 128), 1) < HEAD_DIM
    return jnp.where(low, stacked[:SEQ_LEN], stacked[SEQ_LEN:])


def join_heads_t(stacked):
    both = jnp.concatenate([stacked[:HEAD_DIM, :SEQ_LEN], stacked[HEAD_DIM:, SEQ_LEN:]], axis=0)
    return both.T


def cross_mask(tile, low, high):
    rows = tile * 128 + lax.broadcasted_iota(jnp.int32, (128, 2 * SEQ_LEN), 0)
    return (rows >= low) & (rows < high)


def cross_forward_kernel(bound, q, pairs, *rest, extra):
    context, summary, stack, scores, top, total, acc = rest[extra:]

    def sequence(s, carry):
        low, high = bound[0, s], bound[1, s]
        first, last = low // 128, (high + 127) // 128
        rows = pl.ds(pl.multiple_of(s * SEQ_LEN, SEQ_LEN), SEQ_LEN)
        for p in range(PAIRS):
            stack[p] = split_heads(q[rows, cols(p)] * jnp.bfloat16(HEAD_DIM**-0.5))
        top[...] = jnp.full_like(top, neg_fill)
        total[...] = jnp.zeros_like(total)
        acc[...] = jnp.zeros_like(acc)

        def one(t, carry):
            keys = pl.ds(pl.multiple_of(t * 128, 128), 128)
            ok = cross_mask(t, low, high)
            for p in range(PAIRS):
                raw = jnp.where(ok, dot(pairs[keys, cols(p)], stack[p], (1, 1)), neg_fill)
                scores[t, p] = raw
                top[p] = jnp.maximum(top[p], jnp.max(raw, axis=0, keepdims=True))
            return carry

        lax.fori_loop(first, last, one, 0)

        def two(t, carry):
            keys = pl.ds(pl.multiple_of(t * 128, 128), 128)
            for p in range(PAIRS):
                weights = jnp.exp(scores[t, p] - top[p])
                total[p] += jnp.sum(weights, axis=0, keepdims=True)
                acc[p] += dot(pairs[keys, cols(p, PAIRS)], weights.astype(jnp.bfloat16), (0, 0))
            return carry

        lax.fori_loop(first, last, two, 0)
        for p in range(PAIRS):
            context[rows, cols(p)] = join_heads_t(acc[p] / total[p]).astype(jnp.bfloat16)
            summary[s, p] = top[p] + jnp.log(total[p])
        return carry

    lax.fori_loop(0, bound.shape[1], sequence, 0)


def cross_backward_kernel(bound, q, pairs, grad, summary, *rest, extra):
    q_grad, pair_grad, stack, grads, probs, prob_grads, delta, acc, pair_acc = rest[extra:]
    pair_acc[...] = jnp.zeros_like(pair_acc)
    scale = HEAD_DIM**-0.5

    def sequence(s, carry):
        low, high = bound[0, s], bound[1, s]
        first, last = low // 128, (high + 127) // 128
        rows = pl.ds(pl.multiple_of(s * SEQ_LEN, SEQ_LEN), SEQ_LEN)
        for p in range(PAIRS):
            stack[p] = split_heads(q[rows, cols(p)] * jnp.bfloat16(scale))
            grads[p] = split_heads(grad[rows, cols(p)])
        delta[...] = jnp.zeros_like(delta)
        acc[...] = jnp.zeros_like(acc)

        def one(t, carry):
            keys = pl.ds(pl.multiple_of(t * 128, 128), 128)
            ok = cross_mask(t, low, high)
            for p in range(PAIRS):
                raw = dot(pairs[keys, cols(p)], stack[p], (1, 1))
                weights = jnp.where(ok, jnp.exp(raw - summary[s, p]), 0.0)
                back = dot(pairs[keys, cols(p, PAIRS)], grads[p], (1, 1))
                delta[p] += jnp.sum(weights * back, axis=0, keepdims=True)
                probs[t, p] = weights
                prob_grads[t, p] = back
                pair_acc[keys, cols(p, PAIRS)] += dot(weights.astype(jnp.bfloat16), grads[p], (1, 0))
            return carry

        lax.fori_loop(first, last, one, 0)

        def two(t, carry):
            keys = pl.ds(pl.multiple_of(t * 128, 128), 128)
            for p in range(PAIRS):
                score = (probs[t, p] * (prob_grads[t, p] - delta[p])).astype(jnp.bfloat16)
                pair_acc[keys, cols(p)] += dot(score, stack[p], (1, 0))
                acc[p] += dot(pairs[keys, cols(p)], score, (0, 0))
            return carry

        lax.fori_loop(first, last, two, 0)
        for p in range(PAIRS):
            q_grad[rows, cols(p)] = (join_heads_t(acc[p]) * scale).astype(jnp.bfloat16)
        return carry

    lax.fori_loop(0, bound.shape[1], sequence, 0)
    pair_grad[...] = pair_acc[...].astype(jnp.bfloat16)


def cross_forward(bound, q, pairs, after=()):
    seqs, tiles = bound.shape[1], pairs.shape[0] // 128
    wide = 2 * SEQ_LEN
    return pl.pallas_call(
        functools.partial(cross_forward_kernel, extra=len(after)),
        out_shape=(
            jax.ShapeDtypeStruct(q.shape, jnp.bfloat16),
            jax.ShapeDtypeStruct((seqs, PAIRS, 1, wide), jnp.float32),
        ),
        in_specs=[smem, vmem, vmem] + [anywhere] * len(after),
        out_specs=(vmem, vmem),
        scratch_shapes=[
            pltpu.VMEM((PAIRS, wide, 128), jnp.bfloat16),
            pltpu.VMEM((tiles, PAIRS, 128, wide), jnp.float32),
            pltpu.VMEM((PAIRS, 1, wide), jnp.float32),
            pltpu.VMEM((PAIRS, 1, wide), jnp.float32),
            pltpu.VMEM((PAIRS, 128, wide), jnp.float32),
        ],
        compiler_params=kernel_params(40),
        cost_estimate=pl.CostEstimate(flops=8 * 10**9, bytes_accessed=8 * 2**20, transcendentals=2 * 10**6),
    )(bound, q, pairs, *after)


def cross_backward(bound, q, pairs, grad, summary, after=()):
    seqs, tiles = bound.shape[1], pairs.shape[0] // 128
    wide = 2 * SEQ_LEN
    return pl.pallas_call(
        functools.partial(cross_backward_kernel, extra=len(after)),
        out_shape=(
            jax.ShapeDtypeStruct(q.shape, jnp.bfloat16),
            jax.ShapeDtypeStruct(pairs.shape, jnp.bfloat16),
        ),
        in_specs=[smem, vmem, vmem, vmem, vmem] + [anywhere] * len(after),
        out_specs=(vmem, vmem),
        scratch_shapes=[
            pltpu.VMEM((PAIRS, wide, 128), jnp.bfloat16),
            pltpu.VMEM((PAIRS, wide, 128), jnp.bfloat16),
            pltpu.VMEM((tiles, PAIRS, 128, wide), jnp.float32),
            pltpu.VMEM((tiles, PAIRS, 128, wide), jnp.float32),
            pltpu.VMEM((PAIRS, 1, wide), jnp.float32),
            pltpu.VMEM((PAIRS, 128, wide), jnp.float32),
            pltpu.VMEM(pairs.shape, jnp.float32),
        ],
        compiler_params=kernel_params(56),
        cost_estimate=pl.CostEstimate(flops=16 * 10**9, bytes_accessed=12 * 2**20, transcendentals=2 * 10**6),
    )(bound, q, pairs, grad, summary, *after)


def self_mask(length):
    keys = lax.broadcasted_iota(jnp.int32, (SEQ_LEN, 2 * SEQ_LEN), 0)
    tokens = lax.broadcasted_iota(jnp.int32, (SEQ_LEN, 2 * SEQ_LEN), 1) & (SEQ_LEN - 1)
    return (keys <= tokens) & (keys < length)


def self_forward_kernel(lengths, qkv, *rest, extra):
    context, summary = rest[extra:]

    def sequence(s, carry):
        ok = self_mask(lengths[s])
        rows = pl.ds(pl.multiple_of(s * SEQ_LEN, SEQ_LEN), SEQ_LEN)
        for p in range(PAIRS):
            stack = split_heads(qkv[rows, cols(p)] * jnp.bfloat16(HEAD_DIM**-0.5))
            raw = jnp.where(ok, dot(qkv[rows, cols(p, PAIRS)], stack, (1, 1)), neg_fill)
            top = jnp.max(raw, axis=0, keepdims=True)
            weights = jnp.exp(raw - top)
            total = jnp.sum(weights, axis=0, keepdims=True)
            weights = (weights / total).astype(jnp.bfloat16)
            acc = dot(qkv[rows, cols(p, 2 * PAIRS)], weights, (0, 0))
            context[rows, cols(p)] = join_heads_t(acc).astype(jnp.bfloat16)
            summary[s, p] = top + jnp.log(total)
        return carry

    lax.fori_loop(0, lengths.shape[0], sequence, 0)


def self_backward_kernel(lengths, qkv, grad, summary, *rest, extra):
    [delta_out] = rest[extra:]
    scale = HEAD_DIM**-0.5

    def sequence(s, carry):
        ok = self_mask(lengths[s])
        rows = pl.ds(pl.multiple_of(s * SEQ_LEN, SEQ_LEN), SEQ_LEN)
        for p in range(PAIRS):
            stack = split_heads(qkv[rows, cols(p)] * jnp.bfloat16(scale))
            grads = split_heads(grad[rows, cols(p)])
            keys = qkv[rows, cols(p, PAIRS)]
            raw = dot(keys, stack, (1, 1))
            weights = jnp.where(ok, jnp.exp(raw - summary[s, p]), 0.0)
            back = dot(qkv[rows, cols(p, 2 * PAIRS)], grads, (1, 1))
            delta = jnp.sum(weights * back, axis=0, keepdims=True)
            score = (weights * (back - delta)).astype(jnp.bfloat16)
            value_grad = dot(weights.astype(jnp.bfloat16), grads, (1, 0))
            key_grad = dot(score, stack, (1, 0))
            query_grad = join_heads_t(dot(keys, score, (0, 0))) * scale
            delta_out[rows, cols(p)] = query_grad.astype(jnp.bfloat16)
            delta_out[rows, cols(p, PAIRS)] = key_grad.astype(jnp.bfloat16)
            delta_out[rows, cols(p, 2 * PAIRS)] = value_grad.astype(jnp.bfloat16)
        return carry

    lax.fori_loop(0, lengths.shape[0], sequence, 0)


def self_forward(lengths, qkv, after=()):
    tokens, width = qkv.shape[0], qkv.shape[1] // 3
    return pl.pallas_call(
        functools.partial(self_forward_kernel, extra=len(after)),
        out_shape=(
            jax.ShapeDtypeStruct((tokens, width), jnp.bfloat16),
            jax.ShapeDtypeStruct((lengths.shape[0], PAIRS, 1, 2 * SEQ_LEN), jnp.float32),
        ),
        in_specs=[smem, vmem] + [anywhere] * len(after),
        out_specs=(vmem, vmem),
        compiler_params=kernel_params(24),
        cost_estimate=pl.CostEstimate(flops=2 * 10**9, bytes_accessed=4 * 2**20, transcendentals=10**6),
    )(lengths, qkv, *after)


def self_backward(lengths, qkv, grad, summary, after=()):
    return pl.pallas_call(
        functools.partial(self_backward_kernel, extra=len(after)),
        out_shape=jax.ShapeDtypeStruct(qkv.shape, jnp.bfloat16),
        in_specs=[smem, vmem, vmem, vmem] + [anywhere] * len(after),
        out_specs=vmem,
        compiler_params=kernel_params(24),
        cost_estimate=pl.CostEstimate(flops=4 * 10**9, bytes_accessed=6 * 2**20, transcendentals=10**6),
    )(lengths, qkv, grad, summary, *after)


def normalize(values, gain, shift):
    centered = values - jnp.mean(values, axis=-1, keepdims=True)
    inverse = lax.rsqrt(jnp.mean(centered * centered, axis=-1, keepdims=True) + norm_eps)
    unit = centered * inverse
    return (unit * gain + shift, unit, inverse)


def normalize_back(grad, unit, inverse, gain):
    scaled = grad * gain
    inner = (
        scaled
        - jnp.mean(scaled, axis=-1, keepdims=True)
        - unit * jnp.mean(scaled * unit, axis=-1, keepdims=True)
    )
    return inverse * inner


def sum_rows(*rows):
    stacked = [jnp.sum(r, axis=0, keepdims=True) for r in rows]
    return jnp.concatenate(stacked + [jnp.zeros_like(stacked[0])] * (8 - len(rows)), axis=0)


def deal(core, product, rows, keep, send):
    for i in range(product.shape[0] // (2 * rows)):
        even = product[2 * i * rows : (2 * i + 1) * rows]
        odd = product[(2 * i + 1) * rows : (2 * i + 2) * rows]
        here = slice(i * rows, (i + 1) * rows)
        keep[here, :] = jnp.where(core == 0, even, odd).astype(jnp.bfloat16)
        send[here, :] = jnp.where(core == 0, odd, even).astype(jnp.bfloat16)


def ffn_forward_kernel(
    second, w_in, bias, w_out, cot, vectors, hidden, slope, block_out, third_grad, out_grad, sums, acc, low
):
    step = pl.program_id(0)

    @pl.when(step == 0)
    def _():
        low[...] = second[...].astype(jnp.bfloat16)
        acc[...] = second[...] + vectors[0:1]

    pre = dot(low[...], w_in[...], (1, 0)) + bias[...]
    part = 0.5 + 0.5 * lax.erf(pre * 0.5**0.5)
    active = (pre * part).astype(jnp.bfloat16)
    hidden[...] = active
    slope[...] = (part + pre * jnp.exp(-0.5 * pre * pre) * 0.3989422804014327).astype(jnp.bfloat16)
    acc[...] += dot(active, w_out[...], (1, 0))

    @pl.when(step == pl.num_programs(0) - 1)
    def _():
        gain = vectors[1:2]
        third, unit, inverse = normalize(acc[...], gain, vectors[2:3])
        block_out[...] = third.astype(jnp.bfloat16)
        grad = cot[...].astype(jnp.float32)
        third = normalize_back(grad, unit, inverse, gain)
        third_grad[...] = third
        lower = third.astype(jnp.bfloat16)
        out_grad[...] = lower
        sums[...] = sum_rows(grad * unit, grad, lower.astype(jnp.float32))


def ffn_forward(second, w_in, bias, w_out, cot, vectors):
    tokens, width = second.shape
    hidden = w_in.shape[1]
    chunk = 512
    whole = lambda shape: pl.BlockSpec(shape, lambda j: (0, 0))
    full = whole((tokens, width))
    strip = pl.BlockSpec((tokens, chunk), lambda j: (0, j))
    return pl.pallas_call(
        ffn_forward_kernel,
        grid=(hidden // chunk,),
        out_shape=(
            jax.ShapeDtypeStruct((tokens, hidden), jnp.bfloat16),
            jax.ShapeDtypeStruct((tokens, hidden), jnp.bfloat16),
            jax.ShapeDtypeStruct((tokens, width), jnp.bfloat16),
            jax.ShapeDtypeStruct((tokens, width), jnp.float32),
            jax.ShapeDtypeStruct((tokens, width), jnp.bfloat16),
            jax.ShapeDtypeStruct((8, width), jnp.float32),
        ),
        in_specs=[
            full,
            pl.BlockSpec((width, chunk), lambda j: (0, j)),
            pl.BlockSpec((1, chunk), lambda j: (0, j)),
            pl.BlockSpec((chunk, width), lambda j: (j, 0)),
            full,
            whole((8, width)),
        ],
        out_specs=(strip, strip, full, full, full, whole((8, width))),
        scratch_shapes=[
            pltpu.VMEM((tokens, width), jnp.float32),
            pltpu.VMEM((tokens, width), jnp.bfloat16),
        ],
        compiler_params=kernel_params(40),
        cost_estimate=cost(16e9, 26, 4e6),
    )(second, w_in, bias, w_out, cot, vectors)


def ffn_out_kernel(core, hidden, out_grad, keep, send, *, rows):
    deal(core[0], dot(hidden[...], out_grad[...], (0, 0)), rows, keep, send)


def ffn_out_grads(core, hidden, out_grad, rows):
    tokens, width = out_grad.shape
    size = hidden.shape[1]
    chunk = 1024
    half = jax.ShapeDtypeStruct((size // 2, width), jnp.bfloat16)
    block = pl.BlockSpec((chunk // 2, width), lambda j: (j, 0))
    return pl.pallas_call(
        functools.partial(ffn_out_kernel, rows=rows),
        grid=(size // chunk,),
        out_shape=(half, half),
        in_specs=[
            smem,
            pl.BlockSpec((tokens, chunk), lambda j: (0, j)),
            pl.BlockSpec((tokens, width), lambda j: (0, 0)),
        ],
        out_specs=(block, block),
        compiler_params=kernel_params(40),
        cost_estimate=cost(8e9, 12),
    )(core, hidden, out_grad)


def ffn_backward_kernel(
    core, second, w_in, w_out, slope, third_grad, out_grad, unit, inverse, gain, *rest, extra, rows
):
    keep, send, bias_grad, second_grad, branch, sums, acc, turned = rest[extra:]
    step = pl.program_id(0)

    @pl.when(step == 0)
    def _():
        turned[...] = second[...].astype(jnp.bfloat16).T
        acc[...] = third_grad[...]

    grad = dot(out_grad[...], w_out[...], (1, 1)) * slope[...].astype(jnp.float32)
    lower = grad.astype(jnp.bfloat16)
    bias_grad[...] = jnp.sum(lower.astype(jnp.float32), axis=0, keepdims=True)
    deal(core[0], dot(turned[...], lower, (1, 0)), rows, keep, send)
    acc[...] += dot(lower, w_in[...], (1, 1))

    @pl.when(step == pl.num_programs(0) - 1)
    def _():
        total = acc[...]
        grad = normalize_back(total, unit[...], inverse[...], gain[...])
        second_grad[...] = grad
        lower = grad.astype(jnp.bfloat16)
        branch[...] = lower
        sums[...] = sum_rows(total * unit[...], total, lower.astype(jnp.float32))


def ffn_backward(core, second, w_in, w_out, slope, third_grad, out_grad, unit, inverse, gain, rows, after):
    tokens, width = second.shape
    hidden = w_in.shape[1]
    chunk = 512
    whole = lambda shape: pl.BlockSpec(shape, lambda j: (0, 0))
    full = whole((tokens, width))
    half = jax.ShapeDtypeStruct((width // 2, hidden), jnp.bfloat16)
    block = pl.BlockSpec((width // 2, chunk), lambda j: (0, j))
    return pl.pallas_call(
        functools.partial(ffn_backward_kernel, extra=len(after), rows=rows),
        grid=(hidden // chunk,),
        out_shape=(
            half,
            half,
            jax.ShapeDtypeStruct((1, hidden), jnp.float32),
            jax.ShapeDtypeStruct((tokens, width), jnp.float32),
            jax.ShapeDtypeStruct((tokens, width), jnp.bfloat16),
            jax.ShapeDtypeStruct((8, width), jnp.float32),
        ),
        in_specs=[
            smem,
            full,
            pl.BlockSpec((width, chunk), lambda j: (0, j)),
            pl.BlockSpec((chunk, width), lambda j: (j, 0)),
            pl.BlockSpec((tokens, chunk), lambda j: (0, j)),
            full,
            full,
            full,
            whole((tokens, 1)),
            whole((1, width)),
        ]
        + [anywhere] * len(after),
        out_specs=(block, block, pl.BlockSpec((1, chunk), lambda j: (0, j)), full, full, whole((8, width))),
        scratch_shapes=[
            pltpu.VMEM((tokens, width), jnp.float32),
            pltpu.VMEM((width, tokens), jnp.bfloat16),
        ],
        compiler_params=kernel_params(44),
        cost_estimate=cost(24e9, 32),
    )(core, second, w_in, w_out, slope, third_grad, out_grad, unit, inverse, gain, *after)


def product_grads_kernel(core, *rest, spans, extra, rows, chunk):
    n_left = 1 + max(s[0] for s in spans)
    lefts, rights = rest[:n_left], rest[n_left : n_left + len(spans)]
    small = rest[n_left + len(spans)] if extra[0] else None
    keep, send, *turned = rest[n_left + len(spans) + extra[0] + extra[1] :]
    step = pl.program_id(0)

    @pl.when(step == 0)
    def _():
        for left, out in zip(lefts, turned):
            out[...] = left[...].T

    for left, right, first, count in spans:

        @pl.when((step >= first) & (step < first + count))
        def _(left=left, right=right, first=first):
            columns = pl.ds(pl.multiple_of((step - first) * chunk, chunk), chunk)
            deal(core[0], dot(turned[left][...], rights[right][:, columns], (1, 0)), rows, keep, send)

    if small is not None:

        @pl.when(step == pl.num_programs(0) - 1)
        def _():
            deal(core[0], small[...], rows, keep, send)


def product_grads(core, lefts, rights, rows, chunk, small=None, after=()):
    width = lefts[0].shape[1]
    spans, first = [], 0
    for i, right in enumerate(rights):
        spans.append((i, i, first, right.shape[1] // chunk))
        first += right.shape[1] // chunk
    steps = first + (small is not None)
    half = jax.ShapeDtypeStruct((width // 2, steps * chunk), jnp.bfloat16)
    block = pl.BlockSpec((width // 2, chunk), lambda j: (0, j))
    whole = lambda array: pl.BlockSpec(array.shape, lambda j: (0, 0))
    smalls = [] if small is None else [small]
    return pl.pallas_call(
        functools.partial(
            product_grads_kernel, spans=spans, extra=(len(smalls), len(after)), rows=rows, chunk=chunk
        ),
        grid=(steps,),
        out_shape=(half, half),
        in_specs=[smem] + [whole(x) for x in (*lefts, *rights, *smalls)] + [anywhere] * len(after),
        out_specs=(block, block),
        scratch_shapes=[pltpu.VMEM(x.shape[::-1], jnp.bfloat16) for x in lefts],
        compiler_params=kernel_params(44),
        cost_estimate=cost(sum(2.5 * x.shape[0] * width * y.shape[1] for x, y in zip(lefts, rights)), 20),
    )(core, *lefts, *rights, *smalls, *after)


def exchange(values, bit):
    count = lax.axis_size(AXES)
    return lax.ppermute(values, AXES, [(i, i ^ (1 << bit)) for i in range(count)])


class Chain:
    def __init__(self, parts, rows, order):
        bits = lax.axis_size(AXES).bit_length() - 1
        self.bits = list(range(1, bits))[::-1]
        self.order = [b for b in order if b < bits] + [b for b in range(3, bits)]
        self.parts = []
        for keep, send in parts:
            shape = (2,) * len(self.bits) + (rows, keep.shape[-1])
            self.parts.append((keep.reshape(shape), exchange(send, 0).reshape(shape)))

    def pick(self, bit, other):
        mine = (lax.axis_index(AXES) >> bit) & 1
        take = functools.partial(
            lax.dynamic_index_in_dim,
            index=1 - mine if other else mine,
            axis=self.bits.index(bit),
            keepdims=False,
        )
        sums = [take(a).astype(jnp.float32) + take(b).astype(jnp.float32) for a, b in self.parts]
        return jnp.concatenate(sums, axis=-1).astype(jnp.bfloat16)

    def step(self):
        bit = self.order.pop(0)
        self.send = self.pick(bit, True)
        keep = self.pick(bit, False)
        self.bits = [b for b in self.bits if b != bit]
        self.parts = [(keep, exchange(self.send, bit))]
        return self.send

    def finish(self):
        while self.order:
            self.step()
        [(keep, arrived)] = self.parts
        return keep.astype(jnp.float32) + arrived.astype(jnp.float32)


def body(
    target_in,
    memory,
    block_rows,
    pad_rows,
    seq_lengths,
    self_qkv,
    self_out,
    cross_query,
    cross_kv,
    cross_out,
    ffn_in,
    ffn_out,
    norm_scale,
    small_bias,
    ffn_bias,
    cotangent,
):
    width = target_in.shape[1]
    owned = self_qkv.shape[0]
    core = (lax.axis_index(AXES) & 1).reshape(1)
    pack = jnp.concatenate([norm_scale.T, small_bias.T, ffn_bias.reshape(owned, -1)], axis=1)
    small_cols = pack.shape[1]
    pack = jnp.pad(pack, ((0, 0), (0, -small_cols % 128)))
    attn = lax.all_gather(
        jnp.concatenate([self_qkv, self_out, cross_query, cross_kv, cross_out, pack], axis=1),
        AXES,
        axis=0,
        tiled=True,
    )
    w_qkv = attn[:, : 3 * width]
    w_self = attn[:, 3 * width : 4 * width]
    w_query = attn[:, 4 * width : 5 * width]
    w_pairs = attn[:, 5 * width : 7 * width]
    w_cross = attn[:, 7 * width : 8 * width]
    small = attn[:, 8 * width : 8 * width + small_cols].astype(jnp.float32)
    gains = small[:, :3].T
    biases = small[:, 3:13].T
    in_bias = small[:, 13:].reshape(1, -1)
    w_in = lax.all_gather(ffn_in, AXES, axis=0, tiled=True)
    w_out = lax.all_gather(ffn_out, AXES, axis=0, tiled=True)

    bound = memory_bounds(block_rows[0], pad_rows[0])
    lengths = seq_lengths[0]
    zeros = jnp.zeros((width,), jnp.float32)
    qkv = (matmul(target_in, w_qkv) + jnp.concatenate([biases[0], zeros, biases[1]])).astype(
        jnp.bfloat16
    )
    self_context, self_summary = self_forward(lengths, qkv)
    first, first_unit, first_inverse = normalize(
        target_in.astype(jnp.float32) + matmul(self_context, w_self) + biases[2],
        gains[0],
        biases[7],
    )
    first_low = first.astype(jnp.bfloat16)
    cross_q = (matmul(first_low, w_query) + biases[3]).astype(jnp.bfloat16)
    cross_pairs = (matmul(memory, w_pairs) + jnp.concatenate([zeros, biases[4]])).astype(
        jnp.bfloat16
    )
    cross_context, cross_summary = cross_forward(bound, cross_q, cross_pairs)
    second, second_unit, second_inverse = normalize(
        first + matmul(cross_context, w_cross) + biases[5], gains[1], biases[8]
    )

    vectors = jnp.concatenate([biases[6:7], gains[2:3], biases[9:10], jnp.zeros((5, width), jnp.float32)])
    hidden, slope, block_out, third_grad, out_grad, third_sums = ffn_forward(
        second, w_in, in_bias, w_out, cotangent, vectors
    )
    keep, send = ffn_out_grads(core, hidden, out_grad, ffn_out.shape[0])
    out_chain = Chain([(keep, send)], ffn_out.shape[0], [2, 1])
    keep, send, ffn_bias_grad, second_grad, cross_branch, second_sums = ffn_backward(
        core,
        second,
        w_in,
        w_out,
        slope,
        third_grad,
        out_grad,
        second_unit,
        second_inverse,
        gains[1:2],
        owned,
        after=(send,),
    )
    in_chain = Chain([(keep, send)], owned, [1, 2])

    context_grad = inner_cols(cross_branch, w_cross).astype(jnp.bfloat16)
    query_delta, pair_delta = cross_backward(
        bound,
        cross_q,
        cross_pairs,
        context_grad,
        cross_summary,
        after=(out_chain.step(), in_chain.step()),
    )
    keep, send = product_grads(
        core,
        [first_low, memory, cross_context],
        [query_delta, pair_delta, cross_branch],
        owned,
        512,
    )
    cross_chain = Chain([(keep, send)], owned, [2, 1])

    first_total = second_grad + inner_cols(query_delta, w_query)
    first_grad = normalize_back(first_total, first_unit, first_inverse, gains[0])
    self_branch = first_grad.astype(jnp.bfloat16)
    self_context_grad = inner_cols(self_branch, w_self).astype(jnp.bfloat16)
    qkv_delta = self_backward(lengths, qkv, self_context_grad, self_summary, after=(send,))
    keep, send = product_grads(core, [target_in, self_context], [qkv_delta, self_branch], owned, 512)

    norm_grad = jnp.stack([jnp.sum(first_total * first_unit, axis=0), second_sums[0], third_sums[0]])
    bias_grad = jnp.stack(
        [
            column_sums(qkv_delta[:, :width]),
            column_sums(qkv_delta[:, 2 * width :]),
            column_sums(self_branch),
            column_sums(query_delta),
            column_sums(pair_delta[:, width:]),
            second_sums[2],
            third_sums[2],
            jnp.sum(first_total, axis=0),
            second_sums[1],
            third_sums[1],
        ]
    )
    small_grad = jnp.concatenate(
        [norm_grad.T, bias_grad.T, ffn_bias_grad.reshape(width, -1)], axis=1
    )
    small_grad = jnp.pad(small_grad, ((0, 0), (0, -small_cols % 128))).astype(jnp.bfloat16)
    small_grad = small_grad.reshape(-1, 2, owned, small_grad.shape[1])
    small_keep, small_send = [
        lax.dynamic_index_in_dim(small_grad, i, 1, keepdims=False).reshape(width // 2, -1)
        for i in (core[0], 1 - core[0])
    ]
    self_chain = Chain([(keep, send), (small_keep, small_send)], owned, [1, 2])
    memory_grad = inner_cols(pair_delta, w_pairs)
    target_grad = first_grad + inner_cols(qkv_delta, w_qkv)
    ffn_out_shard = out_chain.finish()
    ffn_in_shard = in_chain.finish()
    cross_shard = cross_chain.finish()
    self_shard = self_chain.finish()
    small_shard = self_shard[:, 4 * width : 4 * width + small_cols]
    return (
        block_out,
        target_grad,
        memory_grad,
        self_shard[:, : 3 * width],
        self_shard[:, 3 * width : 4 * width],
        cross_shard[:, :width],
        cross_shard[:, width : 3 * width],
        cross_shard[:, 3 * width :],
        ffn_in_shard,
        ffn_out_shard,
        small_shard[:, :3].T,
        small_shard[:, 3:13].T,
        small_shard[:, 13:].reshape(-1),
    )


def solution(mesh):
    in_specs = (
        P(("wide", "narrow"), None),
        P(("wide", "narrow"), None),
        P(("wide", "narrow"), None),
        P(("wide", "narrow"), None),
        P(("wide", "narrow"), None),
        P(("wide", "narrow"), None),
        P(("wide", "narrow"), None),
        P(("wide", "narrow"), None),
        P(("wide", "narrow"), None),
        P(("wide", "narrow"), None),
        P(("wide", "narrow"), None),
        P(("wide", "narrow"), None),
        P(None, ("wide", "narrow")),
        P(None, ("wide", "narrow")),
        P(("wide", "narrow")),
        P(("wide", "narrow"), None),
    )
    out_specs = (
        P(("wide", "narrow"), None),
        P(("wide", "narrow"), None),
        P(("wide", "narrow"), None),
        P(("wide", "narrow"), None),
        P(("wide", "narrow"), None),
        P(("wide", "narrow"), None),
        P(("wide", "narrow"), None),
        P(("wide", "narrow"), None),
        P(("wide", "narrow"), None),
        P(("wide", "narrow"), None),
        P(None, ("wide", "narrow")),
        P(None, ("wide", "narrow")),
        P(("wide", "narrow")),
    )
    return jax.shard_map(body, mesh=mesh, in_specs=in_specs, out_specs=out_specs, check_vma=False)
```

```python
import functools

import jax
import jax.numpy as jnp
from jax import lax
from jax.experimental import pallas as pl
from jax.experimental.pallas import tpu as pltpu
from jax.sharding import PartitionSpec as P

HEADS = 16
HEAD_DIM = 64
SEQ_LEN = 128
PAIRS = HEADS // 2
neg_fill = -1e30
AXES = ("wide", "narrow")
vmem = pl.BlockSpec(memory_space=pltpu.VMEM)
smem = pl.BlockSpec(memory_space=pltpu.SMEM)
anywhere = pl.BlockSpec(memory_space=pl.ANY)
norm_eps = 1e-05


def kernel_params(megabytes):
    return pltpu.CompilerParams(vmem_limit_bytes=megabytes << 20)


def cost(flops, megabytes, transcendentals=0):
    return pl.CostEstimate(
        flops=int(10 * flops), bytes_accessed=int(10 * megabytes * 2**20), transcendentals=int(10 * transcendentals)
    )


def matmul(first, second):
    return jnp.dot(first, second, preferred_element_type=jnp.float32)


def inner_cols(first, second):
    return lax.dot_general(
        first, second, (((1,), (1,)), ((), ())), preferred_element_type=jnp.float32
    )


def column_sums(values):
    return jnp.sum(values.astype(jnp.float32), axis=0)


def memory_bounds(block_rows, pad_rows):
    count = block_rows.shape[0]
    before = jnp.arange(count)[None, :] < jnp.arange(count)[:, None]
    starts = jnp.sum(jnp.where(before, block_rows[None, :], 0), axis=1)
    valid = jnp.maximum(block_rows - pad_rows, (block_rows + 1) // 2)
    return jnp.stack([starts, starts + valid])


def dot(first, second, contract):
    return lax.dot_general(
        first, second, ((contract[:1], contract[1:]), ((), ())), preferred_element_type=jnp.float32
    )


def cols(pair, base=0):
    return slice((base + pair) * 128, (base + pair + 1) * 128)


def split_heads(block):
    low = lax.broadcasted_iota(jnp.int32, block.shape, 1) < HEAD_DIM
    zero = jnp.zeros_like(block)
    return jnp.concatenate([jnp.where(low, block, zero), jnp.where(low, zero, block)], axis=0)


def join_heads(stacked):
    low = lax.broadcasted_iota(jnp.int32, (SEQ_LEN, 128), 1) < HEAD_DIM
    return jnp.where(low, stacked[:SEQ_LEN], stacked[SEQ_LEN:])


def join_heads_t(stacked):
    both = jnp.concatenate([stacked[:HEAD_DIM, :SEQ_LEN], stacked[HEAD_DIM:, SEQ_LEN:]], axis=0)
    return both.T


def cross_mask(tile, low, high):
    rows = tile * 128 + lax.broadcasted_iota(jnp.int32, (128, 2 * SEQ_LEN), 0)
    return (rows >= low) & (rows < high)


def cross_forward_kernel(bound, q, pairs, *rest, extra):
    context, summary, stack, scores, top, total, acc = rest[extra:]

    def sequence(s, carry):
        low, high = bound[0, s], bound[1, s]
        first, last = low // 128, (high + 127) // 128
        rows = pl.ds(pl.multiple_of(s * SEQ_LEN, SEQ_LEN), SEQ_LEN)
        for p in range(PAIRS):
            stack[p] = split_heads(q[rows, cols(p)] * jnp.bfloat16(HEAD_DIM**-0.5))
        top[...] = jnp.full_like(top, neg_fill)
        total[...] = jnp.zeros_like(total)
        acc[...] = jnp.zeros_like(acc)

        def one(t, carry):
            keys = pl.ds(pl.multiple_of(t * 128, 128), 128)
            ok = cross_mask(t, low, high)
            for p in range(PAIRS):
                raw = jnp.where(ok, dot(pairs[keys, cols(p)], stack[p], (1, 1)), neg_fill)
                scores[t, p] = raw
                top[p] = jnp.maximum(top[p], jnp.max(raw, axis=0, keepdims=True))
            return carry

        lax.fori_loop(first, last, one, 0)

        def two(t, carry):
            keys = pl.ds(pl.multiple_of(t * 128, 128), 128)
            for p in range(PAIRS):
                weights = jnp.exp(scores[t, p] - top[p])
                total[p] += jnp.sum(weights, axis=0, keepdims=True)
                acc[p] += dot(pairs[keys, cols(p, PAIRS)], weights.astype(jnp.bfloat16), (0, 0))
            return carry

        lax.fori_loop(first, last, two, 0)
        for p in range(PAIRS):
            context[rows, cols(p)] = join_heads_t(acc[p] / total[p]).astype(jnp.bfloat16)
            summary[s, p] = top[p] + jnp.log(total[p])
        return carry

    lax.fori_loop(0, bound.shape[1], sequence, 0)


def cross_backward_kernel(bound, q, pairs, summary, branch, weight, *rest, extra):
    out, sums, grad, stack, grads, probs, prob_grads, delta, acc, pair_acc = rest[extra:]
    pair_acc[...] = jnp.zeros_like(pair_acc)
    scale = HEAD_DIM**-0.5
    (tokens, width), mems = q.shape, pairs.shape[0]
    grad[...] = dot(branch[...], weight[...], (1, 1)).astype(jnp.bfloat16)
    keys_at, values_at = 2 * tokens, 2 * tokens + mems

    def sequence(s, carry):
        low, high = bound[0, s], bound[1, s]
        first, last = low // 128, (high + 127) // 128
        rows = pl.ds(pl.multiple_of(s * SEQ_LEN, SEQ_LEN), SEQ_LEN)
        for p in range(PAIRS):
            stack[p] = split_heads(q[rows, cols(p)] * jnp.bfloat16(scale))
            grads[p] = split_heads(grad[rows, cols(p)])
        delta[...] = jnp.zeros_like(delta)
        acc[...] = jnp.zeros_like(acc)

        def one(t, carry):
            keys = pl.ds(pl.multiple_of(t * 128, 128), 128)
            ok = cross_mask(t, low, high)
            for p in range(PAIRS):
                raw = dot(pairs[keys, cols(p)], stack[p], (1, 1))
                weights = jnp.where(ok, jnp.exp(raw - summary[s, p]), 0.0)
                back = dot(pairs[keys, cols(p, PAIRS)], grads[p], (1, 1))
                delta[p] += jnp.sum(weights * back, axis=0, keepdims=True)
                probs[t, p] = weights
                prob_grads[t, p] = back
                pair_acc[keys, cols(p, PAIRS)] += dot(weights.astype(jnp.bfloat16), grads[p], (1, 0))
            return carry

        lax.fori_loop(first, last, one, 0)

        def two(t, carry):
            keys = pl.ds(pl.multiple_of(t * 128, 128), 128)
            for p in range(PAIRS):
                score = (probs[t, p] * (prob_grads[t, p] - delta[p])).astype(jnp.bfloat16)
                pair_acc[keys, cols(p)] += dot(score, stack[p], (1, 0))
                acc[p] += dot(pairs[keys, cols(p)], score, (0, 0))
            return carry

        lax.fori_loop(first, last, two, 0)
        for p in range(PAIRS):
            out[rows, cols(p)] = (join_heads_t(acc[p]) * scale).astype(jnp.bfloat16)
        return carry

    lax.fori_loop(0, bound.shape[1], sequence, 0)
    out[keys_at:values_at, :] = pair_acc[:, :width].astype(jnp.bfloat16)
    out[values_at:, :] = pair_acc[:, width:].astype(jnp.bfloat16)
    out[tokens:keys_at, :] = branch[...]
    sums[...] = sum_rows(out[:tokens, :].astype(jnp.float32), out[values_at:, :].astype(jnp.float32))


def cross_forward(bound, q, pairs, after=()):
    seqs, tiles = bound.shape[1], pairs.shape[0] // 128
    wide = 2 * SEQ_LEN
    return pl.pallas_call(
        functools.partial(cross_forward_kernel, extra=len(after)),
        out_shape=(
            jax.ShapeDtypeStruct(q.shape, jnp.bfloat16),
            jax.ShapeDtypeStruct((seqs, PAIRS, 1, wide), jnp.float32),
        ),
        in_specs=[smem, vmem, vmem] + [anywhere] * len(after),
        out_specs=(vmem, vmem),
        scratch_shapes=[
            pltpu.VMEM((PAIRS, wide, 128), jnp.bfloat16),
            pltpu.VMEM((tiles, PAIRS, 128, wide), jnp.float32),
            pltpu.VMEM((PAIRS, 1, wide), jnp.float32),
            pltpu.VMEM((PAIRS, 1, wide), jnp.float32),
            pltpu.VMEM((PAIRS, 128, wide), jnp.float32),
        ],
        compiler_params=kernel_params(40),
        cost_estimate=cost(8e9, 8),
    )(bound, q, pairs, *after)


def cross_backward(bound, q, pairs, summary, branch, weights, column, after=()):
    seqs, tiles = bound.shape[1], pairs.shape[0] // 128
    wide = 2 * SEQ_LEN
    width = q.shape[1]
    whole = lambda shape: pl.BlockSpec(shape, lambda i: (0,) * len(shape))
    rows = 2 * pairs.shape[0] + 2 * q.shape[0]
    return pl.pallas_call(
        functools.partial(cross_backward_kernel, extra=len(after)),
        grid=(1,),
        out_shape=(
            jax.ShapeDtypeStruct((rows, width), jnp.bfloat16),
            jax.ShapeDtypeStruct((8, width), jnp.float32),
        ),
        in_specs=[smem]
        + [whole(x.shape) for x in (q, pairs, summary, branch)]
        + [pl.BlockSpec((width, width), lambda i: (0, column))]
        + [anywhere] * len(after),
        out_specs=(whole((rows, width)), whole((8, width))),
        scratch_shapes=[
            pltpu.VMEM(q.shape, jnp.bfloat16),
            pltpu.VMEM((PAIRS, wide, 128), jnp.bfloat16),
            pltpu.VMEM((PAIRS, wide, 128), jnp.bfloat16),
            pltpu.VMEM((tiles, PAIRS, 128, wide), jnp.float32),
            pltpu.VMEM((tiles, PAIRS, 128, wide), jnp.float32),
            pltpu.VMEM((PAIRS, 1, wide), jnp.float32),
            pltpu.VMEM((PAIRS, 128, wide), jnp.float32),
            pltpu.VMEM(pairs.shape, jnp.float32),
        ],
        compiler_params=kernel_params(58),
        cost_estimate=cost(16e9, 12),
    )(bound, q, pairs, summary, branch, weights, *after)


def self_mask(length):
    keys = lax.broadcasted_iota(jnp.int32, (SEQ_LEN, 2 * SEQ_LEN), 0)
    tokens = lax.broadcasted_iota(jnp.int32, (SEQ_LEN, 2 * SEQ_LEN), 1) & (SEQ_LEN - 1)
    return (keys <= tokens) & (keys < length)


def self_forward_kernel(lengths, qkv, *rest, extra):
    context, summary = rest[extra:]

    def sequence(s, carry):
        ok = self_mask(lengths[s])
        rows = pl.ds(pl.multiple_of(s * SEQ_LEN, SEQ_LEN), SEQ_LEN)
        for p in range(PAIRS):
            stack = split_heads(qkv[rows, cols(p)] * jnp.bfloat16(HEAD_DIM**-0.5))
            raw = jnp.where(ok, dot(qkv[rows, cols(p, PAIRS)], stack, (1, 1)), neg_fill)
            top = jnp.max(raw, axis=0, keepdims=True)
            weights = jnp.exp(raw - top)
            total = jnp.sum(weights, axis=0, keepdims=True)
            weights = (weights / total).astype(jnp.bfloat16)
            acc = dot(qkv[rows, cols(p, 2 * PAIRS)], weights, (0, 0))
            context[rows, cols(p)] = join_heads_t(acc).astype(jnp.bfloat16)
            summary[s, p] = top + jnp.log(total)
        return carry

    lax.fori_loop(0, lengths.shape[0], sequence, 0)


def self_backward_kernel(
    lengths, qkv, summary, second_grad, query_delta, w_query, w_self, unit, inverse, gain, *rest, extra
):
    out, sums, first_grad, grad = rest[extra:]
    scale = HEAD_DIM**-0.5
    tokens = qkv.shape[0]
    total = second_grad[...] + dot(query_delta[...], w_query[...], (1, 1))
    first = normalize_back(total, unit[...], inverse[...], gain[...])
    first_grad[...] = first
    branch = first.astype(jnp.bfloat16)
    out[3 * tokens :, :] = branch
    grad[...] = dot(branch, w_self[...], (1, 1)).astype(jnp.bfloat16)

    def sequence(s, carry):
        ok = self_mask(lengths[s])
        rows = pl.ds(pl.multiple_of(s * SEQ_LEN, SEQ_LEN), SEQ_LEN)
        for p in range(PAIRS):
            stack = split_heads(qkv[rows, cols(p)] * jnp.bfloat16(scale))
            grads = split_heads(grad[rows, cols(p)])
            keys = qkv[rows, cols(p, PAIRS)]
            raw = dot(keys, stack, (1, 1))
            weights = jnp.where(ok, jnp.exp(raw - summary[s, p]), 0.0)
            back = dot(qkv[rows, cols(p, 2 * PAIRS)], grads, (1, 1))
            delta = jnp.sum(weights * back, axis=0, keepdims=True)
            score = (weights * (back - delta)).astype(jnp.bfloat16)
            value_grad = dot(weights.astype(jnp.bfloat16), grads, (1, 0))
            key_grad = dot(score, stack, (1, 0))
            query_grad = join_heads_t(dot(keys, score, (0, 0))) * scale
            for i, part in enumerate((query_grad, key_grad, value_grad)):
                place = pl.ds(pl.multiple_of(i * tokens + s * SEQ_LEN, SEQ_LEN), SEQ_LEN)
                out[place, cols(p)] = part.astype(jnp.bfloat16)
        return carry

    lax.fori_loop(0, lengths.shape[0], sequence, 0)
    sums[...] = sum_rows(
        *[out[i * tokens : (i + 1) * tokens, :].astype(jnp.float32) for i in (0, 2, 3)],
        total * unit[...],
        total,
    )


def self_forward(lengths, qkv, after=()):
    tokens, width = qkv.shape[0], qkv.shape[1] // 3
    return pl.pallas_call(
        functools.partial(self_forward_kernel, extra=len(after)),
        out_shape=(
            jax.ShapeDtypeStruct((tokens, width), jnp.bfloat16),
            jax.ShapeDtypeStruct((lengths.shape[0], PAIRS, 1, 2 * SEQ_LEN), jnp.float32),
        ),
        in_specs=[smem, vmem] + [anywhere] * len(after),
        out_specs=(vmem, vmem),
        compiler_params=kernel_params(24),
        cost_estimate=cost(2e9, 4),
    )(lengths, qkv, *after)


def self_backward(
    lengths, qkv, summary, second_grad, cross_delta, late, early, unit, inverse, gain, after=()
):
    tokens, width = second_grad.shape
    whole = lambda shape: pl.BlockSpec(shape, lambda i: (0,) * len(shape))
    full = whole((tokens, width))
    return pl.pallas_call(
        functools.partial(self_backward_kernel, extra=len(after)),
        grid=(1,),
        out_shape=(
            jax.ShapeDtypeStruct((4 * tokens, width), jnp.bfloat16),
            jax.ShapeDtypeStruct((8, width), jnp.float32),
            jax.ShapeDtypeStruct((tokens, width), jnp.float32),
        ),
        in_specs=[
            smem,
            whole(qkv.shape),
            whole(summary.shape),
            full,
            full,
            pl.BlockSpec((width, width), lambda i: (0, 0)),
            pl.BlockSpec((width, width), lambda i: (0, 3)),
            full,
            whole((tokens, 1)),
            whole((1, width)),
        ]
        + [anywhere] * len(after),
        out_specs=(whole((4 * tokens, width)), whole((8, width)), full),
        scratch_shapes=[pltpu.VMEM((tokens, width), jnp.bfloat16)],
        compiler_params=kernel_params(48),
        cost_estimate=cost(6e9, 12),
    )(lengths, qkv, summary, second_grad, cross_delta, late, early, unit, inverse, gain, *after)


def normalize(values, gain, shift):
    centered = values - jnp.mean(values, axis=-1, keepdims=True)
    inverse = lax.rsqrt(jnp.mean(centered * centered, axis=-1, keepdims=True) + norm_eps)
    unit = centered * inverse
    return (unit * gain + shift, unit, inverse)


def normalize_back(grad, unit, inverse, gain):
    scaled = grad * gain
    inner = (
        scaled
        - jnp.mean(scaled, axis=-1, keepdims=True)
        - unit * jnp.mean(scaled * unit, axis=-1, keepdims=True)
    )
    return inverse * inner


def sum_rows(*rows):
    stacked = [jnp.sum(r, axis=0, keepdims=True) for r in rows]
    return jnp.concatenate(stacked + [jnp.zeros_like(stacked[0])] * (8 - len(rows)), axis=0)


def deal(core, turned, rows, keep, send):
    for i in range(turned.shape[0] // (2 * rows)):
        even = turned[2 * i * rows : (2 * i + 1) * rows]
        odd = turned[(2 * i + 1) * rows : (2 * i + 2) * rows]
        here = slice(i * rows, (i + 1) * rows)
        keep(here, jnp.where(core == 0, even, odd).astype(jnp.bfloat16))
        send(here, jnp.where(core == 0, odd, even).astype(jnp.bfloat16))


def into(ref, columns):
    def store(rows, values):
        ref[rows, columns] = values

    return store


def turn_kernel(core, *refs, rows, count):
    arrays, (keep, send) = refs[:count], refs[-2:]
    start = 0
    for array in arrays:
        tokens = array.shape[0]
        columns = slice(start, start + tokens)
        turned = array[...].astype(jnp.float32).T
        deal(core[0], turned, rows, into(keep, columns), into(send, columns))
        start += tokens


def turn(core, arrays, rows, after=()):
    width = arrays[0].shape[1]
    half = jax.ShapeDtypeStruct((width // 2, sum(x.shape[0] for x in arrays)), jnp.bfloat16)
    return pl.pallas_call(
        functools.partial(turn_kernel, rows=rows, count=len(arrays)),
        out_shape=(half, half),
        in_specs=[smem] + [vmem] * len(arrays) + [anywhere] * len(after),
        out_specs=(vmem, vmem),
        compiler_params=kernel_params(32),
        cost_estimate=cost(0, 8),
    )(core, *arrays, *after)


def flat(block):
    values = block[...]
    if values.shape[1] % 16:
        values = values.astype(jnp.float32)
    return values.reshape(-1, values.shape[-1]).astype(jnp.bfloat16)


def weight_blocks(packed, chunk):
    devices, rows, width = packed.shape
    hidden = devices * rows // 2
    strips, owned = width // chunk, rows * width // (2 * hidden)
    return [
        pl.BlockSpec((devices, owned, chunk), lambda j: (0, j // strips, j % strips)),
        pl.BlockSpec((devices * chunk // hidden, rows // 2, width), lambda j: (j, 1, 0)),
    ]


def ffn_forward_kernel(
    core, second, w_in, w_out, bias, cot, vectors, *rest, rows, extra
):
    keep, send, slope, block_out, third_grad, out_grad, sums, acc, low = rest[extra:]

    step = pl.program_id(0)

    @pl.when(step == 0)
    def _():
        low[...] = second[...].astype(jnp.bfloat16)
        acc[...] = second[...] + vectors[0:1]

    pre = dot(low[...], flat(w_in), (1, 0)) + bias[...]
    part = 0.5 + 0.5 * lax.erf(pre * 0.5**0.5)
    active = pre * part
    everything = slice(None)
    deal(core[0], active.T, rows, into(keep, everything), into(send, everything))
    active = active.astype(jnp.bfloat16)
    slope[...] = (part + pre * jnp.exp(-0.5 * pre * pre) * 0.3989422804014327).astype(jnp.bfloat16)
    acc[...] += dot(active, flat(w_out), (1, 0))

    @pl.when(step == pl.num_programs(0) - 1)
    def _():
        gain = vectors[1:2]
        third, unit, inverse = normalize(acc[...], gain, vectors[2:3])
        block_out[...] = third.astype(jnp.bfloat16)
        grad = cot[...].astype(jnp.float32)
        third = normalize_back(grad, unit, inverse, gain)
        third_grad[...] = third
        lower = third.astype(jnp.bfloat16)
        out_grad[...] = lower
        sums[...] = sum_rows(grad * unit, grad, lower.astype(jnp.float32))


def ffn_forward(core, second, packed, bias, cot, vectors, rows, after):
    tokens, width = second.shape
    hidden = packed.shape[0] * packed.shape[1] // 2
    chunk = 512
    whole = lambda shape: pl.BlockSpec(shape, lambda j: (0, 0))
    full = whole((tokens, width))
    strip = pl.BlockSpec((tokens, chunk), lambda j: (0, j))
    turned = pl.BlockSpec((chunk // 2, tokens), lambda j: (j, 0))
    return pl.pallas_call(
        functools.partial(ffn_forward_kernel, rows=rows, extra=len(after)),
        grid=(hidden // chunk,),
        out_shape=(
            jax.ShapeDtypeStruct((hidden // 2, tokens), jnp.bfloat16),
            jax.ShapeDtypeStruct((hidden // 2, tokens), jnp.bfloat16),
            jax.ShapeDtypeStruct((tokens, hidden), jnp.bfloat16),
            jax.ShapeDtypeStruct((tokens, width), jnp.bfloat16),
            jax.ShapeDtypeStruct((tokens, width), jnp.float32),
            jax.ShapeDtypeStruct((tokens, width), jnp.bfloat16),
            jax.ShapeDtypeStruct((8, width), jnp.float32),
        ),
        in_specs=[
            smem,
            full,
            *weight_blocks(packed, chunk),
            pl.BlockSpec((1, chunk), lambda j: (0, j)),
            full,
            whole((8, width)),
        ]
        + [anywhere] * len(after),
        out_specs=(turned, turned, strip, full, full, full, whole((8, width))),
        scratch_shapes=[
            pltpu.VMEM((tokens, width), jnp.float32),
            pltpu.VMEM((tokens, width), jnp.bfloat16),
        ],
        compiler_params=kernel_params(40),
        cost_estimate=cost(16e9, 26, 4e6),
    )(core, second, packed, packed, bias, cot, vectors, *after)


def ffn_backward_kernel(
    w_in, w_out, slope, third_grad, out_grad, unit, inverse, gain, *rest, extra
):
    pre_grad, bias_grad, second_grad, branch, sums, acc = rest[extra:]
    step = pl.program_id(0)

    @pl.when(step == 0)
    def _():
        acc[...] = third_grad[...]

    grad = dot(out_grad[...], flat(w_out), (1, 1)) * slope[...].astype(jnp.float32)
    lower = grad.astype(jnp.bfloat16)
    pre_grad[...] = lower
    bias_grad[...] = jnp.sum(lower.astype(jnp.float32), axis=0, keepdims=True)
    acc[...] += dot(lower, flat(w_in), (1, 1))

    @pl.when(step == pl.num_programs(0) - 1)
    def _():
        total = acc[...]
        grad = normalize_back(total, unit[...], inverse[...], gain[...])
        second_grad[...] = grad
        lower = grad.astype(jnp.bfloat16)
        branch[...] = lower
        sums[...] = sum_rows(total * unit[...], total, lower.astype(jnp.float32))


def ffn_backward(packed, slope, third_grad, out_grad, unit, inverse, gain, after):
    tokens, width = third_grad.shape
    hidden = packed.shape[0] * packed.shape[1] // 2
    chunk = 512
    whole = lambda shape: pl.BlockSpec(shape, lambda j: (0, 0))
    full = whole((tokens, width))
    strip = pl.BlockSpec((tokens, chunk), lambda j: (0, j))
    return pl.pallas_call(
        functools.partial(ffn_backward_kernel, extra=len(after)),
        grid=(hidden // chunk,),
        out_shape=(
            jax.ShapeDtypeStruct((tokens, hidden), jnp.bfloat16),
            jax.ShapeDtypeStruct((1, hidden), jnp.float32),
            jax.ShapeDtypeStruct((tokens, width), jnp.float32),
            jax.ShapeDtypeStruct((tokens, width), jnp.bfloat16),
            jax.ShapeDtypeStruct((8, width), jnp.float32),
        ),
        in_specs=[
            *weight_blocks(packed, chunk),
            strip,
            full,
            full,
            full,
            whole((tokens, 1)),
            whole((1, width)),
        ]
        + [anywhere] * len(after),
        out_specs=(strip, pl.BlockSpec((1, chunk), lambda j: (0, j)), full, full, whole((8, width))),
        scratch_shapes=[pltpu.VMEM((tokens, width), jnp.float32)],
        compiler_params=kernel_params(40),
        cost_estimate=cost(14e9, 26),
    )(packed, packed, slope, third_grad, out_grad, unit, inverse, gain, *after)


def product_kernel(ids, *refs, spans, n_left, rows, chunk, extra):
    lefts, rights = refs[:n_left], refs[n_left : n_left + 2]
    keep_a, send_a, keep_b, send_b, ordered, *wide = refs[n_left + 2 + extra :]
    step = pl.program_id(0)
    blocks = lefts[0].shape[0] // rows
    half = blocks // 2 * rows

    @pl.when(step == 0)
    def _():
        start = 0
        for left in lefts:
            source, size = left, left.shape[1]
            if wide:
                source = wide[0].at[:, pl.ds(0, size)]
                source[...] = left[...].astype(jnp.float32)
            for order, bit in ((0, 1), (1, 0)):
                for i in range(blocks):
                    low, high = i % (1 << bit), (i % (blocks // 2)) >> bit
                    mine = ids[2 - order] if i < blocks // 2 else 1 - ids[2 - order]
                    place = (high << (bit + 1)) + (mine << bit) + low
                    taken = source[pl.ds(pl.multiple_of(place * rows, rows), rows), :]
                    ordered[order, i * rows : (i + 1) * rows, start : start + size] = taken.astype(jnp.bfloat16)
            start += size

    steps = sum(s[-1] for s in spans)
    first = 0
    for mine, other, tokens, row, count in spans:
        a, b = max(first, 0), min(first + count, steps)
        for order, keep, send in ((0, keep_a, send_a), (1, keep_b, send_b)):
            low, high = max(a, order * steps // 2), min(b, (order + 1) * steps // 2)
            if low >= high:
                continue

            @pl.when((step >= low) & (step < high))
            def _(mine=mine, other=other, tokens=tokens, row=row, order=order, keep=keep, send=send, first=first):
                columns = pl.ds(pl.multiple_of((step - first) * chunk, chunk), chunk)
                total = jnp.zeros((2 * half, chunk), jnp.float32)
                for start, right in ((mine, rights[0]), (other, rights[1])):
                    total += dot(
                        ordered[order, :, start : start + tokens], right[row : row + tokens, columns], (1, 0)
                    )
                keep[...] = total[:half].astype(jnp.bfloat16)
                send[...] = total[half:].astype(jnp.bfloat16)

        first += count


def products(ids, lefts, right, spans, rows, chunk, after=()):
    height = lefts[0][0].shape[0]
    columns = sum(s[-1] for s in spans)
    steps = columns // chunk
    spans = [(*s[:-1], s[-1] // chunk) for s in spans]
    part = jax.ShapeDtypeStruct((height // 2, columns // 2), jnp.bfloat16)
    block_a = pl.BlockSpec((height // 2, chunk), lambda j: (0, jnp.minimum(j, steps // 2 - 1)))
    block_b = pl.BlockSpec((height // 2, chunk), lambda j: (0, jnp.maximum(j - steps // 2, 0)))
    whole = lambda array: pl.BlockSpec(array.shape, lambda j: (0, 0))
    tokens = sum(x[1] for x in lefts)
    wide = [pltpu.VMEM((height, max(x[1] for x in lefts)), jnp.float32)] if rows % 16 else []
    taken = [pl.BlockSpec((height, size), lambda j, place=place: (0, place)) for _, size, place in lefts]
    return pl.pallas_call(
        functools.partial(
            product_kernel, spans=spans, n_left=len(lefts), rows=rows, chunk=chunk, extra=len(after)
        ),
        grid=(steps,),
        out_shape=(part,) * 4,
        in_specs=[smem] + taken + [whole(x) for x in right] + [anywhere] * len(after),
        out_specs=(block_a, block_a, block_b, block_b),
        scratch_shapes=[pltpu.VMEM((2, height, tokens), jnp.bfloat16)] + wide,
        compiler_params=kernel_params(48),
        cost_estimate=cost(2.5 * height * tokens * columns / len(lefts), 20),
    )(ids, *[x[0] for x in lefts], *right, *after)


def exchange(values, bit):
    count = lax.axis_size(AXES)
    return lax.ppermute(values, AXES, [(i, i ^ (1 << bit)) for i in range(count)])


def pack_kernel(*refs, places, extra):
    parts, out, sems = refs[: len(places)], refs[-2], refs[-1]
    copies = [
        pltpu.make_async_copy(
            part.at[:, pl.ds(begin, size)],
            out.at[pl.ds(row, part.shape[0]), pl.ds(column, size)],
            sems.at[i],
        )
        for i, (part, (begin, size, row, column)) in enumerate(zip(parts, places))
    ]
    for copy in copies:
        copy.start()
    for copy in copies:
        copy.wait()


def pack_rows(parts, places, shape, after):
    return pl.pallas_call(
        functools.partial(pack_kernel, places=places, extra=len(after)),
        out_shape=jax.ShapeDtypeStruct(shape, jnp.bfloat16),
        in_specs=[anywhere] * (len(parts) + len(after)),
        out_specs=anywhere,
        scratch_shapes=[pltpu.SemaphoreType.DMA((len(parts),))],
        compiler_params=kernel_params(16),
        cost_estimate=cost(0, 4 * shape[0] * shape[1] / 2**20),
    )(*parts, *after)


def place_kernel(*refs, slots, rows):
    me = lax.axis_index(AXES)
    pieces, out, sems = refs[:-2], refs[-2], refs[-1]
    copies = []
    for piece, (start, order) in zip(pieces, slots):
        columns = pl.ds(start, piece.shape[-1])
        for i, slot in enumerate(order):
            place = pl.ds(pl.multiple_of((me ^ slot) * rows, rows), rows)
            copies.append(
                pltpu.make_async_copy(piece.at[i], out.at[place, columns], sems.at[len(copies)])
            )
    for copy in copies:
        copy.start()
    for copy in copies:
        copy.wait()


def join_kernel(mine, arrived, *refs):
    out = refs[-1]
    out[: mine.shape[0]] = mine[...]
    out[mine.shape[0] :] = arrived[...]


def join(mine, arrived, after):
    return pl.pallas_call(
        join_kernel,
        out_shape=jax.ShapeDtypeStruct((2 * mine.shape[0], *mine.shape[1:]), mine.dtype),
        in_specs=[vmem] * 2 + [anywhere] * len(after),
        out_specs=vmem,
        compiler_params=kernel_params(16),
        cost_estimate=cost(0, 8 * mine.size / 2**20),
    )(mine, arrived, *after)


def gather_rows(local, after=()):
    rows, width = local.shape
    count = lax.axis_size(AXES)
    values, order, stages = local[None], [0], []
    for bit in range(count.bit_length() - 2, 2, -1):
        stages.append(exchange(values, bit))
        values = jnp.concatenate([values, stages[-1]], axis=0)
        order = order + [i ^ (1 << bit) for i in order]
    half = width // 256 * 128
    pieces, slots = [], []
    for start, stop, bits in ((0, half, (2, 1)), (half, width, (1, 2))):
        part, listed = values[:, :, start:stop], order
        for bit in bits:
            if bit == bits[-1] and len(after):
                part = join(part, exchange(part, bit), after)
            else:
                part = jnp.concatenate([part, exchange(part, bit)], axis=0)
            listed = listed + [i ^ (1 << bit) for i in listed]
        pieces += [part, exchange(part, 0)]
        slots += [(start, listed), (start, [i ^ 1 for i in listed])]
    placed = pl.pallas_call(
        functools.partial(place_kernel, slots=slots, rows=rows),
        out_shape=jax.ShapeDtypeStruct((count * rows, width), local.dtype),
        in_specs=[anywhere] * len(pieces),
        out_specs=pl.BlockSpec(memory_space=pltpu.HBM),
        scratch_shapes=[pltpu.SemaphoreType.DMA((2 * count,))],
        compiler_params=kernel_params(16),
        cost_estimate=cost(0, 4 * count * rows * width / 2**20),
    )(*pieces)
    return placed, stages


def stage_kernel(ids, *refs, groups, extra):
    inputs = refs[: 2 * sum(count for _, count in groups)]
    outputs = refs[len(inputs) + extra :]
    for g, (bit, count) in enumerate(groups):
        send, keep = outputs[2 * g : 2 * g + 2]
        mine = ids[bit]
        start = 0
        for _ in range(count):
            left, right, *inputs = inputs
            columns = slice(start, start + left.shape[-1])
            for i in range(left.shape[0]):
                for out, b in ((send, 1 - mine), (keep, mine)):
                    total = left[i, b].astype(jnp.float32) + right[i, b].astype(jnp.float32)
                    out[i, :, columns] = total.astype(jnp.bfloat16)
            start += left.shape[-1]


class Chain:
    def __init__(self, ids, parts, rows):
        self.ids, self.rows = ids, rows
        self.rest = list(range(3, ids.shape[0]))
        keep_a, send_a, keep_b, send_b = parts
        self.sends = [send_a, send_b]
        self.groups = [
            [(keep_a, exchange(send_a, 2))],
            [(keep_b, exchange(send_b, 1))],
        ]

    def advance(self, groups, bits, after):
        rows = self.rows
        shaped = [
            a.reshape(-1, 2, rows, a.shape[-1]) for group in groups for part in group for a in part
        ]
        shapes = [
            jax.ShapeDtypeStruct(
                (g[0][0].size // (2 * rows * g[0][0].shape[-1]), rows, sum(p[0].shape[-1] for p in g)),
                jnp.bfloat16,
            )
            for g in groups
            for _ in range(2)
        ]
        outs = pl.pallas_call(
            functools.partial(
                stage_kernel, groups=[(b, len(g)) for b, g in zip(bits, groups)], extra=len(after)
            ),
            out_shape=shapes,
            in_specs=[smem] + [vmem] * len(shaped) + [anywhere] * len(after),
            out_specs=[vmem] * len(shapes),
            compiler_params=kernel_params(24),
            cost_estimate=cost(0, sum(3 * x.size for x in shaped) / 2**20),
        )(self.ids, *shaped, *after)
        self.sends = outs[::2]
        self.groups = [
            [(keep, exchange(send, b))] for send, keep, b in zip(outs[::2], outs[1::2], bits)
        ]
        return outs[1::2]

    def second(self, after=()):
        return self.advance(self.groups, [1, 2], after)

    def third(self, after=()):
        if len(self.groups) == 2:
            self.groups = [self.groups[0] + self.groups[1]]
        return self.advance(self.groups, [self.rest.pop(0)], after)

    def finish(self):
        [[(keep, arrived)]] = self.groups
        return (keep.astype(jnp.float32) + arrived.astype(jnp.float32))[0]


def small_kernel(*refs, rows, count, owned):
    sums, bias, out = refs[:count], refs[count], refs[-1]
    lines = [sums[i][row : row + 1] for i, row in rows]
    lines += [jnp.zeros_like(lines[0])] * (128 - len(lines))
    out[:, :128] = jnp.concatenate(lines, axis=0).T
    out[:, 128:] = jnp.zeros((out.shape[0], 128), jnp.float32)
    for i in range(bias.shape[0]):
        out[i * owned : i * owned + 1, 128:] = bias[i : i + 1]


def small_block(lines, sums, bias, owned, after):
    width = sums[0].shape[1]
    devices = width // owned
    bias = bias.reshape(devices, -1)
    bias = jnp.pad(bias, ((0, 0), (0, 128 - bias.shape[1])))
    places = [([i for i, x in enumerate(sums) if x is s][0], row) for s, row in lines]
    block = pl.pallas_call(
        functools.partial(small_kernel, rows=places, count=len(sums), owned=owned),
        out_shape=jax.ShapeDtypeStruct((width, 256), jnp.float32),
        in_specs=[vmem] * (len(sums) + 1) + [anywhere] * len(after),
        out_specs=vmem,
        compiler_params=kernel_params(16),
        cost_estimate=cost(0, 2),
    )(*sums, bias, *after)
    return block.astype(jnp.bfloat16)


def add_product_kernel(*refs, count, base, extra):
    out = refs[-1]
    total = refs[2 * count][...] if base else jnp.zeros(out.shape, jnp.float32)
    for left, right in zip(refs[:count], refs[count : 2 * count]):
        total += dot(left[...], right[...], (1, 1))
    out[...] = total


def add_product(stack, places, weights, columns, rows, chunk, base=None, after=()):
    width = stack.shape[1]
    count = len(places)
    bases = [] if base is None else [base]
    block = pl.BlockSpec((chunk, width), lambda i: (i, 0))
    return pl.pallas_call(
        functools.partial(add_product_kernel, count=count, base=len(bases), extra=len(after)),
        grid=(rows // chunk,),
        out_shape=jax.ShapeDtypeStruct((rows, width), jnp.float32),
        in_specs=[pl.BlockSpec((chunk, width), lambda i, p=p: (p // chunk + i, 0)) for p in places]
        + [pl.BlockSpec((width, width), lambda i, c=c: (0, c)) for c in columns]
        + [block] * len(bases)
        + [anywhere] * len(after),
        out_specs=block,
        compiler_params=kernel_params(40),
        cost_estimate=cost(3 * rows * count * width * width, 12),
    )(*[stack] * count, *[weights] * count, *bases, *after)


def body(
    target_in,
    memory,
    block_rows,
    pad_rows,
    seq_lengths,
    self_qkv,
    self_out,
    cross_query,
    cross_kv,
    cross_out,
    ffn_in,
    ffn_out,
    norm_scale,
    small_bias,
    ffn_bias,
    cotangent,
):
    width = target_in.shape[1]
    owned = self_qkv.shape[0]
    me = lax.axis_index(AXES)
    core = (me & 1).reshape(1)
    ids = (me >> jnp.arange(lax.axis_size(AXES).bit_length() - 1)) & 1
    tokens, mems = target_in.shape[0], memory.shape[0]

    def turned(*arrays, after=()):
        keep, send = turn(core, arrays, owned, after)
        return keep, exchange(send, 0)

    memory_turned = turned(memory)
    target_turned = turned(target_in)
    pack = jnp.concatenate([norm_scale.T, small_bias.T, ffn_bias.reshape(owned, -1)], axis=1)
    small_cols = pack.shape[1]
    pack = jnp.pad(pack, ((0, 0), (0, -small_cols % 128)))
    early, stages = gather_rows(jnp.concatenate([self_qkv, self_out, pack], axis=1))
    late = pack_rows(
        [cross_query, cross_kv, cross_out],
        [(0, width, 0, 0), (0, 2 * width, 0, width), (0, width, 0, 3 * width)],
        (owned, 4 * width),
        stages[:1],
    )
    blocks = ffn_in.shape[1] // width
    packed = pack_rows(
        [ffn_in] * blocks + [ffn_out],
        [(i * width, width, i * owned, 0) for i in range(blocks)] + [(0, width, blocks * owned, 0)],
        (blocks * owned + ffn_out.shape[0], width),
        stages[:1],
    )
    packed = lax.all_gather(packed, AXES)
    w_qkv, w_self = early[:, : 3 * width], early[:, 3 * width : 4 * width]
    small = early[:, 4 * width : 4 * width + small_cols].astype(jnp.float32)
    gains = small[:, :3].T
    biases = small[:, 3:13].T
    in_bias = small[:, 13:].reshape(1, -1)

    bound = memory_bounds(block_rows[0], pad_rows[0])
    lengths = seq_lengths[0]
    zeros = jnp.zeros((width,), jnp.float32)
    qkv = (matmul(target_in, w_qkv) + jnp.concatenate([biases[0], zeros, biases[1]])).astype(
        jnp.bfloat16
    )
    self_context, self_summary = self_forward(lengths, qkv)
    first, first_unit, first_inverse = normalize(
        target_in.astype(jnp.float32) + matmul(self_context, w_self) + biases[2],
        gains[0],
        biases[7],
    )
    first_low = first.astype(jnp.bfloat16)
    self_turned = turned(self_context, first_low)
    late, _ = gather_rows(late, after=self_turned[:1])
    w_query, w_pairs, w_cross = late[:, :width], late[:, width : 3 * width], late[:, 3 * width :]
    cross_q = (matmul(first_low, w_query) + biases[3]).astype(jnp.bfloat16)
    cross_pairs = (matmul(memory, w_pairs) + jnp.concatenate([zeros, biases[4]])).astype(
        jnp.bfloat16
    )
    cross_context, cross_summary = cross_forward(bound, cross_q, cross_pairs)
    second, second_unit, second_inverse = normalize(
        first + matmul(cross_context, w_cross) + biases[5], gains[1], biases[8]
    )

    cross_turned = turned(cross_context, second)
    vectors = jnp.concatenate([biases[6:7], gains[2:3], biases[9:10], jnp.zeros((5, width), jnp.float32)])
    hidden, hidden_send, slope, block_out, third_grad, out_grad, third_sums = ffn_forward(
        core,
        second,
        packed,
        in_bias,
        cotangent,
        vectors,
        ffn_out.shape[0],
        after=(memory_turned[1], target_turned[1], self_turned[1]),
    )
    hidden_other, out_grad_other = exchange(hidden_send, 0), exchange(out_grad, 0)
    pre_grad, ffn_bias_grad, second_grad, cross_branch, second_sums = ffn_backward(
        packed, slope, third_grad, out_grad, second_unit, second_inverse, gains[1:2], cross_turned[1:]
    )
    pre_grad_other = exchange(pre_grad, 0)
    parts = products(
        ids,
        [(hidden, tokens, 0), (hidden_other, tokens, 0)],
        (out_grad, out_grad_other),
        [(0, tokens, tokens, 0, width)],
        ffn_out.shape[0],
        256,
        after=(pre_grad,),
    )
    out_chain = Chain(ids, parts, ffn_out.shape[0])
    parts = products(
        ids,
        [(x, tokens, 1) for x in cross_turned],
        (pre_grad, pre_grad_other),
        [(0, tokens, tokens, 0, ffn_in.shape[1])],
        owned,
        512,
        after=out_chain.sends,
    )
    in_chain = Chain(ids, parts, owned)

    cross_delta, cross_sums = cross_backward(
        bound, cross_q, cross_pairs, cross_summary, cross_branch, late, 3, after=in_chain.sends
    )
    cross_other = exchange(cross_delta, 0)
    self_delta, self_sums, first_grad = self_backward(
        lengths,
        qkv,
        self_summary,
        second_grad,
        cross_delta,
        late,
        early,
        first_unit,
        first_inverse,
        gains[0:1],
        after=out_chain.second(after=(cross_sums,)),
    )
    self_other = exchange(self_delta, 0)
    beyond = mems + 2 * tokens
    parts = products(
        ids,
        [
            part
            for i in range(2)
            for part in (
                (memory_turned[i], mems, 0),
                (self_turned[i], tokens, 1),
                (cross_turned[i], tokens, 0),
            )
        ],
        (cross_delta, cross_other),
        [
            (mems, beyond + mems, tokens, 0, width),
            (0, beyond, mems, 2 * tokens, width),
            (0, beyond, mems, 2 * tokens + mems, width),
            (mems + tokens, beyond + mems + tokens, tokens, tokens, width),
        ],
        owned,
        512,
        after=in_chain.second(after=(self_sums,)),
    )
    cross_chain = Chain(ids, parts, owned)
    parts = products(
        ids,
        [part for i in range(2) for part in ((target_turned[i], tokens, 0), (self_turned[i], tokens, 0))],
        (self_delta, self_other),
        [(0, 2 * tokens, tokens, i * tokens, width) for i in range(3)]
        + [(tokens, 3 * tokens, tokens, 3 * tokens, width)],
        owned,
        512,
        after=out_chain.third(after=parts[:1]),
    )
    self_chain = Chain(ids, parts, owned)
    last = in_chain.third(after=parts[:1])

    small_grad = small_block(
        [
            (self_sums, 3),
            (second_sums, 0),
            (third_sums, 0),
            (self_sums, 0),
            (self_sums, 1),
            (self_sums, 2),
            (cross_sums, 0),
            (cross_sums, 1),
            (second_sums, 2),
            (third_sums, 2),
            (self_sums, 4),
            (second_sums, 1),
            (third_sums, 1),
        ],
        [self_sums, cross_sums, second_sums, third_sums],
        ffn_bias_grad,
        owned,
        last,
    )
    bits = list(range(lax.axis_size(AXES).bit_length() - 1))[::-1]
    small_part = small_grad.reshape((2,) * len(bits) + (owned, -1))
    for bit in (0, 1):
        mine = (me >> bit) & 1
        keep, send = [
            lax.dynamic_index_in_dim(small_part, i, bits.index(bit), keepdims=False)
            for i in (mine, 1 - mine)
        ]
        arrived = exchange(send, bit)
        small_part = (keep.astype(jnp.float32) + arrived.astype(jnp.float32)).astype(jnp.bfloat16)
        bits.remove(bit)
    self_chain.groups[1].append((keep, arrived))

    memory_grad = add_product(
        cross_delta, [2 * tokens, 2 * tokens + mems], late, [1, 2], mems, 256, after=(small_grad,)
    )
    last = cross_chain.second(after=(memory_grad,))
    last = out_chain.third(after=last)
    target_grad = add_product(
        self_delta, [0, tokens, 2 * tokens], early, [0, 1, 2], tokens, tokens, first_grad, after=last
    )
    last = in_chain.third(after=(target_grad,))
    last = self_chain.second(after=last)
    last = cross_chain.third(after=last)
    last = cross_chain.third(after=last)
    last = self_chain.third(after=last)
    while self_chain.rest:
        last = self_chain.third(after=last)
    for chain in (out_chain, in_chain, cross_chain):
        while chain.rest:
            last = chain.third(after=last)
    ffn_out_shard = out_chain.finish()
    ffn_in_shard = in_chain.finish()
    cross_shard = cross_chain.finish()
    self_shard = self_chain.finish()
    small_shard = self_shard[:, 4 * width :]
    return (
        block_out,
        target_grad,
        memory_grad,
        self_shard[:, : 3 * width],
        self_shard[:, 3 * width : 4 * width],
        cross_shard[:, :width],
        cross_shard[:, width : 3 * width],
        cross_shard[:, 3 * width :],
        ffn_in_shard,
        ffn_out_shard,
        small_shard[:, :3].T,
        small_shard[:, 3:13].T,
        small_shard[0, 128 : 128 + ffn_bias.shape[0]],
    )


def solution(mesh):
    in_specs = (
        P(("wide", "narrow"), None),
        P(("wide", "narrow"), None),
        P(("wide", "narrow"), None),
        P(("wide", "narrow"), None),
        P(("wide", "narrow"), None),
        P(("wide", "narrow"), None),
        P(("wide", "narrow"), None),
        P(("wide", "narrow"), None),
        P(("wide", "narrow"), None),
        P(("wide", "narrow"), None),
        P(("wide", "narrow"), None),
        P(("wide", "narrow"), None),
        P(None, ("wide", "narrow")),
        P(None, ("wide", "narrow")),
        P(("wide", "narrow")),
        P(("wide", "narrow"), None),
    )
    out_specs = (
        P(("wide", "narrow"), None),
        P(("wide", "narrow"), None),
        P(("wide", "narrow"), None),
        P(("wide", "narrow"), None),
        P(("wide", "narrow"), None),
        P(("wide", "narrow"), None),
        P(("wide", "narrow"), None),
        P(("wide", "narrow"), None),
        P(("wide", "narrow"), None),
        P(("wide", "narrow"), None),
        P(None, ("wide", "narrow")),
        P(None, ("wide", "narrow")),
        P(("wide", "narrow")),
    )
    return jax.shard_map(body, mesh=mesh, in_specs=in_specs, out_specs=out_specs, check_vma=False)
```

```python
import functools

import jax
import jax.numpy as jnp
from jax import lax
from jax.experimental import pallas as pl
from jax.experimental.pallas import tpu as pltpu
from jax.sharding import PartitionSpec as P

HEADS = 16
HEAD_DIM = 64
SEQ_LEN = 128
PAIRS = HEADS // 2
neg_fill = -1e30
AXES = ("wide", "narrow")
vmem = pl.BlockSpec(memory_space=pltpu.VMEM)
smem = pl.BlockSpec(memory_space=pltpu.SMEM)
anywhere = pl.BlockSpec(memory_space=pl.ANY)
norm_eps = 1e-05


def kernel_params(megabytes):
    return pltpu.CompilerParams(vmem_limit_bytes=megabytes << 20)


def cost(flops, megabytes, transcendentals=0):
    return pl.CostEstimate(
        flops=int(10 * flops), bytes_accessed=int(10 * megabytes * 2**20), transcendentals=int(10 * transcendentals)
    )


def matmul(first, second):
    return jnp.dot(first, second, preferred_element_type=jnp.float32)


def inner_cols(first, second):
    return lax.dot_general(
        first, second, (((1,), (1,)), ((), ())), preferred_element_type=jnp.float32
    )


def column_sums(values):
    return jnp.sum(values.astype(jnp.float32), axis=0)


def memory_bounds(block_rows, pad_rows):
    count = block_rows.shape[0]
    before = jnp.arange(count)[None, :] < jnp.arange(count)[:, None]
    starts = jnp.sum(jnp.where(before, block_rows[None, :], 0), axis=1)
    valid = jnp.maximum(block_rows - pad_rows, (block_rows + 1) // 2)
    return jnp.stack([starts, starts + valid])


def dot(first, second, contract):
    return lax.dot_general(
        first, second, ((contract[:1], contract[1:]), ((), ())), preferred_element_type=jnp.float32
    )


def cols(pair, base=0):
    return slice((base + pair) * 128, (base + pair + 1) * 128)


def split_heads(block):
    low = lax.broadcasted_iota(jnp.int32, block.shape, 1) < HEAD_DIM
    zero = jnp.zeros_like(block)
    return jnp.concatenate([jnp.where(low, block, zero), jnp.where(low, zero, block)], axis=0)


def join_heads(stacked):
    low = lax.broadcasted_iota(jnp.int32, (SEQ_LEN, 128), 1) < HEAD_DIM
    return jnp.where(low, stacked[:SEQ_LEN], stacked[SEQ_LEN:])


def join_heads_t(stacked):
    both = jnp.concatenate([stacked[:HEAD_DIM, :SEQ_LEN], stacked[HEAD_DIM:, SEQ_LEN:]], axis=0)
    return both.T


def cross_mask(tile, low, high):
    rows = tile * 128 + lax.broadcasted_iota(jnp.int32, (128, 2 * SEQ_LEN), 0)
    return (rows >= low) & (rows < high)


def cross_forward_kernel(bound, q, pairs, *rest, extra):
    context, summary, stack, scores, top, total, acc = rest[extra:]

    def sequence(s, carry):
        low, high = bound[0, s], bound[1, s]
        first, last = low // 128, (high + 127) // 128
        rows = pl.ds(pl.multiple_of(s * SEQ_LEN, SEQ_LEN), SEQ_LEN)
        for p in range(PAIRS):
            stack[p] = split_heads(q[rows, cols(p)] * jnp.bfloat16(HEAD_DIM**-0.5))
        top[...] = jnp.full_like(top, neg_fill)
        total[...] = jnp.zeros_like(total)
        acc[...] = jnp.zeros_like(acc)

        def one(t, carry):
            keys = pl.ds(pl.multiple_of(t * 128, 128), 128)
            ok = cross_mask(t, low, high)
            for p in range(PAIRS):
                raw = jnp.where(ok, dot(pairs[keys, cols(p)], stack[p], (1, 1)), neg_fill)
                scores[t, p] = raw
                top[p] = jnp.maximum(top[p], jnp.max(raw, axis=0, keepdims=True))
            return carry

        lax.fori_loop(first, last, one, 0)

        def two(t, carry):
            keys = pl.ds(pl.multiple_of(t * 128, 128), 128)
            for p in range(PAIRS):
                weights = jnp.exp(scores[t, p] - top[p])
                total[p] += jnp.sum(weights, axis=0, keepdims=True)
                acc[p] += dot(pairs[keys, cols(p, PAIRS)], weights.astype(jnp.bfloat16), (0, 0))
            return carry

        lax.fori_loop(first, last, two, 0)
        for p in range(PAIRS):
            context[rows, cols(p)] = join_heads_t(acc[p] / total[p]).astype(jnp.bfloat16)
            summary[s, p] = top[p] + jnp.log(total[p])
        return carry

    lax.fori_loop(0, bound.shape[1], sequence, 0)


def cross_backward_kernel(bound, q, pairs, summary, branch, weight, *rest, extra):
    out, sums, grad, stack, grads, probs, prob_grads, delta, acc, pair_acc = rest[extra:]
    pair_acc[...] = jnp.zeros_like(pair_acc)
    scale = HEAD_DIM**-0.5
    (tokens, width), mems = q.shape, pairs.shape[0]
    grad[...] = dot(branch[...], weight[...], (1, 1)).astype(jnp.bfloat16)
    pad = (out.shape[0] - 2 * mems) // 2
    query_at, branch_at = 2 * mems, 2 * mems + pad

    def sequence(s, carry):
        low, high = bound[0, s], bound[1, s]
        first, last = low // 128, (high + 127) // 128
        rows = pl.ds(pl.multiple_of(s * SEQ_LEN, SEQ_LEN), SEQ_LEN)
        for p in range(PAIRS):
            stack[p] = split_heads(q[rows, cols(p)] * jnp.bfloat16(scale))
            grads[p] = split_heads(grad[rows, cols(p)])
        delta[...] = jnp.zeros_like(delta)
        acc[...] = jnp.zeros_like(acc)

        def one(t, carry):
            keys = pl.ds(pl.multiple_of(t * 128, 128), 128)
            ok = cross_mask(t, low, high)
            for p in range(PAIRS):
                raw = dot(pairs[keys, cols(p)], stack[p], (1, 1))
                weights = jnp.where(ok, jnp.exp(raw - summary[s, p]), 0.0)
                back = dot(pairs[keys, cols(p, PAIRS)], grads[p], (1, 1))
                delta[p] += jnp.sum(weights * back, axis=0, keepdims=True)
                probs[t, p] = weights
                prob_grads[t, p] = back
                pair_acc[keys, cols(p, PAIRS)] += dot(weights.astype(jnp.bfloat16), grads[p], (1, 0))
            return carry

        lax.fori_loop(first, last, one, 0)

        def two(t, carry):
            keys = pl.ds(pl.multiple_of(t * 128, 128), 128)
            for p in range(PAIRS):
                score = (probs[t, p] * (prob_grads[t, p] - delta[p])).astype(jnp.bfloat16)
                pair_acc[keys, cols(p)] += dot(score, stack[p], (1, 0))
                acc[p] += dot(pairs[keys, cols(p)], score, (0, 0))
            return carry

        lax.fori_loop(first, last, two, 0)
        for p in range(PAIRS):
            place = pl.ds(pl.multiple_of(query_at + s * SEQ_LEN, SEQ_LEN), SEQ_LEN)
            out[place, cols(p)] = (join_heads_t(acc[p]) * scale).astype(jnp.bfloat16)
        return carry

    lax.fori_loop(0, bound.shape[1], sequence, 0)
    out[:mems, :] = pair_acc[:, :width].astype(jnp.bfloat16)
    out[mems:query_at, :] = pair_acc[:, width:].astype(jnp.bfloat16)
    out[branch_at : branch_at + tokens, :] = branch[...]
    for at in (query_at, branch_at):
        out[at + tokens : at + pad, :] = jnp.zeros((pad - tokens, width), jnp.bfloat16)
    sums[...] = sum_rows(
        out[query_at : query_at + tokens, :].astype(jnp.float32), out[mems:query_at, :].astype(jnp.float32)
    )


def cross_forward(bound, q, pairs, after=()):
    seqs, tiles = bound.shape[1], pairs.shape[0] // 128
    wide = 2 * SEQ_LEN
    return pl.pallas_call(
        functools.partial(cross_forward_kernel, extra=len(after)),
        out_shape=(
            jax.ShapeDtypeStruct(q.shape, jnp.bfloat16),
            jax.ShapeDtypeStruct((seqs, PAIRS, 1, wide), jnp.float32),
        ),
        in_specs=[smem, vmem, vmem] + [anywhere] * len(after),
        out_specs=(vmem, vmem),
        scratch_shapes=[
            pltpu.VMEM((PAIRS, wide, 128), jnp.bfloat16),
            pltpu.VMEM((tiles, PAIRS, 128, wide), jnp.float32),
            pltpu.VMEM((PAIRS, 1, wide), jnp.float32),
            pltpu.VMEM((PAIRS, 1, wide), jnp.float32),
            pltpu.VMEM((PAIRS, 128, wide), jnp.float32),
        ],
        compiler_params=kernel_params(40),
        cost_estimate=cost(8e9, 8),
    )(bound, q, pairs, *after)


def cross_backward(bound, q, pairs, summary, branch, weights, column, after=()):
    seqs, tiles = bound.shape[1], pairs.shape[0] // 128
    wide = 2 * SEQ_LEN
    width = q.shape[1]
    whole = lambda shape: pl.BlockSpec(shape, lambda i: (0,) * len(shape))
    rows = 3 * pairs.shape[0]
    return pl.pallas_call(
        functools.partial(cross_backward_kernel, extra=len(after)),
        grid=(1,),
        out_shape=(
            jax.ShapeDtypeStruct((rows, width), jnp.bfloat16),
            jax.ShapeDtypeStruct((8, width), jnp.float32),
        ),
        in_specs=[smem]
        + [whole(x.shape) for x in (q, pairs, summary, branch)]
        + [pl.BlockSpec((width, width), lambda i: (0, column))]
        + [anywhere] * len(after),
        out_specs=(whole((rows, width)), whole((8, width))),
        scratch_shapes=[
            pltpu.VMEM(q.shape, jnp.bfloat16),
            pltpu.VMEM((PAIRS, wide, 128), jnp.bfloat16),
            pltpu.VMEM((PAIRS, wide, 128), jnp.bfloat16),
            pltpu.VMEM((tiles, PAIRS, 128, wide), jnp.float32),
            pltpu.VMEM((tiles, PAIRS, 128, wide), jnp.float32),
            pltpu.VMEM((PAIRS, 1, wide), jnp.float32),
            pltpu.VMEM((PAIRS, 128, wide), jnp.float32),
            pltpu.VMEM(pairs.shape, jnp.float32),
        ],
        compiler_params=kernel_params(58),
        cost_estimate=cost(16e9, 12),
    )(bound, q, pairs, summary, branch, weights, *after)


def self_mask(length):
    keys = lax.broadcasted_iota(jnp.int32, (SEQ_LEN, 2 * SEQ_LEN), 0)
    tokens = lax.broadcasted_iota(jnp.int32, (SEQ_LEN, 2 * SEQ_LEN), 1) & (SEQ_LEN - 1)
    return (keys <= tokens) & (keys < length)


def self_forward_kernel(lengths, qkv, *rest, extra):
    context, summary = rest[extra:]

    def sequence(s, carry):
        ok = self_mask(lengths[s])
        rows = pl.ds(pl.multiple_of(s * SEQ_LEN, SEQ_LEN), SEQ_LEN)
        for p in range(PAIRS):
            stack = split_heads(qkv[rows, cols(p)] * jnp.bfloat16(HEAD_DIM**-0.5))
            raw = jnp.where(ok, dot(qkv[rows, cols(p, PAIRS)], stack, (1, 1)), neg_fill)
            top = jnp.max(raw, axis=0, keepdims=True)
            weights = jnp.exp(raw - top)
            total = jnp.sum(weights, axis=0, keepdims=True)
            weights = (weights / total).astype(jnp.bfloat16)
            acc = dot(qkv[rows, cols(p, 2 * PAIRS)], weights, (0, 0))
            context[rows, cols(p)] = join_heads_t(acc).astype(jnp.bfloat16)
            summary[s, p] = top + jnp.log(total)
        return carry

    lax.fori_loop(0, lengths.shape[0], sequence, 0)


def self_backward_kernel(
    lengths, qkv, summary, second_grad, query_delta, w_query, w_self, unit, inverse, gain, *rest, extra
):
    out, sums, first_grad, grad = rest[extra:]
    scale = HEAD_DIM**-0.5
    tokens = qkv.shape[0]
    total = second_grad[...] + dot(query_delta[:tokens, :], w_query[...], (1, 1))
    first = normalize_back(total, unit[...], inverse[...], gain[...])
    first_grad[...] = first
    branch = first.astype(jnp.bfloat16)
    out[3 * tokens :, :] = branch
    grad[...] = dot(branch, w_self[...], (1, 1)).astype(jnp.bfloat16)

    def sequence(s, carry):
        ok = self_mask(lengths[s])
        rows = pl.ds(pl.multiple_of(s * SEQ_LEN, SEQ_LEN), SEQ_LEN)
        for p in range(PAIRS):
            stack = split_heads(qkv[rows, cols(p)] * jnp.bfloat16(scale))
            grads = split_heads(grad[rows, cols(p)])
            keys = qkv[rows, cols(p, PAIRS)]
            raw = dot(keys, stack, (1, 1))
            weights = jnp.where(ok, jnp.exp(raw - summary[s, p]), 0.0)
            back = dot(qkv[rows, cols(p, 2 * PAIRS)], grads, (1, 1))
            delta = jnp.sum(weights * back, axis=0, keepdims=True)
            score = (weights * (back - delta)).astype(jnp.bfloat16)
            value_grad = dot(weights.astype(jnp.bfloat16), grads, (1, 0))
            key_grad = dot(score, stack, (1, 0))
            query_grad = join_heads_t(dot(keys, score, (0, 0))) * scale
            for i, part in enumerate((query_grad, key_grad, value_grad)):
                place = pl.ds(pl.multiple_of(i * tokens + s * SEQ_LEN, SEQ_LEN), SEQ_LEN)
                out[place, cols(p)] = part.astype(jnp.bfloat16)
        return carry

    lax.fori_loop(0, lengths.shape[0], sequence, 0)
    sums[...] = sum_rows(
        *[out[i * tokens : (i + 1) * tokens, :].astype(jnp.float32) for i in (0, 2, 3)],
        total * unit[...],
        total,
    )


def self_forward(lengths, qkv, after=()):
    tokens, width = qkv.shape[0], qkv.shape[1] // 3
    return pl.pallas_call(
        functools.partial(self_forward_kernel, extra=len(after)),
        out_shape=(
            jax.ShapeDtypeStruct((tokens, width), jnp.bfloat16),
            jax.ShapeDtypeStruct((lengths.shape[0], PAIRS, 1, 2 * SEQ_LEN), jnp.float32),
        ),
        in_specs=[smem, vmem] + [anywhere] * len(after),
        out_specs=(vmem, vmem),
        compiler_params=kernel_params(24),
        cost_estimate=cost(2e9, 4),
    )(lengths, qkv, *after)


def self_backward(
    lengths, qkv, summary, second_grad, cross_delta, weights, unit, inverse, gain, after=()
):
    tokens, width = second_grad.shape
    whole = lambda shape: pl.BlockSpec(shape, lambda i: (0,) * len(shape))
    full = whole((tokens, width))
    return pl.pallas_call(
        functools.partial(self_backward_kernel, extra=len(after)),
        grid=(1,),
        out_shape=(
            jax.ShapeDtypeStruct((4 * tokens, width), jnp.bfloat16),
            jax.ShapeDtypeStruct((8, width), jnp.float32),
            jax.ShapeDtypeStruct((tokens, width), jnp.float32),
        ),
        in_specs=[
            smem,
            whole(qkv.shape),
            whole(summary.shape),
            full,
            pl.BlockSpec((cross_delta.shape[0] // 6, width), lambda i: (4, 0)),
            pl.BlockSpec((width, width), lambda i: (0, 4)),
            pl.BlockSpec((width, width), lambda i: (0, 3)),
            full,
            whole((tokens, 1)),
            whole((1, width)),
        ]
        + [anywhere] * len(after),
        out_specs=(whole((4 * tokens, width)), whole((8, width)), full),
        scratch_shapes=[pltpu.VMEM((tokens, width), jnp.bfloat16)],
        compiler_params=kernel_params(48),
        cost_estimate=cost(6e9, 12),
    )(lengths, qkv, summary, second_grad, cross_delta, weights, weights, unit, inverse, gain, *after)


def normalize(values, gain, shift):
    centered = values - jnp.mean(values, axis=-1, keepdims=True)
    inverse = lax.rsqrt(jnp.mean(centered * centered, axis=-1, keepdims=True) + norm_eps)
    unit = centered * inverse
    return (unit * gain + shift, unit, inverse)


def normalize_back(grad, unit, inverse, gain):
    scaled = grad * gain
    inner = (
        scaled
        - jnp.mean(scaled, axis=-1, keepdims=True)
        - unit * jnp.mean(scaled * unit, axis=-1, keepdims=True)
    )
    return inverse * inner


def sum_rows(*rows):
    stacked = [jnp.sum(r, axis=0, keepdims=True) for r in rows]
    return jnp.concatenate(stacked + [jnp.zeros_like(stacked[0])] * (8 - len(rows)), axis=0)


def deal(core, turned, rows, keep, send):
    for i in range(turned.shape[0] // (2 * rows)):
        even = turned[2 * i * rows : (2 * i + 1) * rows]
        odd = turned[(2 * i + 1) * rows : (2 * i + 2) * rows]
        here = slice(i * rows, (i + 1) * rows)
        keep(here, jnp.where(core == 0, even, odd).astype(jnp.bfloat16))
        send(here, jnp.where(core == 0, odd, even).astype(jnp.bfloat16))


def into(ref, columns):
    def store(rows, values):
        ref[rows, columns] = values

    return store


def turn_kernel(core, *refs, rows, count):
    arrays, (keep, send) = refs[:count], refs[-2:]
    start = 0
    for array in arrays:
        tokens = array.shape[0]
        columns = slice(start, start + tokens)
        turned = array[...].astype(jnp.float32).T
        deal(core[0], turned, rows, into(keep, columns), into(send, columns))
        start += tokens


def turn(core, arrays, rows, after=()):
    width = arrays[0].shape[1]
    half = jax.ShapeDtypeStruct((width // 2, sum(x.shape[0] for x in arrays)), jnp.bfloat16)
    return pl.pallas_call(
        functools.partial(turn_kernel, rows=rows, count=len(arrays)),
        out_shape=(half, half),
        in_specs=[smem] + [vmem] * len(arrays) + [anywhere] * len(after),
        out_specs=(vmem, vmem),
        compiler_params=kernel_params(32),
        cost_estimate=cost(0, 8),
    )(core, *arrays, *after)


def flat(block):
    values = block[...]
    if values.shape[1] % 16:
        values = values.astype(jnp.float32)
    return values.reshape(-1, values.shape[-1]).astype(jnp.bfloat16)


def weight_blocks(packed, chunk):
    devices, rows, width = packed.shape
    hidden = devices * rows // 2
    strips, owned = width // chunk, rows * width // (2 * hidden)
    return [
        pl.BlockSpec((devices, owned, chunk), lambda j: (0, j // strips, j % strips)),
        pl.BlockSpec((devices * chunk // hidden, rows // 2, width), lambda j: (j, 1, 0)),
    ]


def ffn_forward_kernel(
    core, second, w_in, w_out, bias, cot, vectors, *rest, rows, extra
):
    keep, send, slope, block_out, third_grad, out_grad, sums, acc, low = rest[extra:]

    step = pl.program_id(0)

    @pl.when(step == 0)
    def _():
        low[...] = second[...].astype(jnp.bfloat16)
        acc[...] = second[...] + vectors[0:1]

    pre = dot(low[...], flat(w_in), (1, 0)) + bias[...]
    part = 0.5 + 0.5 * lax.erf(pre * 0.5**0.5)
    active = pre * part
    everything = slice(None)
    deal(core[0], active.T, rows, into(keep, everything), into(send, everything))
    active = active.astype(jnp.bfloat16)
    slope[...] = (part + pre * jnp.exp(-0.5 * pre * pre) * 0.3989422804014327).astype(jnp.bfloat16)
    acc[...] += dot(active, flat(w_out), (1, 0))

    @pl.when(step == pl.num_programs(0) - 1)
    def _():
        gain = vectors[1:2]
        third, unit, inverse = normalize(acc[...], gain, vectors[2:3])
        block_out[...] = third.astype(jnp.bfloat16)
        grad = cot[...].astype(jnp.float32)
        third = normalize_back(grad, unit, inverse, gain)
        third_grad[...] = third
        lower = third.astype(jnp.bfloat16)
        out_grad[...] = lower
        sums[...] = sum_rows(grad * unit, grad, lower.astype(jnp.float32))


def ffn_forward(core, second, packed, bias, cot, vectors, rows, after):
    tokens, width = second.shape
    hidden = packed.shape[0] * packed.shape[1] // 2
    chunk = 512
    whole = lambda shape: pl.BlockSpec(shape, lambda j: (0, 0))
    full = whole((tokens, width))
    strip = pl.BlockSpec((tokens, chunk), lambda j: (0, j))
    turned = pl.BlockSpec((chunk // 2, tokens), lambda j: (j, 0))
    return pl.pallas_call(
        functools.partial(ffn_forward_kernel, rows=rows, extra=len(after)),
        grid=(hidden // chunk,),
        out_shape=(
            jax.ShapeDtypeStruct((hidden // 2, tokens), jnp.bfloat16),
            jax.ShapeDtypeStruct((hidden // 2, tokens), jnp.bfloat16),
            jax.ShapeDtypeStruct((tokens, hidden), jnp.bfloat16),
            jax.ShapeDtypeStruct((tokens, width), jnp.bfloat16),
            jax.ShapeDtypeStruct((tokens, width), jnp.float32),
            jax.ShapeDtypeStruct((tokens, width), jnp.bfloat16),
            jax.ShapeDtypeStruct((8, width), jnp.float32),
        ),
        in_specs=[
            smem,
            full,
            *weight_blocks(packed, chunk),
            pl.BlockSpec((1, chunk), lambda j: (0, j)),
            full,
            whole((8, width)),
        ]
        + [anywhere] * len(after),
        out_specs=(turned, turned, strip, full, full, full, whole((8, width))),
        scratch_shapes=[
            pltpu.VMEM((tokens, width), jnp.float32),
            pltpu.VMEM((tokens, width), jnp.bfloat16),
        ],
        compiler_params=kernel_params(40),
        cost_estimate=cost(16e9, 26, 4e6),
    )(core, second, packed, packed, bias, cot, vectors, *after)


def ffn_backward_kernel(
    w_in, w_out, slope, third_grad, out_grad, unit, inverse, gain, *rest, extra
):
    pre_grad, bias_grad, second_grad, branch, sums, acc = rest[extra:]
    step = pl.program_id(0)

    @pl.when(step == 0)
    def _():
        acc[...] = third_grad[...]

    grad = dot(out_grad[...], flat(w_out), (1, 1)) * slope[...].astype(jnp.float32)
    lower = grad.astype(jnp.bfloat16)
    pre_grad[...] = lower
    bias_grad[...] = jnp.sum(lower.astype(jnp.float32), axis=0, keepdims=True)
    acc[...] += dot(lower, flat(w_in), (1, 1))

    @pl.when(step == pl.num_programs(0) - 1)
    def _():
        total = acc[...]
        grad = normalize_back(total, unit[...], inverse[...], gain[...])
        second_grad[...] = grad
        lower = grad.astype(jnp.bfloat16)
        branch[...] = lower
        sums[...] = sum_rows(total * unit[...], total, lower.astype(jnp.float32))


def ffn_backward(packed, slope, third_grad, out_grad, unit, inverse, gain, after):
    tokens, width = third_grad.shape
    hidden = packed.shape[0] * packed.shape[1] // 2
    chunk = 512
    whole = lambda shape: pl.BlockSpec(shape, lambda j: (0, 0))
    full = whole((tokens, width))
    strip = pl.BlockSpec((tokens, chunk), lambda j: (0, j))
    return pl.pallas_call(
        functools.partial(ffn_backward_kernel, extra=len(after)),
        grid=(hidden // chunk,),
        out_shape=(
            jax.ShapeDtypeStruct((tokens, hidden), jnp.bfloat16),
            jax.ShapeDtypeStruct((1, hidden), jnp.float32),
            jax.ShapeDtypeStruct((tokens, width), jnp.float32),
            jax.ShapeDtypeStruct((tokens, width), jnp.bfloat16),
            jax.ShapeDtypeStruct((8, width), jnp.float32),
        ),
        in_specs=[
            *weight_blocks(packed, chunk),
            strip,
            full,
            full,
            full,
            whole((tokens, 1)),
            whole((1, width)),
        ]
        + [anywhere] * len(after),
        out_specs=(strip, pl.BlockSpec((1, chunk), lambda j: (0, j)), full, full, whole((8, width))),
        scratch_shapes=[pltpu.VMEM((tokens, width), jnp.float32)],
        compiler_params=kernel_params(40),
        cost_estimate=cost(14e9, 26),
    )(packed, packed, slope, third_grad, out_grad, unit, inverse, gain, *after)


def product_kernel(ids, *refs, spans, n_left, n_right, rows, chunk, extra, sides):
    lefts, rights = refs[:n_left], refs[n_left : n_left + 2 * n_right]
    rest = refs[n_left + 2 * n_right + extra :]
    outs, (ordered, *wide) = rest[: 2 * len(sides)], rest[2 * len(sides) :]
    step = pl.program_id(0)
    blocks = lefts[0].shape[0] // rows
    half = blocks // 2 * rows

    @pl.when(step == 0)
    def _():
        start = 0
        for left in lefts:
            source, size = left, left.shape[1]
            if wide:
                source = wide[0].at[:, pl.ds(0, size)]
                source[...] = left[...].astype(jnp.float32)
            for side, order in enumerate(sides):
                bit = 1 - order
                for i in range(blocks):
                    low, high = i % (1 << bit), (i % (blocks // 2)) >> bit
                    mine = ids[2 - order] if i < blocks // 2 else 1 - ids[2 - order]
                    place = (high << (bit + 1)) + (mine << bit) + low
                    taken = source[pl.ds(pl.multiple_of(place * rows, rows), rows), :]
                    ordered[side, i * rows : (i + 1) * rows, start : start + size] = taken.astype(jnp.bfloat16)
            start += size

    steps = sum(s[-1] for s in spans)
    first = 0
    for mine, other, tokens, which, _, count in spans:
        for side in range(len(sides)):
            keep, send = outs[2 * side : 2 * side + 2]
            low = max(first, side * steps // len(sides))
            high = min(first + count, (side + 1) * steps // len(sides))
            if low >= high:
                continue

            @pl.when((step >= low) & (step < high))
            def _(mine=mine, other=other, tokens=tokens, which=which, side=side, keep=keep, send=send):
                total = dot(
                    ordered[side, :, mine : mine + tokens], rights[2 * which][:tokens, :], (1, 0)
                ) + dot(
                    ordered[side, :, other : other + tokens], rights[2 * which + 1][:tokens, :], (1, 0)
                )
                keep[...] = total[:half].astype(jnp.bfloat16)
                send[...] = total[half:].astype(jnp.bfloat16)

        first += count


def products(ids, lefts, rights, spans, rows, chunk, sides=(0, 1), after=()):
    height = lefts[0][0].shape[0]
    columns = sum(s[-1] for s in spans)
    steps = columns // chunk
    spans = [(*s[:-1], s[-1] // chunk) for s in spans]
    count = len(sides)
    part = jax.ShapeDtypeStruct((height // 2, columns // count), jnp.bfloat16)
    blocks = [
        pl.BlockSpec(
            (height // 2, chunk),
            lambda j, side=side: (0, jnp.clip(j - side * steps // count, 0, steps // count - 1)),
        )
        for side in range(count)
        for _ in range(2)
    ]
    tokens = sum(x[1] for x in lefts)
    wide = [pltpu.VMEM((height, max(x[1] for x in lefts)), jnp.float32)] if rows % 16 else []
    taken = [pl.BlockSpec((height, size), lambda j, place=place: (0, place)) for _, size, place in lefts]

    def place_of(which):
        def index(j):
            first, found = 0, []
            for _, _, _, w, row, count in spans:
                if w == which:
                    found.append((first, first + count, row))
                first += count
            first, end, row = found[-1]
            at_row, at_column = row, jnp.clip(j - first, 0, end - first - 1)
            for first, end, row in found[-2::-1]:
                at_row = jnp.where(j < end, row, at_row)
                at_column = jnp.where(j < end, jnp.clip(j - first, 0, end - first - 1), at_column)
            return at_row, at_column

        return index

    strips = [
        pl.BlockSpec((block, chunk), place_of(i)) for i, (_, _, block) in enumerate(rights) for _ in range(2)
    ]
    return pl.pallas_call(
        functools.partial(
            product_kernel,
            spans=spans,
            n_left=len(lefts),
            n_right=len(rights),
            rows=rows,
            chunk=chunk,
            extra=len(after),
            sides=sides,
        ),
        grid=(steps,),
        out_shape=(part,) * (2 * count),
        in_specs=[smem] + taken + strips + [anywhere] * len(after),
        out_specs=blocks,
        scratch_shapes=[pltpu.VMEM((count, height, tokens), jnp.bfloat16)] + wide,
        compiler_params=kernel_params(48),
        cost_estimate=cost(2.5 * height * tokens * columns / len(lefts), 20),
    )(ids, *[x[0] for x in lefts], *[x for right in rights for x in right[:2]], *after)


def exchange(values, bit):
    count = lax.axis_size(AXES)
    return lax.ppermute(values, AXES, [(i, i ^ (1 << bit)) for i in range(count)])


def place_kernel(*refs, slots, rows):
    me = lax.axis_index(AXES)
    pieces, out, sems = refs[: len(slots)], refs[-2], refs[-1]
    copies = []
    for piece, (start, order) in zip(pieces, slots):
        columns = pl.ds(start, piece.shape[-1])
        for i, slot in enumerate(order):
            place = pl.ds(pl.multiple_of((me ^ slot) * rows, rows), rows)
            copies.append(
                pltpu.make_async_copy(piece.at[i], out.at[place, columns], sems.at[len(copies)])
            )
    for copy in copies:
        copy.start()
    for copy in copies:
        copy.wait()


def join_kernel(*refs, count, split):
    parts, outs = refs[: 2 * count], refs[-(2 if split else count) :]
    for i in range(count):
        first = 0
        for part in parts[2 * i : 2 * i + 2]:
            rows = slice(first, first + part.shape[0])
            if split:
                outs[0][rows] = part[:, :, :split]
                outs[1][rows] = part[:, :, split:]
            else:
                outs[i][rows] = part[...]
            first += part.shape[0]


def pack_kernel(w_in, w_out, *refs):
    out = refs[-1]
    rows, width = w_in.shape[0], out.shape[1]
    count = w_in.shape[1] // width
    for i in range(count):
        out[i * rows : (i + 1) * rows, :] = w_in[:, i * width : (i + 1) * width]
    out[count * rows :, :] = w_out[...]


def pack_ffn(w_in, w_out, after):
    return pl.pallas_call(
        pack_kernel,
        out_shape=jax.ShapeDtypeStruct((2 * w_out.shape[0], w_out.shape[1]), jnp.bfloat16),
        in_specs=[vmem] * 2 + [anywhere] * len(after),
        out_specs=vmem,
        compiler_params=kernel_params(16),
        cost_estimate=cost(0, 1),
    )(w_in, w_out, *after)


class Gather:
    def __init__(self, local):
        self.rows, self.width = local.shape
        bits = lax.axis_size(AXES).bit_length() - 1
        self.half = self.width // 256 * 128
        high = [(b,) for b in range(bits - 1, 2, -1)]
        self.bits = high + [(2, 1), (1, 2), (0, 0)]
        self.count = len(high)
        self.values, self.order, self.stage = [local[None]], [[0]], 0
        self.send()

    def send(self):
        self.arrived = [exchange(v, b) for v, b in zip(self.values, self.bits[self.stage])]

    def step(self, after=()):
        self.order = [
            order + [i ^ (1 << b) for i in order] for order, b in zip(self.order, self.bits[self.stage])
        ]
        self.stage += 1
        split = self.half if self.stage == self.count else 0
        slots, columns = 2 * self.values[0].shape[0], [v.shape[-1] for v in self.values]
        if split:
            self.order = self.order * 2
            columns = [split, self.width - split]
        parts = [x for pair in zip(self.values, self.arrived) for x in pair]
        self.values = pl.pallas_call(
            functools.partial(join_kernel, count=len(self.values), split=split),
            out_shape=[jax.ShapeDtypeStruct((slots, self.rows, n), jnp.bfloat16) for n in columns],
            in_specs=[vmem] * len(parts) + [anywhere] * len(after),
            out_specs=[vmem] * len(columns),
            compiler_params=kernel_params(32),
            cost_estimate=cost(0, 4 * slots * self.rows * self.width / 2**20),
        )(*parts, *after)
        self.send()
        return self.values[:1]

    def place(self, after=()):
        pieces = [x for pair in zip(self.values, self.arrived) for x in pair]
        slots = []
        for start, order in zip((0, self.half), self.order):
            slots += [(start, order), (start, [i ^ 1 for i in order])]
        count = lax.axis_size(AXES)
        return pl.pallas_call(
            functools.partial(place_kernel, slots=slots, rows=self.rows),
            out_shape=jax.ShapeDtypeStruct((count * self.rows, self.width), jnp.bfloat16),
            in_specs=[anywhere] * (len(pieces) + len(after)),
            out_specs=anywhere,
            scratch_shapes=[pltpu.SemaphoreType.DMA((2 * count,))],
            compiler_params=kernel_params(16),
            cost_estimate=cost(0, 4 * count * self.rows * self.width / 2**20),
        )(*pieces, *after)


def stage_kernel(ids, *refs, groups, extra):
    inputs = refs[: 2 * sum(count for _, count in groups)]
    outputs = refs[len(inputs) + extra :]
    for g, (bit, count) in enumerate(groups):
        send, keep = outputs[2 * g : 2 * g + 2]
        mine, rows = ids[bit], send.shape[1]
        start = 0
        for _ in range(count):
            left, right, *inputs = inputs
            for j in range(left.shape[2] // rows):
                columns, block = slice(start, start + left.shape[-1]), slice(j * rows, (j + 1) * rows)
                for i in range(left.shape[0]):
                    for out, b in ((send, 1 - mine), (keep, mine)):
                        total = left[i, b, block].astype(jnp.float32) + right[i, b, block].astype(jnp.float32)
                        out[i, :, columns] = total.astype(jnp.bfloat16)
                start += left.shape[-1]


class Chain:
    def __init__(self, ids, parts, rows, sides=(0, 1)):
        self.ids, self.rows = ids, rows
        self.rest = list(range(3, ids.shape[0]))
        self.sends = parts[1::2]
        self.next = [(1, 2)[side] for side in sides]
        self.groups = [
            [(keep, exchange(send, (2, 1)[side]), rows)]
            for keep, send, side in zip(parts[::2], parts[1::2], sides)
        ]

    def arrived(self):
        return [part[1] for group in self.groups for part in group]

    def advance(self, groups, bits, after):
        shaped, shapes = [], []
        for group in groups:
            columns = 0
            for keep, arrived, rows in group:
                shaped += [x.reshape(-1, 2, rows, x.shape[-1]) for x in (keep, arrived)]
                columns += keep.shape[-1] * rows // self.rows
            shapes += [jax.ShapeDtypeStruct((shaped[-1].shape[0], self.rows, columns), jnp.bfloat16)] * 2
        outs = pl.pallas_call(
            functools.partial(
                stage_kernel, groups=[(b, len(g)) for b, g in zip(bits, groups)], extra=len(after)
            ),
            out_shape=shapes,
            in_specs=[smem] + [vmem] * len(shaped) + [anywhere] * len(after),
            out_specs=[vmem] * len(shapes),
            compiler_params=kernel_params(32),
            cost_estimate=cost(0, sum(3 * x.size for x in shaped) / 2**20),
        )(self.ids, *shaped, *after)
        self.groups = [
            [(keep, exchange(send, b), self.rows)] for send, keep, b in zip(outs[::2], outs[1::2], bits)
        ]
        return outs[1::2]

    def join(self, other):
        self.rows = other.rows
        self.groups = [[part for chain in (self, other) for group in chain.groups for part in group]]

    def second(self, after=()):
        return self.advance(self.groups, self.next, after)

    def third(self, after=()):
        self.groups = [[part for group in self.groups for part in group]]
        return self.advance(self.groups, [self.rest.pop(0)], after)

    def finish(self):
        [[(keep, arrived, _)]] = self.groups
        return (keep.astype(jnp.float32) + arrived.astype(jnp.float32))[0]


def small_kernel(*refs, rows, count, owned):
    sums, bias, out = refs[:count], refs[count], refs[-1]
    lines = [sums[i][row : row + 1] for i, row in rows]
    lines += [jnp.zeros_like(lines[0])] * (128 - len(lines))
    out[:, :128] = jnp.concatenate(lines, axis=0).T
    out[:, 128:] = jnp.zeros((out.shape[0], 128), jnp.float32)
    for i in range(bias.shape[0]):
        out[i * owned : i * owned + 1, 128:] = bias[i : i + 1]


def small_block(lines, sums, bias, owned, after):
    width = sums[0].shape[1]
    devices = width // owned
    bias = bias.reshape(devices, -1)
    bias = jnp.pad(bias, ((0, 0), (0, 128 - bias.shape[1])))
    places = [([i for i, x in enumerate(sums) if x is s][0], row) for s, row in lines]
    block = pl.pallas_call(
        functools.partial(small_kernel, rows=places, count=len(sums), owned=owned),
        out_shape=jax.ShapeDtypeStruct((width, 256), jnp.float32),
        in_specs=[vmem] * (len(sums) + 1) + [anywhere] * len(after),
        out_specs=vmem,
        compiler_params=kernel_params(16),
        cost_estimate=cost(0, 2),
    )(*sums, bias, *after)
    return block.astype(jnp.bfloat16)


def add_product_kernel(*refs, count, base, extra):
    out = refs[-1]
    total = refs[2 * count][...] if base else jnp.zeros(out.shape, jnp.float32)
    for left, right in zip(refs[:count], refs[count : 2 * count]):
        total += dot(left[...], right[...], (1, 1))
    out[...] = total


def add_product(stack, places, weights, columns, rows, chunk, base=None, after=()):
    width = stack.shape[1]
    count = len(places)
    bases = [] if base is None else [base]
    block = pl.BlockSpec((chunk, width), lambda i: (i, 0))
    return pl.pallas_call(
        functools.partial(add_product_kernel, count=count, base=len(bases), extra=len(after)),
        grid=(rows // chunk,),
        out_shape=jax.ShapeDtypeStruct((rows, width), jnp.float32),
        in_specs=[pl.BlockSpec((chunk, width), lambda i, p=p: (p // chunk + i, 0)) for p in places]
        + [pl.BlockSpec((width, width), lambda i, c=c: (0, c)) for c in columns]
        + [block] * len(bases)
        + [anywhere] * len(after),
        out_specs=block,
        compiler_params=kernel_params(40),
        cost_estimate=cost(3 * rows * count * width * width, 12),
    )(*[stack] * count, *[weights] * count, *bases, *after)


def body(
    target_in,
    memory,
    block_rows,
    pad_rows,
    seq_lengths,
    self_qkv,
    self_out,
    cross_query,
    cross_kv,
    cross_out,
    ffn_in,
    ffn_out,
    norm_scale,
    small_bias,
    ffn_bias,
    cotangent,
):
    width = target_in.shape[1]
    owned = self_qkv.shape[0]
    me = lax.axis_index(AXES)
    core = (me & 1).reshape(1)
    ids = (me >> jnp.arange(lax.axis_size(AXES).bit_length() - 1)) & 1
    tokens, mems = target_in.shape[0], memory.shape[0]

    def turned(*arrays, after=()):
        keep, send = turn(core, arrays, owned, after)
        return keep, exchange(send, 0)

    pack = jnp.concatenate([norm_scale.T, small_bias.T, ffn_bias.reshape(owned, -1)], axis=1)
    small_cols = pack.shape[1]
    pack = jnp.pad(pack, ((0, 0), (0, -small_cols % 128)))
    early = Gather(jnp.concatenate([self_qkv, self_out, cross_query, pack], axis=1))
    late = Gather(jnp.concatenate([cross_kv, cross_out], axis=1))
    memory_turned = turned(memory)
    target_turned = turned(target_in, after=memory_turned[:1])
    last = target_turned[:1]
    for _ in range(early.count + 2):
        last = early.step(last)
        if early.stage == early.count:
            packed = lax.all_gather(pack_ffn(ffn_in, ffn_out, last), AXES)
        if early.stage < early.count + 2:
            last = late.step(last)
    early = early.place(last)

    w_qkv, w_self, w_query = early[:, : 3 * width], early[:, 3 * width : 4 * width], early[:, 4 * width : 5 * width]
    small = early[:, 5 * width : 5 * width + small_cols].astype(jnp.float32)
    gains = small[:, :3].T
    biases = small[:, 3:13].T
    in_bias = small[:, 13:].reshape(1, -1)

    bound = memory_bounds(block_rows[0], pad_rows[0])
    lengths = seq_lengths[0]
    zeros = jnp.zeros((width,), jnp.float32)
    qkv = (matmul(target_in, w_qkv) + jnp.concatenate([biases[0], zeros, biases[1]])).astype(
        jnp.bfloat16
    )
    self_context, self_summary = self_forward(lengths, qkv)
    first, first_unit, first_inverse = normalize(
        target_in.astype(jnp.float32) + matmul(self_context, w_self) + biases[2],
        gains[0],
        biases[7],
    )
    first_low = first.astype(jnp.bfloat16)
    self_turned = turned(self_context, first_low)
    cross_q = (matmul(first_low, w_query) + biases[3]).astype(jnp.bfloat16)
    late.step((cross_q, self_turned[0]))
    late = late.place()
    w_pairs, w_cross = late[:, : 2 * width], late[:, 2 * width :]
    cross_pairs = (matmul(memory, w_pairs) + jnp.concatenate([zeros, biases[4]])).astype(
        jnp.bfloat16
    )
    cross_context, cross_summary = cross_forward(bound, cross_q, cross_pairs)
    second, second_unit, second_inverse = normalize(
        first + matmul(cross_context, w_cross) + biases[5], gains[1], biases[8]
    )

    cross_turned = turned(cross_context, second)
    vectors = jnp.concatenate([biases[6:7], gains[2:3], biases[9:10], jnp.zeros((5, width), jnp.float32)])
    hidden, hidden_send, slope, block_out, third_grad, out_grad, third_sums = ffn_forward(
        core,
        second,
        packed,
        in_bias,
        cotangent,
        vectors,
        ffn_out.shape[0],
        after=(memory_turned[1], target_turned[1], self_turned[1]),
    )
    hidden_other, out_grad_other = exchange(hidden_send, 0), exchange(out_grad, 0)
    pre_grad, ffn_bias_grad, second_grad, cross_branch, second_sums = ffn_backward(
        packed, slope, third_grad, out_grad, second_unit, second_inverse, gains[1:2], cross_turned[1:]
    )
    pre_grad_other = exchange(pre_grad, 0)
    parts = products(
        ids,
        [(hidden, tokens, 0), (hidden_other, tokens, 0)],
        [(out_grad, out_grad_other, tokens)],
        [(0, tokens, tokens, 0, 0, width)],
        ffn_out.shape[0],
        512,
        sides=(0,),
        after=(pre_grad,),
    )
    out_chain = Chain(ids, parts, ffn_out.shape[0], sides=(0,))
    parts = products(
        ids,
        [(x, tokens, 1) for x in cross_turned],
        [(pre_grad, pre_grad_other, tokens)],
        [(0, tokens, tokens, 0, 0, ffn_in.shape[1])],
        owned,
        1024,
        sides=(1,),
        after=out_chain.sends,
    )
    in_chain = Chain(ids, parts, owned, sides=(1,))

    cross_delta, cross_sums = cross_backward(
        bound, cross_q, cross_pairs, cross_summary, cross_branch, late, 2, after=in_chain.sends
    )
    cross_other = exchange(cross_delta, 0)
    self_delta, self_sums, first_grad = self_backward(
        lengths,
        qkv,
        self_summary,
        second_grad,
        cross_delta,
        early,
        first_unit,
        first_inverse,
        gains[0:1],
    )
    self_other = exchange(self_delta, 0)
    small_grad = small_block(
        [
            (self_sums, 3),
            (second_sums, 0),
            (third_sums, 0),
            (self_sums, 0),
            (self_sums, 1),
            (self_sums, 2),
            (cross_sums, 0),
            (cross_sums, 1),
            (second_sums, 2),
            (third_sums, 2),
            (self_sums, 4),
            (second_sums, 1),
            (third_sums, 1),
        ],
        [self_sums, cross_sums, second_sums, third_sums],
        ffn_bias_grad,
        owned,
        (self_sums,),
    )
    bits = list(range(lax.axis_size(AXES).bit_length() - 1))[::-1]
    small_part = small_grad.reshape((2,) * len(bits) + (owned, -1))
    for bit in (0, 1):
        mine = (me >> bit) & 1
        small_keep, small_send = [
            lax.dynamic_index_in_dim(small_part, i, bits.index(bit), keepdims=False)
            for i in (mine, 1 - mine)
        ]
        small_other = exchange(small_send, bit)
        small_part = (small_keep.astype(jnp.float32) + small_other.astype(jnp.float32)).astype(jnp.bfloat16)
        bits.remove(bit)
    beyond = mems + 2 * tokens
    parts = products(
        ids,
        [
            part
            for i in range(2)
            for part in (
                (memory_turned[i], mems, 0),
                (self_turned[i], tokens, 1),
                (cross_turned[i], tokens, 0),
            )
        ],
        [(cross_delta, cross_other, mems), (cross_delta, cross_other, mems // 2)],
        [
            (mems, beyond + mems, tokens, 1, 4, width),
            (0, beyond, mems, 0, 0, width),
            (0, beyond, mems, 0, 1, width),
            (mems + tokens, beyond + mems + tokens, tokens, 1, 5, width),
        ],
        owned,
        1024,
        after=in_chain.second(after=out_chain.second(after=(small_grad,))),
    )
    cross_chain = Chain(ids, parts, owned)
    out_chain.join(in_chain)
    parts = products(
        ids,
        [part for i in range(2) for part in ((target_turned[i], tokens, 0), (self_turned[i], tokens, 0))],
        [(self_delta, self_other, tokens)],
        [(0, 2 * tokens, tokens, 0, i, width) for i in range(3)]
        + [(tokens, 3 * tokens, tokens, 0, 3, width)],
        owned,
        1024,
        after=(*out_chain.third(after=parts[:1]), small_other),
    )
    self_chain = Chain(ids, parts, owned)
    self_chain.groups[1].append((small_keep, small_other, owned))
    last = cross_chain.second(after=parts[:1])
    memory_grad = add_product(cross_delta, [0, mems], late, [0, 1], mems, 512, after=last)
    last = (memory_grad,)
    while out_chain.rest:
        last = out_chain.third(after=last)
    target_grad = add_product(
        self_delta,
        [0, tokens, 2 * tokens],
        early,
        [0, 1, 2],
        tokens,
        tokens,
        first_grad,
        after=last,
    )
    last = self_chain.second(after=(target_grad,))
    last = cross_chain.third(after=last)
    last = self_chain.third(after=last)
    while self_chain.rest:
        last = cross_chain.third(after=last)
        last = self_chain.third(after=last)
    ffn_shard = out_chain.finish()
    size = ffn_in.shape[1]
    ffn_out_shard = ffn_shard[:, :size].reshape(owned, -1, width).swapaxes(0, 1).reshape(ffn_out.shape)
    ffn_in_shard = ffn_shard[:, size:]
    cross_shard = cross_chain.finish()
    self_shard = self_chain.finish()
    small_shard = self_shard[:, 4 * width :]
    return (
        block_out,
        target_grad,
        memory_grad,
        self_shard[:, : 3 * width],
        self_shard[:, 3 * width : 4 * width],
        cross_shard[:, :width],
        cross_shard[:, width : 3 * width],
        cross_shard[:, 3 * width :],
        ffn_in_shard,
        ffn_out_shard,
        small_shard[:, :3].T,
        small_shard[:, 3:13].T,
        small_shard[0, 128 : 128 + ffn_bias.shape[0]],
    )


def solution(mesh):
    in_specs = (
        P(("wide", "narrow"), None),
        P(("wide", "narrow"), None),
        P(("wide", "narrow"), None),
        P(("wide", "narrow"), None),
        P(("wide", "narrow"), None),
        P(("wide", "narrow"), None),
        P(("wide", "narrow"), None),
        P(("wide", "narrow"), None),
        P(("wide", "narrow"), None),
        P(("wide", "narrow"), None),
        P(("wide", "narrow"), None),
        P(("wide", "narrow"), None),
        P(None, ("wide", "narrow")),
        P(None, ("wide", "narrow")),
        P(("wide", "narrow")),
        P(("wide", "narrow"), None),
    )
    out_specs = (
        P(("wide", "narrow"), None),
        P(("wide", "narrow"), None),
        P(("wide", "narrow"), None),
        P(("wide", "narrow"), None),
        P(("wide", "narrow"), None),
        P(("wide", "narrow"), None),
        P(("wide", "narrow"), None),
        P(("wide", "narrow"), None),
        P(("wide", "narrow"), None),
        P(("wide", "narrow"), None),
        P(None, ("wide", "narrow")),
        P(None, ("wide", "narrow")),
        P(("wide", "narrow")),
    )
    return jax.shard_map(body, mesh=mesh, in_specs=in_specs, out_specs=out_specs, check_vma=False)
```

```python
import functools

import jax
import jax.numpy as jnp
from jax import lax
from jax.experimental import pallas as pl
from jax.experimental.pallas import tpu as pltpu
from jax.sharding import PartitionSpec as P

HEADS = 16
HEAD_DIM = 64
SEQ_LEN = 128
PAIRS = HEADS // 2
neg_fill = -1e30
AXES = ("wide", "narrow")
vmem = pl.BlockSpec(memory_space=pltpu.VMEM)
smem = pl.BlockSpec(memory_space=pltpu.SMEM)
anywhere = pl.BlockSpec(memory_space=pl.ANY)
norm_eps = 1e-05


def kernel_params(megabytes):
    return pltpu.CompilerParams(vmem_limit_bytes=megabytes << 20)


def cost(flops, megabytes, transcendentals=0):
    return pl.CostEstimate(
        flops=int(10 * flops), bytes_accessed=int(10 * megabytes * 2**20), transcendentals=int(10 * transcendentals)
    )


def matmul(first, second):
    return jnp.dot(first, second, preferred_element_type=jnp.float32)


def inner_cols(first, second):
    return lax.dot_general(
        first, second, (((1,), (1,)), ((), ())), preferred_element_type=jnp.float32
    )


def column_sums(values):
    return jnp.sum(values.astype(jnp.float32), axis=0)


def memory_bounds(block_rows, pad_rows):
    count = block_rows.shape[0]
    before = jnp.arange(count)[None, :] < jnp.arange(count)[:, None]
    starts = jnp.sum(jnp.where(before, block_rows[None, :], 0), axis=1)
    valid = jnp.maximum(block_rows - pad_rows, (block_rows + 1) // 2)
    return jnp.stack([starts, starts + valid])


def dot(first, second, contract):
    return lax.dot_general(
        first, second, ((contract[:1], contract[1:]), ((), ())), preferred_element_type=jnp.float32
    )


def cols(pair, base=0):
    return slice((base + pair) * 128, (base + pair + 1) * 128)


def split_heads(block):
    low = lax.broadcasted_iota(jnp.int32, block.shape, 1) < HEAD_DIM
    zero = jnp.zeros_like(block)
    return jnp.concatenate([jnp.where(low, block, zero), jnp.where(low, zero, block)], axis=0)


def join_heads(stacked):
    low = lax.broadcasted_iota(jnp.int32, (SEQ_LEN, 128), 1) < HEAD_DIM
    return jnp.where(low, stacked[:SEQ_LEN], stacked[SEQ_LEN:])


def join_heads_t(stacked):
    both = jnp.concatenate([stacked[:HEAD_DIM, :SEQ_LEN], stacked[HEAD_DIM:, SEQ_LEN:]], axis=0)
    return both.T


def cross_mask(tile, low, high):
    rows = tile * 128 + lax.broadcasted_iota(jnp.int32, (128, 2 * SEQ_LEN), 0)
    return (rows >= low) & (rows < high)


def cross_forward_kernel(bound, q, pairs, *rest, extra):
    context, summary, stack, scores, top, total, acc = rest[extra:]

    def sequence(s, carry):
        low, high = bound[0, s], bound[1, s]
        first, last = low // 128, (high + 127) // 128
        rows = pl.ds(pl.multiple_of(s * SEQ_LEN, SEQ_LEN), SEQ_LEN)
        for p in range(PAIRS):
            stack[p] = split_heads(q[rows, cols(p)] * jnp.bfloat16(HEAD_DIM**-0.5))
        top[...] = jnp.full_like(top, neg_fill)
        total[...] = jnp.zeros_like(total)
        acc[...] = jnp.zeros_like(acc)

        def one(t, carry):
            keys = pl.ds(pl.multiple_of(t * 128, 128), 128)
            ok = cross_mask(t, low, high)
            for p in range(PAIRS):
                raw = jnp.where(ok, dot(pairs[keys, cols(p)], stack[p], (1, 1)), neg_fill)
                scores[t, p] = raw
                top[p] = jnp.maximum(top[p], jnp.max(raw, axis=0, keepdims=True))
            return carry

        lax.fori_loop(first, last, one, 0)

        def two(t, carry):
            keys = pl.ds(pl.multiple_of(t * 128, 128), 128)
            for p in range(PAIRS):
                weights = jnp.exp(scores[t, p] - top[p])
                total[p] += jnp.sum(weights, axis=0, keepdims=True)
                acc[p] += dot(pairs[keys, cols(p, PAIRS)], weights.astype(jnp.bfloat16), (0, 0))
            return carry

        lax.fori_loop(first, last, two, 0)
        for p in range(PAIRS):
            context[rows, cols(p)] = join_heads_t(acc[p] / total[p]).astype(jnp.bfloat16)
            summary[s, p] = top[p] + jnp.log(total[p])
        return carry

    lax.fori_loop(0, bound.shape[1], sequence, 0)


def cross_backward_kernel(bound, q, pairs, summary, branch, weight, *rest, extra):
    out, sums, grad, stack, grads, probs, prob_grads, delta, acc, pair_acc = rest[extra:]
    pair_acc[...] = jnp.zeros_like(pair_acc)
    scale = HEAD_DIM**-0.5
    (tokens, width), mems = q.shape, pairs.shape[0]
    grad[...] = dot(branch[...], weight[...], (1, 1)).astype(jnp.bfloat16)
    pad = (out.shape[0] - 2 * mems) // 2
    query_at, branch_at = 2 * mems, 2 * mems + pad

    def sequence(s, carry):
        low, high = bound[0, s], bound[1, s]
        first, last = low // 128, (high + 127) // 128
        rows = pl.ds(pl.multiple_of(s * SEQ_LEN, SEQ_LEN), SEQ_LEN)
        for p in range(PAIRS):
            stack[p] = split_heads(q[rows, cols(p)] * jnp.bfloat16(scale))
            grads[p] = split_heads(grad[rows, cols(p)])
        delta[...] = jnp.zeros_like(delta)
        acc[...] = jnp.zeros_like(acc)

        def one(t, carry):
            keys = pl.ds(pl.multiple_of(t * 128, 128), 128)
            ok = cross_mask(t, low, high)
            for p in range(PAIRS):
                raw = dot(pairs[keys, cols(p)], stack[p], (1, 1))
                weights = jnp.where(ok, jnp.exp(raw - summary[s, p]), 0.0)
                back = dot(pairs[keys, cols(p, PAIRS)], grads[p], (1, 1))
                delta[p] += jnp.sum(weights * back, axis=0, keepdims=True)
                probs[t, p] = weights
                prob_grads[t, p] = back
                pair_acc[keys, cols(p, PAIRS)] += dot(weights.astype(jnp.bfloat16), grads[p], (1, 0))
            return carry

        lax.fori_loop(first, last, one, 0)

        def two(t, carry):
            keys = pl.ds(pl.multiple_of(t * 128, 128), 128)
            for p in range(PAIRS):
                score = (probs[t, p] * (prob_grads[t, p] - delta[p])).astype(jnp.bfloat16)
                pair_acc[keys, cols(p)] += dot(score, stack[p], (1, 0))
                acc[p] += dot(pairs[keys, cols(p)], score, (0, 0))
            return carry

        lax.fori_loop(first, last, two, 0)
        for p in range(PAIRS):
            place = pl.ds(pl.multiple_of(query_at + s * SEQ_LEN, SEQ_LEN), SEQ_LEN)
            out[place, cols(p)] = (join_heads_t(acc[p]) * scale).astype(jnp.bfloat16)
        return carry

    lax.fori_loop(0, bound.shape[1], sequence, 0)
    out[:mems, :] = pair_acc[:, :width].astype(jnp.bfloat16)
    out[mems:query_at, :] = pair_acc[:, width:].astype(jnp.bfloat16)
    out[branch_at : branch_at + tokens, :] = branch[...]
    for at in (query_at, branch_at):
        out[at + tokens : at + pad, :] = jnp.zeros((pad - tokens, width), jnp.bfloat16)
    sums[...] = sum_rows(
        out[query_at : query_at + tokens, :].astype(jnp.float32), out[mems:query_at, :].astype(jnp.float32)
    )


def cross_forward(bound, q, pairs, after=()):
    seqs, tiles = bound.shape[1], pairs.shape[0] // 128
    wide = 2 * SEQ_LEN
    return pl.pallas_call(
        functools.partial(cross_forward_kernel, extra=len(after)),
        out_shape=(
            jax.ShapeDtypeStruct(q.shape, jnp.bfloat16),
            jax.ShapeDtypeStruct((seqs, PAIRS, 1, wide), jnp.float32),
        ),
        in_specs=[smem, vmem, vmem] + [anywhere] * len(after),
        out_specs=(vmem, vmem),
        scratch_shapes=[
            pltpu.VMEM((PAIRS, wide, 128), jnp.bfloat16),
            pltpu.VMEM((tiles, PAIRS, 128, wide), jnp.float32),
            pltpu.VMEM((PAIRS, 1, wide), jnp.float32),
            pltpu.VMEM((PAIRS, 1, wide), jnp.float32),
            pltpu.VMEM((PAIRS, 128, wide), jnp.float32),
        ],
        compiler_params=kernel_params(40),
        cost_estimate=cost(8e9, 8),
    )(bound, q, pairs, *after)


def cross_backward(bound, q, pairs, summary, branch, weights, column, after=()):
    seqs, tiles = bound.shape[1], pairs.shape[0] // 128
    wide = 2 * SEQ_LEN
    width = q.shape[1]
    whole = lambda shape: pl.BlockSpec(shape, lambda i: (0,) * len(shape))
    rows = 3 * pairs.shape[0]
    return pl.pallas_call(
        functools.partial(cross_backward_kernel, extra=len(after)),
        grid=(1,),
        out_shape=(
            jax.ShapeDtypeStruct((rows, width), jnp.bfloat16),
            jax.ShapeDtypeStruct((8, width), jnp.float32),
        ),
        in_specs=[smem]
        + [whole(x.shape) for x in (q, pairs, summary, branch)]
        + [pl.BlockSpec((width, width), lambda i: (0, column))]
        + [anywhere] * len(after),
        out_specs=(whole((rows, width)), whole((8, width))),
        scratch_shapes=[
            pltpu.VMEM(q.shape, jnp.bfloat16),
            pltpu.VMEM((PAIRS, wide, 128), jnp.bfloat16),
            pltpu.VMEM((PAIRS, wide, 128), jnp.bfloat16),
            pltpu.VMEM((tiles, PAIRS, 128, wide), jnp.float32),
            pltpu.VMEM((tiles, PAIRS, 128, wide), jnp.float32),
            pltpu.VMEM((PAIRS, 1, wide), jnp.float32),
            pltpu.VMEM((PAIRS, 128, wide), jnp.float32),
            pltpu.VMEM(pairs.shape, jnp.float32),
        ],
        compiler_params=kernel_params(58),
        cost_estimate=cost(16e9, 12),
    )(bound, q, pairs, summary, branch, weights, *after)


def self_mask(length):
    keys = lax.broadcasted_iota(jnp.int32, (SEQ_LEN, 2 * SEQ_LEN), 0)
    tokens = lax.broadcasted_iota(jnp.int32, (SEQ_LEN, 2 * SEQ_LEN), 1) & (SEQ_LEN - 1)
    return (keys <= tokens) & (keys < length)


def self_forward_kernel(lengths, qkv, *rest, extra):
    context, summary = rest[extra:]

    def sequence(s, carry):
        ok = self_mask(lengths[s])
        rows = pl.ds(pl.multiple_of(s * SEQ_LEN, SEQ_LEN), SEQ_LEN)
        for p in range(PAIRS):
            stack = split_heads(qkv[rows, cols(p)] * jnp.bfloat16(HEAD_DIM**-0.5))
            raw = jnp.where(ok, dot(qkv[rows, cols(p, PAIRS)], stack, (1, 1)), neg_fill)
            top = jnp.max(raw, axis=0, keepdims=True)
            weights = jnp.exp(raw - top)
            total = jnp.sum(weights, axis=0, keepdims=True)
            weights = (weights / total).astype(jnp.bfloat16)
            acc = dot(qkv[rows, cols(p, 2 * PAIRS)], weights, (0, 0))
            context[rows, cols(p)] = join_heads_t(acc).astype(jnp.bfloat16)
            summary[s, p] = top + jnp.log(total)
        return carry

    lax.fori_loop(0, lengths.shape[0], sequence, 0)


def self_backward_kernel(
    lengths, qkv, summary, second_grad, query_delta, w_query, w_self, unit, inverse, gain, *rest, extra
):
    out, sums, first_grad, grad = rest[extra:]
    scale = HEAD_DIM**-0.5
    tokens = qkv.shape[0]
    total = second_grad[...] + dot(query_delta[:tokens, :], w_query[...], (1, 1))
    first = normalize_back(total, unit[...], inverse[...], gain[...])
    first_grad[...] = first
    branch = first.astype(jnp.bfloat16)
    out[3 * tokens :, :] = branch
    grad[...] = dot(branch, w_self[...], (1, 1)).astype(jnp.bfloat16)

    def sequence(s, carry):
        ok = self_mask(lengths[s])
        rows = pl.ds(pl.multiple_of(s * SEQ_LEN, SEQ_LEN), SEQ_LEN)
        for p in range(PAIRS):
            stack = split_heads(qkv[rows, cols(p)] * jnp.bfloat16(scale))
            grads = split_heads(grad[rows, cols(p)])
            keys = qkv[rows, cols(p, PAIRS)]
            raw = dot(keys, stack, (1, 1))
            weights = jnp.where(ok, jnp.exp(raw - summary[s, p]), 0.0)
            back = dot(qkv[rows, cols(p, 2 * PAIRS)], grads, (1, 1))
            delta = jnp.sum(weights * back, axis=0, keepdims=True)
            score = (weights * (back - delta)).astype(jnp.bfloat16)
            value_grad = dot(weights.astype(jnp.bfloat16), grads, (1, 0))
            key_grad = dot(score, stack, (1, 0))
            query_grad = join_heads_t(dot(keys, score, (0, 0))) * scale
            for i, part in enumerate((query_grad, key_grad, value_grad)):
                place = pl.ds(pl.multiple_of(i * tokens + s * SEQ_LEN, SEQ_LEN), SEQ_LEN)
                out[place, cols(p)] = part.astype(jnp.bfloat16)
        return carry

    lax.fori_loop(0, lengths.shape[0], sequence, 0)
    sums[...] = sum_rows(
        *[out[i * tokens : (i + 1) * tokens, :].astype(jnp.float32) for i in (0, 2, 3)],
        total * unit[...],
        total,
    )


def self_forward(lengths, qkv, after=()):
    tokens, width = qkv.shape[0], qkv.shape[1] // 3
    return pl.pallas_call(
        functools.partial(self_forward_kernel, extra=len(after)),
        out_shape=(
            jax.ShapeDtypeStruct((tokens, width), jnp.bfloat16),
            jax.ShapeDtypeStruct((lengths.shape[0], PAIRS, 1, 2 * SEQ_LEN), jnp.float32),
        ),
        in_specs=[smem, vmem] + [anywhere] * len(after),
        out_specs=(vmem, vmem),
        compiler_params=kernel_params(24),
        cost_estimate=cost(2e9, 4),
    )(lengths, qkv, *after)


def self_backward(
    lengths, qkv, summary, second_grad, cross_delta, weights, unit, inverse, gain, after=()
):
    tokens, width = second_grad.shape
    whole = lambda shape: pl.BlockSpec(shape, lambda i: (0,) * len(shape))
    full = whole((tokens, width))
    return pl.pallas_call(
        functools.partial(self_backward_kernel, extra=len(after)),
        grid=(1,),
        out_shape=(
            jax.ShapeDtypeStruct((4 * tokens, width), jnp.bfloat16),
            jax.ShapeDtypeStruct((8, width), jnp.float32),
            jax.ShapeDtypeStruct((tokens, width), jnp.float32),
        ),
        in_specs=[
            smem,
            whole(qkv.shape),
            whole(summary.shape),
            full,
            pl.BlockSpec((cross_delta.shape[0] // 6, width), lambda i: (4, 0)),
            pl.BlockSpec((width, width), lambda i: (0, 4)),
            pl.BlockSpec((width, width), lambda i: (0, 3)),
            full,
            whole((tokens, 1)),
            whole((1, width)),
        ]
        + [anywhere] * len(after),
        out_specs=(whole((4 * tokens, width)), whole((8, width)), full),
        scratch_shapes=[pltpu.VMEM((tokens, width), jnp.bfloat16)],
        compiler_params=kernel_params(48),
        cost_estimate=cost(6e9, 12),
    )(lengths, qkv, summary, second_grad, cross_delta, weights, weights, unit, inverse, gain, *after)


def normalize(values, gain, shift):
    centered = values - jnp.mean(values, axis=-1, keepdims=True)
    inverse = lax.rsqrt(jnp.mean(centered * centered, axis=-1, keepdims=True) + norm_eps)
    unit = centered * inverse
    return (unit * gain + shift, unit, inverse)


def normalize_back(grad, unit, inverse, gain):
    scaled = grad * gain
    inner = (
        scaled
        - jnp.mean(scaled, axis=-1, keepdims=True)
        - unit * jnp.mean(scaled * unit, axis=-1, keepdims=True)
    )
    return inverse * inner


def sum_rows(*rows):
    stacked = [jnp.sum(r, axis=0, keepdims=True) for r in rows]
    return jnp.concatenate(stacked + [jnp.zeros_like(stacked[0])] * (8 - len(rows)), axis=0)


def deal(core, turned, rows, keep, send):
    for i in range(turned.shape[0] // (2 * rows)):
        even = turned[2 * i * rows : (2 * i + 1) * rows]
        odd = turned[(2 * i + 1) * rows : (2 * i + 2) * rows]
        here = slice(i * rows, (i + 1) * rows)
        keep(here, jnp.where(core == 0, even, odd).astype(jnp.bfloat16))
        send(here, jnp.where(core == 0, odd, even).astype(jnp.bfloat16))


def into(ref, columns):
    def store(rows, values):
        ref[rows, columns] = values

    return store


def turn_kernel(core, *refs, rows, count):
    arrays, (keep, send) = refs[:count], refs[-2:]
    start = 0
    for array in arrays:
        tokens = array.shape[0]
        columns = slice(start, start + tokens)
        turned = array[...].astype(jnp.float32 if rows % 16 else jnp.bfloat16).T
        deal(core[0], turned, rows, into(keep, columns), into(send, columns))
        start += tokens


def turn(core, arrays, rows, after=()):
    width = arrays[0].shape[1]
    half = jax.ShapeDtypeStruct((width // 2, sum(x.shape[0] for x in arrays)), jnp.bfloat16)
    return pl.pallas_call(
        functools.partial(turn_kernel, rows=rows, count=len(arrays)),
        out_shape=(half, half),
        in_specs=[smem] + [vmem] * len(arrays) + [anywhere] * len(after),
        out_specs=(vmem, vmem),
        compiler_params=kernel_params(32),
        cost_estimate=cost(0, 8),
    )(core, *arrays, *after)


def flat(block):
    values = block[...]
    if values.shape[1] % 16:
        values = values.astype(jnp.float32)
    return values.reshape(-1, values.shape[-1]).astype(jnp.bfloat16)


def weight_blocks(packed, chunk):
    devices, rows, width = packed.shape
    hidden = devices * rows // 2
    strips, owned = width // chunk, rows * width // (2 * hidden)
    return [
        pl.BlockSpec((devices, owned, chunk), lambda j: (0, j // strips, j % strips)),
        pl.BlockSpec((devices * chunk // hidden, rows // 2, width), lambda j: (j, 1, 0)),
    ]


def ffn_forward_kernel(
    core, second, w_in, w_out, bias, cot, vectors, *rest, rows, extra
):
    keep, send, slope, block_out, third_grad, out_grad, sums, acc, low = rest[extra:]

    step = pl.program_id(0)

    @pl.when(step == 0)
    def _():
        low[...] = second[...].astype(jnp.bfloat16)
        acc[...] = second[...] + vectors[0:1]

    pre = dot(low[...], flat(w_in), (1, 0)) + bias[...]
    part = 0.5 + 0.5 * lax.erf(pre * 0.5**0.5)
    active = (pre * part).astype(jnp.bfloat16)
    everything = slice(None)
    deal(core[0], active.T, rows, into(keep, everything), into(send, everything))
    slope[...] = (part + pre * jnp.exp(-0.5 * pre * pre) * 0.3989422804014327).astype(jnp.bfloat16)
    acc[...] += dot(active, flat(w_out), (1, 0))

    @pl.when(step == pl.num_programs(0) - 1)
    def _():
        gain = vectors[1:2]
        third, unit, inverse = normalize(acc[...], gain, vectors[2:3])
        block_out[...] = third.astype(jnp.bfloat16)
        grad = cot[...].astype(jnp.float32)
        third = normalize_back(grad, unit, inverse, gain)
        third_grad[...] = third
        lower = third.astype(jnp.bfloat16)
        out_grad[...] = lower
        sums[...] = sum_rows(grad * unit, grad, lower.astype(jnp.float32))


def ffn_forward(core, second, packed, bias, cot, vectors, rows, after):
    tokens, width = second.shape
    hidden = packed.shape[0] * packed.shape[1] // 2
    chunk = 1024
    whole = lambda shape: pl.BlockSpec(shape, lambda j: (0, 0))
    full = whole((tokens, width))
    strip = pl.BlockSpec((tokens, chunk), lambda j: (0, j))
    turned = pl.BlockSpec((chunk // 2, tokens), lambda j: (j, 0))
    return pl.pallas_call(
        functools.partial(ffn_forward_kernel, rows=rows, extra=len(after)),
        grid=(hidden // chunk,),
        out_shape=(
            jax.ShapeDtypeStruct((hidden // 2, tokens), jnp.bfloat16),
            jax.ShapeDtypeStruct((hidden // 2, tokens), jnp.bfloat16),
            jax.ShapeDtypeStruct((tokens, hidden), jnp.bfloat16),
            jax.ShapeDtypeStruct((tokens, width), jnp.bfloat16),
            jax.ShapeDtypeStruct((tokens, width), jnp.float32),
            jax.ShapeDtypeStruct((tokens, width), jnp.bfloat16),
            jax.ShapeDtypeStruct((8, width), jnp.float32),
        ),
        in_specs=[
            smem,
            full,
            *weight_blocks(packed, chunk),
            pl.BlockSpec((1, chunk), lambda j: (0, j)),
            full,
            whole((8, width)),
        ]
        + [anywhere] * len(after),
        out_specs=(turned, turned, strip, full, full, full, whole((8, width))),
        scratch_shapes=[
            pltpu.VMEM((tokens, width), jnp.float32),
            pltpu.VMEM((tokens, width), jnp.bfloat16),
        ],
        compiler_params=kernel_params(40),
        cost_estimate=cost(16e9, 26, 4e6),
    )(core, second, packed, packed, bias, cot, vectors, *after)


def ffn_backward_kernel(
    w_in, w_out, slope, third_grad, out_grad, unit, inverse, gain, *rest, extra
):
    pre_grad, bias_grad, second_grad, branch, sums, acc = rest[extra:]
    step = pl.program_id(0)

    @pl.when(step == 0)
    def _():
        acc[...] = third_grad[...]

    grad = dot(out_grad[...], flat(w_out), (1, 1)) * slope[...].astype(jnp.float32)
    lower = grad.astype(jnp.bfloat16)
    pre_grad[...] = lower
    bias_grad[...] = jnp.sum(lower.astype(jnp.float32), axis=0, keepdims=True)
    acc[...] += dot(lower, flat(w_in), (1, 1))

    @pl.when(step == pl.num_programs(0) - 1)
    def _():
        total = acc[...]
        grad = normalize_back(total, unit[...], inverse[...], gain[...])
        second_grad[...] = grad
        lower = grad.astype(jnp.bfloat16)
        branch[...] = lower
        sums[...] = sum_rows(total * unit[...], total, lower.astype(jnp.float32))


def ffn_backward(packed, slope, third_grad, out_grad, unit, inverse, gain, after):
    tokens, width = third_grad.shape
    hidden = packed.shape[0] * packed.shape[1] // 2
    chunk = 1024
    whole = lambda shape: pl.BlockSpec(shape, lambda j: (0, 0))
    full = whole((tokens, width))
    strip = pl.BlockSpec((tokens, chunk), lambda j: (0, j))
    return pl.pallas_call(
        functools.partial(ffn_backward_kernel, extra=len(after)),
        grid=(hidden // chunk,),
        out_shape=(
            jax.ShapeDtypeStruct((tokens, hidden), jnp.bfloat16),
            jax.ShapeDtypeStruct((1, hidden), jnp.float32),
            jax.ShapeDtypeStruct((tokens, width), jnp.float32),
            jax.ShapeDtypeStruct((tokens, width), jnp.bfloat16),
            jax.ShapeDtypeStruct((8, width), jnp.float32),
        ),
        in_specs=[
            *weight_blocks(packed, chunk),
            strip,
            full,
            full,
            full,
            whole((tokens, 1)),
            whole((1, width)),
        ]
        + [anywhere] * len(after),
        out_specs=(strip, pl.BlockSpec((1, chunk), lambda j: (0, j)), full, full, whole((8, width))),
        scratch_shapes=[pltpu.VMEM((tokens, width), jnp.float32)],
        compiler_params=kernel_params(40),
        cost_estimate=cost(14e9, 26),
    )(packed, packed, slope, third_grad, out_grad, unit, inverse, gain, *after)


def product_kernel(ids, *refs, spans, n_left, n_right, rows, chunk, extra, sides):
    lefts, rights = refs[:n_left], refs[n_left : n_left + 2 * n_right]
    rest = refs[n_left + 2 * n_right + extra :]
    outs, (ordered, *wide) = rest[: 2 * len(sides)], rest[2 * len(sides) :]
    step = pl.program_id(0)
    blocks = lefts[0].shape[0] // rows
    half = blocks // 2 * rows

    @pl.when(step == 0)
    def _():
        start = 0
        for left in lefts:
            source, size = left, left.shape[1]
            if wide:
                source = wide[0].at[:, pl.ds(0, size)]
                source[...] = left[...].astype(jnp.float32)
            for side, order in enumerate(sides):
                bit = 1 - order
                for i in range(blocks):
                    low, high = i % (1 << bit), (i % (blocks // 2)) >> bit
                    mine = ids[2 - order] if i < blocks // 2 else 1 - ids[2 - order]
                    place = (high << (bit + 1)) + (mine << bit) + low
                    taken = source[pl.ds(pl.multiple_of(place * rows, rows), rows), :]
                    ordered[side, i * rows : (i + 1) * rows, start : start + size] = taken.astype(jnp.bfloat16)
            start += size

    steps = sum(s[-1] for s in spans)
    first = 0
    for mine, other, tokens, which, _, count in spans:
        for side in range(len(sides)):
            keep, send = outs[2 * side : 2 * side + 2]
            low = max(first, side * steps // len(sides))
            high = min(first + count, (side + 1) * steps // len(sides))
            if low >= high:
                continue

            @pl.when((step >= low) & (step < high))
            def _(mine=mine, other=other, tokens=tokens, which=which, side=side, keep=keep, send=send):
                total = dot(
                    ordered[side, :, mine : mine + tokens], rights[2 * which][:tokens, :], (1, 0)
                ) + dot(
                    ordered[side, :, other : other + tokens], rights[2 * which + 1][:tokens, :], (1, 0)
                )
                keep[...] = total[:half].astype(jnp.bfloat16)
                send[...] = total[half:].astype(jnp.bfloat16)

        first += count


def products(ids, lefts, rights, spans, rows, chunk, sides=(0, 1), after=()):
    height = lefts[0][0].shape[0]
    columns = sum(s[-1] for s in spans)
    steps = columns // chunk
    spans = [(*s[:-1], s[-1] // chunk) for s in spans]
    count = len(sides)
    part = jax.ShapeDtypeStruct((height // 2, columns // count), jnp.bfloat16)
    blocks = [
        pl.BlockSpec(
            (height // 2, chunk),
            lambda j, side=side: (0, jnp.clip(j - side * steps // count, 0, steps // count - 1)),
        )
        for side in range(count)
        for _ in range(2)
    ]
    tokens = sum(x[1] for x in lefts)
    wide = [pltpu.VMEM((height, max(x[1] for x in lefts)), jnp.float32)] if rows % 16 else []
    taken = [pl.BlockSpec((height, size), lambda j, place=place: (0, place)) for _, size, place in lefts]

    def place_of(which):
        def index(j):
            first, found = 0, []
            for _, _, _, w, row, count in spans:
                if w == which:
                    found.append((first, first + count, row))
                first += count
            first, end, row = found[-1]
            at_row, at_column = row, jnp.clip(j - first, 0, end - first - 1)
            for first, end, row in found[-2::-1]:
                at_row = jnp.where(j < end, row, at_row)
                at_column = jnp.where(j < end, jnp.clip(j - first, 0, end - first - 1), at_column)
            return at_row, at_column

        return index

    strips = [
        pl.BlockSpec((block, chunk), place_of(i)) for i, (_, _, block) in enumerate(rights) for _ in range(2)
    ]
    return pl.pallas_call(
        functools.partial(
            product_kernel,
            spans=spans,
            n_left=len(lefts),
            n_right=len(rights),
            rows=rows,
            chunk=chunk,
            extra=len(after),
            sides=sides,
        ),
        grid=(steps,),
        out_shape=(part,) * (2 * count),
        in_specs=[smem] + taken + strips + [anywhere] * len(after),
        out_specs=blocks,
        scratch_shapes=[pltpu.VMEM((count, height, tokens), jnp.bfloat16)] + wide,
        compiler_params=kernel_params(48),
        cost_estimate=cost(2.5 * height * tokens * columns / len(lefts), 20),
    )(ids, *[x[0] for x in lefts], *[x for right in rights for x in right[:2]], *after)


def exchange(values, bit):
    count = lax.axis_size(AXES)
    return lax.ppermute(values, AXES, [(i, i ^ (1 << bit)) for i in range(count)])


def place_kernel(*refs, slots, rows):
    me = lax.axis_index(AXES)
    pieces, out, sems = refs[: len(slots)], refs[-2], refs[-1]
    copies = []
    for piece, (start, order) in zip(pieces, slots):
        columns = pl.ds(start, piece.shape[-1])
        for i, slot in enumerate(order):
            place = pl.ds(pl.multiple_of((me ^ slot) * rows, rows), rows)
            copies.append(
                pltpu.make_async_copy(piece.at[i], out.at[place, columns], sems.at[len(copies)])
            )
    for copy in copies:
        copy.start()
    for copy in copies:
        copy.wait()


def join_kernel(*refs, count, split):
    parts, outs = refs[: 2 * count], refs[-(2 if split else count) :]
    for i in range(count):
        first = 0
        for part in parts[2 * i : 2 * i + 2]:
            rows = slice(first, first + part.shape[0])
            if split:
                outs[0][rows] = part[:, :, :split]
                outs[1][rows] = part[:, :, split:]
            else:
                outs[i][rows] = part[...]
            first += part.shape[0]


def pack_kernel(w_in, w_out, *refs):
    out = refs[-1]
    rows, width = w_in.shape[0], out.shape[1]
    count = w_in.shape[1] // width
    for i in range(count):
        out[i * rows : (i + 1) * rows, :] = w_in[:, i * width : (i + 1) * width]
    out[count * rows :, :] = w_out[...]


def pack_ffn(w_in, w_out, after):
    return pl.pallas_call(
        pack_kernel,
        out_shape=jax.ShapeDtypeStruct((2 * w_out.shape[0], w_out.shape[1]), jnp.bfloat16),
        in_specs=[vmem] * 2 + [anywhere] * len(after),
        out_specs=vmem,
        compiler_params=kernel_params(16),
        cost_estimate=cost(0, 1),
    )(w_in, w_out, *after)


class Gather:
    def __init__(self, local):
        self.rows, self.width = local.shape
        bits = lax.axis_size(AXES).bit_length() - 1
        self.half = self.width // 256 * 128
        high = [(b,) for b in range(bits - 1, 2, -1)]
        self.bits = high + [(2, 1), (1, 2), (0, 0)]
        self.count = len(high)
        self.values, self.order, self.stage = [local[None]], [[0]], 0
        self.send()

    def send(self):
        self.arrived = [exchange(v, b) for v, b in zip(self.values, self.bits[self.stage])]

    def step(self, after=()):
        self.order = [
            order + [i ^ (1 << b) for i in order] for order, b in zip(self.order, self.bits[self.stage])
        ]
        self.stage += 1
        split = self.half if self.stage == self.count else 0
        slots, columns = 2 * self.values[0].shape[0], [v.shape[-1] for v in self.values]
        if split:
            self.order = self.order * 2
            columns = [split, self.width - split]
        parts = [x for pair in zip(self.values, self.arrived) for x in pair]
        self.values = pl.pallas_call(
            functools.partial(join_kernel, count=len(self.values), split=split),
            out_shape=[jax.ShapeDtypeStruct((slots, self.rows, n), jnp.bfloat16) for n in columns],
            in_specs=[vmem] * len(parts) + [anywhere] * len(after),
            out_specs=[vmem] * len(columns),
            compiler_params=kernel_params(32),
            cost_estimate=cost(0, 4 * slots * self.rows * self.width / 2**20),
        )(*parts, *after)
        self.send()
        return self.values[:1]

    def place(self, after=()):
        pieces = [x for pair in zip(self.values, self.arrived) for x in pair]
        slots = []
        for start, order in zip((0, self.half), self.order):
            slots += [(start, order), (start, [i ^ 1 for i in order])]
        count = lax.axis_size(AXES)
        return pl.pallas_call(
            functools.partial(place_kernel, slots=slots, rows=self.rows),
            out_shape=jax.ShapeDtypeStruct((count * self.rows, self.width), jnp.bfloat16),
            in_specs=[anywhere] * (len(pieces) + len(after)),
            out_specs=anywhere,
            scratch_shapes=[pltpu.SemaphoreType.DMA((2 * count,))],
            compiler_params=kernel_params(16),
            cost_estimate=cost(0, 4 * count * self.rows * self.width / 2**20),
        )(*pieces, *after)


def stage_kernel(ids, *refs, groups, extra):
    inputs = refs[: 2 * sum(count for _, count in groups)]
    outputs = refs[len(inputs) + extra :]
    for g, (bit, count) in enumerate(groups):
        send, keep = outputs[2 * g : 2 * g + 2]
        mine, rows = ids[bit], send.shape[1]
        start = 0
        for _ in range(count):
            left, right, *inputs = inputs
            for j in range(left.shape[2] // rows):
                columns, block = slice(start, start + left.shape[-1]), slice(j * rows, (j + 1) * rows)
                for i in range(left.shape[0]):
                    for out, b in ((send, 1 - mine), (keep, mine)):
                        total = left[i, b, block].astype(jnp.float32) + right[i, b, block].astype(jnp.float32)
                        out[i, :, columns] = total.astype(jnp.bfloat16)
                start += left.shape[-1]


class Chain:
    def __init__(self, ids, parts, rows, sides=(0, 1)):
        self.ids, self.rows = ids, rows
        self.rest = list(range(3, ids.shape[0]))
        self.sends = parts[1::2]
        self.next = [(1, 2)[side] for side in sides]
        self.groups = [
            [(keep, exchange(send, (2, 1)[side]), rows)]
            for keep, send, side in zip(parts[::2], parts[1::2], sides)
        ]

    def arrived(self):
        return [part[1] for group in self.groups for part in group]

    def advance(self, groups, bits, after):
        shaped, shapes = [], []
        for group in groups:
            columns = 0
            for keep, arrived, rows in group:
                shaped += [x.reshape(-1, 2, rows, x.shape[-1]) for x in (keep, arrived)]
                columns += keep.shape[-1] * rows // self.rows
            shapes += [jax.ShapeDtypeStruct((shaped[-1].shape[0], self.rows, columns), jnp.bfloat16)] * 2
        outs = pl.pallas_call(
            functools.partial(
                stage_kernel, groups=[(b, len(g)) for b, g in zip(bits, groups)], extra=len(after)
            ),
            out_shape=shapes,
            in_specs=[smem] + [vmem] * len(shaped) + [anywhere] * len(after),
            out_specs=[vmem] * len(shapes),
            compiler_params=kernel_params(32),
            cost_estimate=cost(0, sum(3 * x.size for x in shaped) / 2**20),
        )(self.ids, *shaped, *after)
        self.groups = [
            [(keep, exchange(send, b), self.rows)] for send, keep, b in zip(outs[::2], outs[1::2], bits)
        ]
        return outs[1::2]

    def join(self, other):
        self.rows = other.rows
        self.groups = [[part for chain in (self, other) for group in chain.groups for part in group]]

    def second(self, after=()):
        return self.advance(self.groups, self.next, after)

    def third(self, after=()):
        self.groups = [[part for group in self.groups for part in group]]
        return self.advance(self.groups, [self.rest.pop(0)], after)

    def finish(self):
        [[(keep, arrived, _)]] = self.groups
        return (keep.astype(jnp.float32) + arrived.astype(jnp.float32))[0]


def small_kernel(*refs, rows, count, owned):
    sums, bias, out = refs[:count], refs[count], refs[-1]
    lines = [sums[i][row : row + 1] for i, row in rows]
    lines += [jnp.zeros_like(lines[0])] * (128 - len(lines))
    out[:, :128] = jnp.concatenate(lines, axis=0).T
    out[:, 128:] = jnp.zeros((out.shape[0], 128), jnp.float32)
    for i in range(bias.shape[0]):
        out[i * owned : i * owned + 1, 128:] = bias[i : i + 1]


def small_block(lines, sums, bias, owned, after):
    width = sums[0].shape[1]
    devices = width // owned
    bias = bias.reshape(devices, -1)
    bias = jnp.pad(bias, ((0, 0), (0, 128 - bias.shape[1])))
    places = [([i for i, x in enumerate(sums) if x is s][0], row) for s, row in lines]
    block = pl.pallas_call(
        functools.partial(small_kernel, rows=places, count=len(sums), owned=owned),
        out_shape=jax.ShapeDtypeStruct((width, 256), jnp.float32),
        in_specs=[vmem] * (len(sums) + 1) + [anywhere] * len(after),
        out_specs=vmem,
        compiler_params=kernel_params(16),
        cost_estimate=cost(0, 2),
    )(*sums, bias, *after)
    return block.astype(jnp.bfloat16)


def add_product_kernel(*refs, count, base, extra):
    out = refs[-1]
    total = refs[2 * count][...] if base else jnp.zeros(out.shape, jnp.float32)
    for left, right in zip(refs[:count], refs[count : 2 * count]):
        total += dot(left[...], right[...], (1, 1))
    out[...] = total


def add_product(stack, places, weights, columns, rows, chunk, base=None, after=()):
    width = stack.shape[1]
    count = len(places)
    bases = [] if base is None else [base]
    block = pl.BlockSpec((chunk, width), lambda i: (i, 0))
    return pl.pallas_call(
        functools.partial(add_product_kernel, count=count, base=len(bases), extra=len(after)),
        grid=(rows // chunk,),
        out_shape=jax.ShapeDtypeStruct((rows, width), jnp.float32),
        in_specs=[pl.BlockSpec((chunk, width), lambda i, p=p: (p // chunk + i, 0)) for p in places]
        + [pl.BlockSpec((width, width), lambda i, c=c: (0, c)) for c in columns]
        + [block] * len(bases)
        + [anywhere] * len(after),
        out_specs=block,
        compiler_params=kernel_params(40),
        cost_estimate=cost(0, 0.001),
    )(*[stack] * count, *[weights] * count, *bases, *after)


def body(
    target_in,
    memory,
    block_rows,
    pad_rows,
    seq_lengths,
    self_qkv,
    self_out,
    cross_query,
    cross_kv,
    cross_out,
    ffn_in,
    ffn_out,
    norm_scale,
    small_bias,
    ffn_bias,
    cotangent,
):
    width = target_in.shape[1]
    owned = self_qkv.shape[0]
    me = lax.axis_index(AXES)
    core = (me & 1).reshape(1)
    ids = (me >> jnp.arange(lax.axis_size(AXES).bit_length() - 1)) & 1
    tokens, mems = target_in.shape[0], memory.shape[0]

    def turned(*arrays, after=()):
        keep, send = turn(core, arrays, owned, after)
        return keep, exchange(send, 0)

    pack = jnp.concatenate([norm_scale.T, small_bias.T, ffn_bias.reshape(owned, -1)], axis=1)
    small_cols = pack.shape[1]
    pack = jnp.pad(pack, ((0, 0), (0, -small_cols % 128)))
    early = Gather(jnp.concatenate([self_qkv, self_out, cross_query, pack], axis=1))
    late = Gather(jnp.concatenate([cross_kv, cross_out], axis=1))
    memory_turned = turned(memory)
    target_turned = turned(target_in, after=memory_turned[:1])
    last = target_turned[:1]
    for _ in range(early.count + 2):
        last = early.step(last)
        if early.stage == early.count:
            packed = lax.all_gather(pack_ffn(ffn_in, ffn_out, last), AXES)
        if early.stage < early.count + 2:
            last = late.step(last)
    early = early.place(last)

    w_qkv, w_self, w_query = early[:, : 3 * width], early[:, 3 * width : 4 * width], early[:, 4 * width : 5 * width]
    small = early[:, 5 * width : 5 * width + small_cols].astype(jnp.float32)
    gains = small[:, :3].T
    biases = small[:, 3:13].T
    in_bias = small[:, 13:].reshape(1, -1)

    bound = memory_bounds(block_rows[0], pad_rows[0])
    lengths = seq_lengths[0]
    zeros = jnp.zeros((width,), jnp.float32)
    qkv = (matmul(target_in, w_qkv) + jnp.concatenate([biases[0], zeros, biases[1]])).astype(
        jnp.bfloat16
    )
    self_context, self_summary = self_forward(lengths, qkv)
    first, first_unit, first_inverse = normalize(
        target_in.astype(jnp.float32) + matmul(self_context, w_self) + biases[2],
        gains[0],
        biases[7],
    )
    first_low = first.astype(jnp.bfloat16)
    self_turned = turned(self_context, first_low)
    cross_q = (matmul(first_low, w_query) + biases[3]).astype(jnp.bfloat16)
    late.step((cross_q, self_turned[0]))
    late = late.place()
    w_pairs, w_cross = late[:, : 2 * width], late[:, 2 * width :]
    cross_pairs = (matmul(memory, w_pairs) + jnp.concatenate([zeros, biases[4]])).astype(
        jnp.bfloat16
    )
    cross_context, cross_summary = cross_forward(bound, cross_q, cross_pairs)
    second, second_unit, second_inverse = normalize(
        first + matmul(cross_context, w_cross) + biases[5], gains[1], biases[8]
    )

    cross_turned = turned(cross_context, second)
    vectors = jnp.concatenate([biases[6:7], gains[2:3], biases[9:10], jnp.zeros((5, width), jnp.float32)])
    hidden, hidden_send, slope, block_out, third_grad, out_grad, third_sums = ffn_forward(
        core,
        second,
        packed,
        in_bias,
        cotangent,
        vectors,
        ffn_out.shape[0],
        after=(memory_turned[1], target_turned[1], self_turned[1]),
    )
    hidden_other, out_grad_other = exchange(hidden_send, 0), exchange(out_grad, 0)
    pre_grad, ffn_bias_grad, second_grad, cross_branch, second_sums = ffn_backward(
        packed, slope, third_grad, out_grad, second_unit, second_inverse, gains[1:2], (cross_turned[1], out_grad_other)
    )
    pre_grad_other = exchange(pre_grad, 0)
    parts = products(
        ids,
        [(hidden, tokens, 0), (hidden_other, tokens, 0)],
        [(out_grad, out_grad_other, tokens)],
        [(0, tokens, tokens, 0, 0, width)],
        ffn_out.shape[0],
        512,
        sides=(0,),
        after=(pre_grad,),
    )
    out_chain = Chain(ids, parts, ffn_out.shape[0], sides=(0,))
    parts = products(
        ids,
        [(x, tokens, 1) for x in cross_turned],
        [(pre_grad, pre_grad_other, tokens)],
        [(0, tokens, tokens, 0, 0, ffn_in.shape[1])],
        owned,
        1024,
        sides=(1,),
        after=out_chain.sends,
    )
    in_chain = Chain(ids, parts, owned, sides=(1,))

    cross_delta, cross_sums = cross_backward(
        bound, cross_q, cross_pairs, cross_summary, cross_branch, late, 2, after=in_chain.sends
    )
    cross_other = exchange(cross_delta, 0)
    self_delta, self_sums, first_grad = self_backward(
        lengths,
        qkv,
        self_summary,
        second_grad,
        cross_delta,
        early,
        first_unit,
        first_inverse,
        gains[0:1],
    )
    self_other = exchange(self_delta, 0)
    small_grad = small_block(
        [
            (self_sums, 3),
            (second_sums, 0),
            (third_sums, 0),
            (self_sums, 0),
            (self_sums, 1),
            (self_sums, 2),
            (cross_sums, 0),
            (cross_sums, 1),
            (second_sums, 2),
            (third_sums, 2),
            (self_sums, 4),
            (second_sums, 1),
            (third_sums, 1),
        ],
        [self_sums, cross_sums, second_sums, third_sums],
        ffn_bias_grad,
        owned,
        (self_sums,),
    )
    bits = list(range(lax.axis_size(AXES).bit_length() - 1))[::-1]
    small_part = small_grad.reshape((2,) * len(bits) + (owned, -1))
    for bit in (0, 1):
        mine = (me >> bit) & 1
        small_keep, small_send = [
            lax.dynamic_index_in_dim(small_part, i, bits.index(bit), keepdims=False)
            for i in (mine, 1 - mine)
        ]
        small_other = exchange(small_send, bit)
        small_part = (small_keep.astype(jnp.float32) + small_other.astype(jnp.float32)).astype(jnp.bfloat16)
        bits.remove(bit)
    beyond = mems + 2 * tokens
    parts = products(
        ids,
        [
            part
            for i in range(2)
            for part in (
                (memory_turned[i], mems, 0),
                (self_turned[i], tokens, 1),
                (cross_turned[i], tokens, 0),
            )
        ],
        [(cross_delta, cross_other, mems), (cross_delta, cross_other, mems // 2)],
        [
            (mems, beyond + mems, tokens, 1, 4, width),
            (0, beyond, mems, 0, 0, width),
            (0, beyond, mems, 0, 1, width),
            (mems + tokens, beyond + mems + tokens, tokens, 1, 5, width),
        ],
        owned,
        1024,
        after=in_chain.second(after=out_chain.second(after=(small_grad,))),
    )
    cross_chain = Chain(ids, parts, owned)
    parts = products(
        ids,
        [part for i in range(2) for part in ((target_turned[i], tokens, 0), (self_turned[i], tokens, 0))],
        [(self_delta, self_other, tokens)],
        [(0, 2 * tokens, tokens, 0, i, width) for i in range(3)]
        + [(tokens, 3 * tokens, tokens, 0, 3, width)],
        owned,
        1024,
        after=(parts[0], small_other),
    )
    self_chain = Chain(ids, parts, owned)
    self_chain.groups[1].append((small_keep, small_other, owned))
    out_chain.join(in_chain)
    last = out_chain.third(after=parts[:1])
    last = cross_chain.second(after=last)
    memory_grad = add_product(cross_delta, [0, mems], late, [0, 1], mems, 512, after=last)
    last = (memory_grad,)
    while out_chain.rest:
        last = out_chain.third(after=last)
    last = self_chain.second(after=last)
    target_grad = add_product(
        self_delta,
        [0, tokens, 2 * tokens],
        early,
        [0, 1, 2],
        tokens,
        tokens,
        first_grad,
        after=last,
    )
    last = (target_grad,)
    last = cross_chain.third(after=last)
    last = self_chain.third(after=last)
    while self_chain.rest:
        last = cross_chain.third(after=last)
        last = self_chain.third(after=last)
    ffn_shard = out_chain.finish()
    size = ffn_in.shape[1]
    ffn_out_shard = ffn_shard[:, :size].reshape(owned, -1, width).swapaxes(0, 1).reshape(ffn_out.shape)
    ffn_in_shard = ffn_shard[:, size:]
    cross_shard = cross_chain.finish()
    self_shard = self_chain.finish()
    small_shard = self_shard[:, 4 * width :]
    return (
        block_out,
        target_grad,
        memory_grad,
        self_shard[:, : 3 * width],
        self_shard[:, 3 * width : 4 * width],
        cross_shard[:, :width],
        cross_shard[:, width : 3 * width],
        cross_shard[:, 3 * width :],
        ffn_in_shard,
        ffn_out_shard,
        small_shard[:, :3].T,
        small_shard[:, 3:13].T,
        small_shard[0, 128 : 128 + ffn_bias.shape[0]],
    )


def solution(mesh):
    in_specs = (
        P(("wide", "narrow"), None),
        P(("wide", "narrow"), None),
        P(("wide", "narrow"), None),
        P(("wide", "narrow"), None),
        P(("wide", "narrow"), None),
        P(("wide", "narrow"), None),
        P(("wide", "narrow"), None),
        P(("wide", "narrow"), None),
        P(("wide", "narrow"), None),
        P(("wide", "narrow"), None),
        P(("wide", "narrow"), None),
        P(("wide", "narrow"), None),
        P(None, ("wide", "narrow")),
        P(None, ("wide", "narrow")),
        P(("wide", "narrow")),
        P(("wide", "narrow"), None),
    )
    out_specs = (
        P(("wide", "narrow"), None),
        P(("wide", "narrow"), None),
        P(("wide", "narrow"), None),
        P(("wide", "narrow"), None),
        P(("wide", "narrow"), None),
        P(("wide", "narrow"), None),
        P(("wide", "narrow"), None),
        P(("wide", "narrow"), None),
        P(("wide", "narrow"), None),
        P(("wide", "narrow"), None),
        P(None, ("wide", "narrow")),
        P(None, ("wide", "narrow")),
        P(("wide", "narrow")),
    )
    return jax.shard_map(body, mesh=mesh, in_specs=in_specs, out_specs=out_specs, check_vma=False)
```

```python
import functools

import jax
import jax.numpy as jnp
from jax import lax
from jax.experimental import pallas as pl
from jax.experimental.pallas import tpu as pltpu
from jax.sharding import PartitionSpec as P

HEADS = 16
HEAD_DIM = 64
SEQ_LEN = 128
PAIRS = HEADS // 2
neg_fill = -1e30
AXES = ("wide", "narrow")
vmem = pl.BlockSpec(memory_space=pltpu.VMEM)
smem = pl.BlockSpec(memory_space=pltpu.SMEM)
anywhere = pl.BlockSpec(memory_space=pl.ANY)
norm_eps = 1e-05


def kernel_params(megabytes):
    return pltpu.CompilerParams(vmem_limit_bytes=megabytes << 20)


def cost(flops, megabytes, transcendentals=0):
    return pl.CostEstimate(
        flops=int(10 * flops), bytes_accessed=int(10 * megabytes * 2**20), transcendentals=int(10 * transcendentals)
    )


def matmul(first, second):
    return jnp.dot(first, second, preferred_element_type=jnp.float32)


def inner_cols(first, second):
    return lax.dot_general(
        first, second, (((1,), (1,)), ((), ())), preferred_element_type=jnp.float32
    )


def column_sums(values):
    return jnp.sum(values.astype(jnp.float32), axis=0)


def memory_bounds(block_rows, pad_rows):
    count = block_rows.shape[0]
    before = jnp.arange(count)[None, :] < jnp.arange(count)[:, None]
    starts = jnp.sum(jnp.where(before, block_rows[None, :], 0), axis=1)
    valid = jnp.maximum(block_rows - pad_rows, (block_rows + 1) // 2)
    return jnp.stack([starts, starts + valid])


def dot(first, second, contract):
    return lax.dot_general(
        first, second, ((contract[:1], contract[1:]), ((), ())), preferred_element_type=jnp.float32
    )


def cols(pair, base=0):
    return slice((base + pair) * 128, (base + pair + 1) * 128)


def split_heads(block):
    low = lax.broadcasted_iota(jnp.int32, block.shape, 1) < HEAD_DIM
    zero = jnp.zeros_like(block)
    return jnp.concatenate([jnp.where(low, block, zero), jnp.where(low, zero, block)], axis=0)


def join_heads(stacked):
    low = lax.broadcasted_iota(jnp.int32, (SEQ_LEN, 128), 1) < HEAD_DIM
    return jnp.where(low, stacked[:SEQ_LEN], stacked[SEQ_LEN:])


def join_heads_t(stacked):
    both = jnp.concatenate([stacked[:HEAD_DIM, :SEQ_LEN], stacked[HEAD_DIM:, SEQ_LEN:]], axis=0)
    return both.T


def cross_mask(tile, low, high):
    rows = tile * 128 + lax.broadcasted_iota(jnp.int32, (128, 2 * SEQ_LEN), 0)
    return (rows >= low) & (rows < high)


def cross_forward_kernel(bound, q, pairs, *rest, extra):
    context, summary, stack, scores, top, total, acc = rest[extra:]

    def sequence(s, carry):
        low, high = bound[0, s], bound[1, s]
        first, last = low // 128, (high + 127) // 128
        rows = pl.ds(pl.multiple_of(s * SEQ_LEN, SEQ_LEN), SEQ_LEN)
        for p in range(PAIRS):
            stack[p] = split_heads(q[rows, cols(p)] * jnp.bfloat16(HEAD_DIM**-0.5))
        top[...] = jnp.full_like(top, neg_fill)
        total[...] = jnp.zeros_like(total)
        acc[...] = jnp.zeros_like(acc)

        def one(t, carry):
            keys = pl.ds(pl.multiple_of(t * 128, 128), 128)
            ok = cross_mask(t, low, high)
            for p in range(PAIRS):
                raw = jnp.where(ok, dot(pairs[keys, cols(p)], stack[p], (1, 1)), neg_fill)
                scores[t, p] = raw
                top[p] = jnp.maximum(top[p], jnp.max(raw, axis=0, keepdims=True))
            return carry

        lax.fori_loop(first, last, one, 0)

        def two(t, carry):
            keys = pl.ds(pl.multiple_of(t * 128, 128), 128)
            for p in range(PAIRS):
                weights = jnp.exp(scores[t, p] - top[p])
                total[p] += jnp.sum(weights, axis=0, keepdims=True)
                acc[p] += dot(pairs[keys, cols(p, PAIRS)], weights.astype(jnp.bfloat16), (0, 0))
            return carry

        lax.fori_loop(first, last, two, 0)
        for p in range(PAIRS):
            context[rows, cols(p)] = join_heads_t(acc[p] / total[p]).astype(jnp.bfloat16)
            summary[s, p] = top[p] + jnp.log(total[p])
        return carry

    lax.fori_loop(0, bound.shape[1], sequence, 0)


def cross_backward_kernel(bound, q, pairs, summary, branch, weight, *rest, extra):
    out, sums, grad, stack, grads, probs, prob_grads, delta, acc, pair_acc = rest[extra:]
    pair_acc[...] = jnp.zeros_like(pair_acc)
    scale = HEAD_DIM**-0.5
    (tokens, width), mems = q.shape, pairs.shape[0]
    grad[...] = dot(branch[...], weight[...], (1, 1)).astype(jnp.bfloat16)
    pad = (out.shape[0] - 2 * mems) // 2
    query_at, branch_at = 2 * mems, 2 * mems + pad

    def sequence(s, carry):
        low, high = bound[0, s], bound[1, s]
        first, last = low // 128, (high + 127) // 128
        rows = pl.ds(pl.multiple_of(s * SEQ_LEN, SEQ_LEN), SEQ_LEN)
        for p in range(PAIRS):
            stack[p] = split_heads(q[rows, cols(p)] * jnp.bfloat16(scale))
            grads[p] = split_heads(grad[rows, cols(p)])
        delta[...] = jnp.zeros_like(delta)
        acc[...] = jnp.zeros_like(acc)

        def one(t, carry):
            keys = pl.ds(pl.multiple_of(t * 128, 128), 128)
            ok = cross_mask(t, low, high)
            for p in range(PAIRS):
                raw = dot(pairs[keys, cols(p)], stack[p], (1, 1))
                weights = jnp.where(ok, jnp.exp(raw - summary[s, p]), 0.0)
                back = dot(pairs[keys, cols(p, PAIRS)], grads[p], (1, 1))
                delta[p] += jnp.sum(weights * back, axis=0, keepdims=True)
                probs[t, p] = weights
                prob_grads[t, p] = back
                pair_acc[keys, cols(p, PAIRS)] += dot(weights.astype(jnp.bfloat16), grads[p], (1, 0))
            return carry

        lax.fori_loop(first, last, one, 0)

        def two(t, carry):
            keys = pl.ds(pl.multiple_of(t * 128, 128), 128)
            for p in range(PAIRS):
                score = (probs[t, p] * (prob_grads[t, p] - delta[p])).astype(jnp.bfloat16)
                pair_acc[keys, cols(p)] += dot(score, stack[p], (1, 0))
                acc[p] += dot(pairs[keys, cols(p)], score, (0, 0))
            return carry

        lax.fori_loop(first, last, two, 0)
        for p in range(PAIRS):
            place = pl.ds(pl.multiple_of(query_at + s * SEQ_LEN, SEQ_LEN), SEQ_LEN)
            out[place, cols(p)] = (join_heads_t(acc[p]) * scale).astype(jnp.bfloat16)
        return carry

    lax.fori_loop(0, bound.shape[1], sequence, 0)
    out[:mems, :] = pair_acc[:, :width].astype(jnp.bfloat16)
    out[mems:query_at, :] = pair_acc[:, width:].astype(jnp.bfloat16)
    out[branch_at : branch_at + tokens, :] = branch[...]
    for at in (query_at, branch_at):
        out[at + tokens : at + pad, :] = jnp.zeros((pad - tokens, width), jnp.bfloat16)
    sums[...] = sum_rows(
        out[query_at : query_at + tokens, :].astype(jnp.float32), out[mems:query_at, :].astype(jnp.float32)
    )


def cross_forward(bound, q, pairs, after=()):
    seqs, tiles = bound.shape[1], pairs.shape[0] // 128
    wide = 2 * SEQ_LEN
    return pl.pallas_call(
        functools.partial(cross_forward_kernel, extra=len(after)),
        out_shape=(
            jax.ShapeDtypeStruct(q.shape, jnp.bfloat16),
            jax.ShapeDtypeStruct((seqs, PAIRS, 1, wide), jnp.float32),
        ),
        in_specs=[smem, vmem, vmem] + [anywhere] * len(after),
        out_specs=(vmem, vmem),
        scratch_shapes=[
            pltpu.VMEM((PAIRS, wide, 128), jnp.bfloat16),
            pltpu.VMEM((tiles, PAIRS, 128, wide), jnp.float32),
            pltpu.VMEM((PAIRS, 1, wide), jnp.float32),
            pltpu.VMEM((PAIRS, 1, wide), jnp.float32),
            pltpu.VMEM((PAIRS, 128, wide), jnp.float32),
        ],
        compiler_params=kernel_params(40),
        cost_estimate=cost(8e9, 8),
    )(bound, q, pairs, *after)


def cross_backward(bound, q, pairs, summary, branch, weights, column, after=()):
    seqs, tiles = bound.shape[1], pairs.shape[0] // 128
    wide = 2 * SEQ_LEN
    width = q.shape[1]
    whole = lambda shape: pl.BlockSpec(shape, lambda i: (0,) * len(shape))
    rows = 3 * pairs.shape[0]
    return pl.pallas_call(
        functools.partial(cross_backward_kernel, extra=len(after)),
        grid=(1,),
        out_shape=(
            jax.ShapeDtypeStruct((rows, width), jnp.bfloat16),
            jax.ShapeDtypeStruct((8, width), jnp.float32),
        ),
        in_specs=[smem]
        + [whole(x.shape) for x in (q, pairs, summary, branch)]
        + [pl.BlockSpec((width, width), lambda i: (0, column))]
        + [anywhere] * len(after),
        out_specs=(whole((rows, width)), whole((8, width))),
        scratch_shapes=[
            pltpu.VMEM(q.shape, jnp.bfloat16),
            pltpu.VMEM((PAIRS, wide, 128), jnp.bfloat16),
            pltpu.VMEM((PAIRS, wide, 128), jnp.bfloat16),
            pltpu.VMEM((tiles, PAIRS, 128, wide), jnp.float32),
            pltpu.VMEM((tiles, PAIRS, 128, wide), jnp.float32),
            pltpu.VMEM((PAIRS, 1, wide), jnp.float32),
            pltpu.VMEM((PAIRS, 128, wide), jnp.float32),
            pltpu.VMEM(pairs.shape, jnp.float32),
        ],
        compiler_params=kernel_params(58),
        cost_estimate=cost(16e9, 12),
    )(bound, q, pairs, summary, branch, weights, *after)


def self_mask(length):
    keys = lax.broadcasted_iota(jnp.int32, (SEQ_LEN, 2 * SEQ_LEN), 0)
    tokens = lax.broadcasted_iota(jnp.int32, (SEQ_LEN, 2 * SEQ_LEN), 1) & (SEQ_LEN - 1)
    return (keys <= tokens) & (keys < length)


def self_forward_kernel(lengths, qkv, *rest, extra):
    context, summary = rest[extra:]

    def sequence(s, carry):
        ok = self_mask(lengths[s])
        rows = pl.ds(pl.multiple_of(s * SEQ_LEN, SEQ_LEN), SEQ_LEN)
        for p in range(PAIRS):
            stack = split_heads(qkv[rows, cols(p)] * jnp.bfloat16(HEAD_DIM**-0.5))
            raw = jnp.where(ok, dot(qkv[rows, cols(p, PAIRS)], stack, (1, 1)), neg_fill)
            top = jnp.max(raw, axis=0, keepdims=True)
            weights = jnp.exp(raw - top)
            total = jnp.sum(weights, axis=0, keepdims=True)
            weights = (weights / total).astype(jnp.bfloat16)
            acc = dot(qkv[rows, cols(p, 2 * PAIRS)], weights, (0, 0))
            context[rows, cols(p)] = join_heads_t(acc).astype(jnp.bfloat16)
            summary[s, p] = top + jnp.log(total)
        return carry

    lax.fori_loop(0, lengths.shape[0], sequence, 0)


def self_backward_kernel(
    lengths, qkv, summary, second_grad, query_delta, w_query, w_self, unit, inverse, gain, *rest, extra
):
    out, sums, first_grad, grad = rest[extra:]
    scale = HEAD_DIM**-0.5
    tokens = qkv.shape[0]
    total = second_grad[...] + dot(query_delta[:tokens, :], w_query[...], (1, 1))
    first = normalize_back(total, unit[...], inverse[...], gain[...])
    first_grad[...] = first
    branch = first.astype(jnp.bfloat16)
    out[3 * tokens :, :] = branch
    grad[...] = dot(branch, w_self[...], (1, 1)).astype(jnp.bfloat16)

    def sequence(s, carry):
        ok = self_mask(lengths[s])
        rows = pl.ds(pl.multiple_of(s * SEQ_LEN, SEQ_LEN), SEQ_LEN)
        for p in range(PAIRS):
            stack = split_heads(qkv[rows, cols(p)] * jnp.bfloat16(scale))
            grads = split_heads(grad[rows, cols(p)])
            keys = qkv[rows, cols(p, PAIRS)]
            raw = dot(keys, stack, (1, 1))
            weights = jnp.where(ok, jnp.exp(raw - summary[s, p]), 0.0)
            back = dot(qkv[rows, cols(p, 2 * PAIRS)], grads, (1, 1))
            delta = jnp.sum(weights * back, axis=0, keepdims=True)
            score = (weights * (back - delta)).astype(jnp.bfloat16)
            value_grad = dot(weights.astype(jnp.bfloat16), grads, (1, 0))
            key_grad = dot(score, stack, (1, 0))
            query_grad = join_heads_t(dot(keys, score, (0, 0))) * scale
            for i, part in enumerate((query_grad, key_grad, value_grad)):
                place = pl.ds(pl.multiple_of(i * tokens + s * SEQ_LEN, SEQ_LEN), SEQ_LEN)
                out[place, cols(p)] = part.astype(jnp.bfloat16)
        return carry

    lax.fori_loop(0, lengths.shape[0], sequence, 0)
    sums[...] = sum_rows(
        *[out[i * tokens : (i + 1) * tokens, :].astype(jnp.float32) for i in (0, 2, 3)],
        total * unit[...],
        total,
    )


def self_forward(lengths, qkv, after=()):
    tokens, width = qkv.shape[0], qkv.shape[1] // 3
    return pl.pallas_call(
        functools.partial(self_forward_kernel, extra=len(after)),
        out_shape=(
            jax.ShapeDtypeStruct((tokens, width), jnp.bfloat16),
            jax.ShapeDtypeStruct((lengths.shape[0], PAIRS, 1, 2 * SEQ_LEN), jnp.float32),
        ),
        in_specs=[smem, vmem] + [anywhere] * len(after),
        out_specs=(vmem, vmem),
        compiler_params=kernel_params(24),
        cost_estimate=cost(2e9, 4),
    )(lengths, qkv, *after)


def self_backward(
    lengths, qkv, summary, second_grad, cross_delta, weights, unit, inverse, gain, after=()
):
    tokens, width = second_grad.shape
    whole = lambda shape: pl.BlockSpec(shape, lambda i: (0,) * len(shape))
    full = whole((tokens, width))
    return pl.pallas_call(
        functools.partial(self_backward_kernel, extra=len(after)),
        grid=(1,),
        out_shape=(
            jax.ShapeDtypeStruct((4 * tokens, width), jnp.bfloat16),
            jax.ShapeDtypeStruct((8, width), jnp.float32),
            jax.ShapeDtypeStruct((tokens, width), jnp.float32),
        ),
        in_specs=[
            smem,
            whole(qkv.shape),
            whole(summary.shape),
            full,
            pl.BlockSpec((cross_delta.shape[0] // 6, width), lambda i: (4, 0)),
            pl.BlockSpec((width, width), lambda i: (0, 4)),
            pl.BlockSpec((width, width), lambda i: (0, 3)),
            full,
            whole((tokens, 1)),
            whole((1, width)),
        ]
        + [anywhere] * len(after),
        out_specs=(whole((4 * tokens, width)), whole((8, width)), full),
        scratch_shapes=[pltpu.VMEM((tokens, width), jnp.bfloat16)],
        compiler_params=kernel_params(48),
        cost_estimate=cost(6e9, 12),
    )(lengths, qkv, summary, second_grad, cross_delta, weights, weights, unit, inverse, gain, *after)


def normalize(values, gain, shift):
    centered = values - jnp.mean(values, axis=-1, keepdims=True)
    inverse = lax.rsqrt(jnp.mean(centered * centered, axis=-1, keepdims=True) + norm_eps)
    unit = centered * inverse
    return (unit * gain + shift, unit, inverse)


def normalize_back(grad, unit, inverse, gain):
    scaled = grad * gain
    inner = (
        scaled
        - jnp.mean(scaled, axis=-1, keepdims=True)
        - unit * jnp.mean(scaled * unit, axis=-1, keepdims=True)
    )
    return inverse * inner


def sum_rows(*rows):
    stacked = [jnp.sum(r, axis=0, keepdims=True) for r in rows]
    return jnp.concatenate(stacked + [jnp.zeros_like(stacked[0])] * (8 - len(rows)), axis=0)


def deal(core, turned, rows, keep, send):
    for i in range(turned.shape[0] // (2 * rows)):
        even = turned[2 * i * rows : (2 * i + 1) * rows]
        odd = turned[(2 * i + 1) * rows : (2 * i + 2) * rows]
        here = slice(i * rows, (i + 1) * rows)
        keep(here, jnp.where(core == 0, even, odd).astype(jnp.bfloat16))
        send(here, jnp.where(core == 0, odd, even).astype(jnp.bfloat16))


def into(ref, columns):
    def store(rows, values):
        ref[rows, columns] = values

    return store


def turn_kernel(core, *refs, rows, count):
    arrays, (keep, send) = refs[:count], refs[-2:]
    start = 0
    for array in arrays:
        tokens = array.shape[0]
        columns = slice(start, start + tokens)
        turned = array[...].astype(jnp.float32 if rows % 16 else jnp.bfloat16).T
        deal(core[0], turned, rows, into(keep, columns), into(send, columns))
        start += tokens


def turn(core, arrays, rows, after=()):
    width = arrays[0].shape[1]
    half = jax.ShapeDtypeStruct((width // 2, sum(x.shape[0] for x in arrays)), jnp.bfloat16)
    return pl.pallas_call(
        functools.partial(turn_kernel, rows=rows, count=len(arrays)),
        out_shape=(half, half),
        in_specs=[smem] + [vmem] * len(arrays) + [anywhere] * len(after),
        out_specs=(vmem, vmem),
        compiler_params=kernel_params(32),
        cost_estimate=cost(0, 8),
    )(core, *arrays, *after)


def flat(block):
    values = block[...]
    if values.shape[1] % 16:
        values = values.astype(jnp.float32)
    return values.reshape(-1, values.shape[-1]).astype(jnp.bfloat16)


def weight_blocks(packed, chunk):
    devices, rows, width = packed.shape
    hidden = devices * rows // 2
    strips, owned = width // chunk, rows * width // (2 * hidden)
    return [
        pl.BlockSpec((devices, owned, chunk), lambda j: (0, j // strips, j % strips)),
        pl.BlockSpec((devices * chunk // hidden, rows // 2, width), lambda j: (j, 1, 0)),
    ]


def ffn_forward_kernel(
    core, second, w_in, w_out, bias, cot, vectors, *rest, rows, extra
):
    keep, send, slope, block_out, third_grad, out_grad, sums, acc, low = rest[extra:]

    step = pl.program_id(0)

    @pl.when(step == 0)
    def _():
        low[...] = second[...].astype(jnp.bfloat16)
        acc[...] = second[...] + vectors[0:1]

    pre = dot(low[...], flat(w_in), (1, 0)) + bias[...]
    part = 0.5 + 0.5 * lax.erf(pre * 0.5**0.5)
    active = (pre * part).astype(jnp.bfloat16)
    everything = slice(None)
    deal(core[0], active.T, rows, into(keep, everything), into(send, everything))
    slope[...] = (part + pre * jnp.exp(-0.5 * pre * pre) * 0.3989422804014327).astype(jnp.bfloat16)
    acc[...] += dot(active, flat(w_out), (1, 0))

    @pl.when(step == pl.num_programs(0) - 1)
    def _():
        gain = vectors[1:2]
        third, unit, inverse = normalize(acc[...], gain, vectors[2:3])
        block_out[...] = third.astype(jnp.bfloat16)
        grad = cot[...].astype(jnp.float32)
        third = normalize_back(grad, unit, inverse, gain)
        third_grad[...] = third
        lower = third.astype(jnp.bfloat16)
        out_grad[...] = lower
        sums[...] = sum_rows(grad * unit, grad, lower.astype(jnp.float32))


def ffn_forward(core, second, packed, bias, cot, vectors, rows, after):
    tokens, width = second.shape
    hidden = packed.shape[0] * packed.shape[1] // 2
    chunk = 1024
    whole = lambda shape: pl.BlockSpec(shape, lambda j: (0, 0))
    full = whole((tokens, width))
    strip = pl.BlockSpec((tokens, chunk), lambda j: (0, j))
    turned = pl.BlockSpec((chunk // 2, tokens), lambda j: (j, 0))
    return pl.pallas_call(
        functools.partial(ffn_forward_kernel, rows=rows, extra=len(after)),
        grid=(hidden // chunk,),
        out_shape=(
            jax.ShapeDtypeStruct((hidden // 2, tokens), jnp.bfloat16),
            jax.ShapeDtypeStruct((hidden // 2, tokens), jnp.bfloat16),
            jax.ShapeDtypeStruct((tokens, hidden), jnp.bfloat16),
            jax.ShapeDtypeStruct((tokens, width), jnp.bfloat16),
            jax.ShapeDtypeStruct((tokens, width), jnp.float32),
            jax.ShapeDtypeStruct((tokens, width), jnp.bfloat16),
            jax.ShapeDtypeStruct((8, width), jnp.float32),
        ),
        in_specs=[
            smem,
            full,
            *weight_blocks(packed, chunk),
            pl.BlockSpec((1, chunk), lambda j: (0, j)),
            full,
            whole((8, width)),
        ]
        + [anywhere] * len(after),
        out_specs=(turned, turned, strip, full, full, full, whole((8, width))),
        scratch_shapes=[
            pltpu.VMEM((tokens, width), jnp.float32),
            pltpu.VMEM((tokens, width), jnp.bfloat16),
        ],
        compiler_params=kernel_params(40),
        cost_estimate=cost(16e9, 26, 4e6),
    )(core, second, packed, packed, bias, cot, vectors, *after)


def ffn_backward_kernel(
    w_in, w_out, slope, third_grad, out_grad, unit, inverse, gain, *rest, extra
):
    pre_grad, bias_grad, second_grad, branch, sums, acc = rest[extra:]
    step = pl.program_id(0)

    @pl.when(step == 0)
    def _():
        acc[...] = third_grad[...]

    grad = dot(out_grad[...], flat(w_out), (1, 1)) * slope[...].astype(jnp.float32)
    lower = grad.astype(jnp.bfloat16)
    pre_grad[...] = lower
    bias_grad[...] = jnp.sum(lower.astype(jnp.float32), axis=0, keepdims=True)
    acc[...] += dot(lower, flat(w_in), (1, 1))

    @pl.when(step == pl.num_programs(0) - 1)
    def _():
        total = acc[...]
        grad = normalize_back(total, unit[...], inverse[...], gain[...])
        second_grad[...] = grad
        lower = grad.astype(jnp.bfloat16)
        branch[...] = lower
        sums[...] = sum_rows(total * unit[...], total, lower.astype(jnp.float32))


def ffn_backward(packed, slope, third_grad, out_grad, unit, inverse, gain, after):
    tokens, width = third_grad.shape
    hidden = packed.shape[0] * packed.shape[1] // 2
    chunk = 1024
    whole = lambda shape: pl.BlockSpec(shape, lambda j: (0, 0))
    full = whole((tokens, width))
    strip = pl.BlockSpec((tokens, chunk), lambda j: (0, j))
    return pl.pallas_call(
        functools.partial(ffn_backward_kernel, extra=len(after)),
        grid=(hidden // chunk,),
        out_shape=(
            jax.ShapeDtypeStruct((tokens, hidden), jnp.bfloat16),
            jax.ShapeDtypeStruct((1, hidden), jnp.float32),
            jax.ShapeDtypeStruct((tokens, width), jnp.float32),
            jax.ShapeDtypeStruct((tokens, width), jnp.bfloat16),
            jax.ShapeDtypeStruct((8, width), jnp.float32),
        ),
        in_specs=[
            *weight_blocks(packed, chunk),
            strip,
            full,
            full,
            full,
            whole((tokens, 1)),
            whole((1, width)),
        ]
        + [anywhere] * len(after),
        out_specs=(strip, pl.BlockSpec((1, chunk), lambda j: (0, j)), full, full, whole((8, width))),
        scratch_shapes=[pltpu.VMEM((tokens, width), jnp.float32)],
        compiler_params=kernel_params(40),
        cost_estimate=cost(14e9, 26),
    )(packed, packed, slope, third_grad, out_grad, unit, inverse, gain, *after)


def product_kernel(ids, *refs, spans, n_left, n_right, rows, chunk, extra, sides):
    lefts, rights = refs[:n_left], refs[n_left : n_left + 2 * n_right]
    rest = refs[n_left + 2 * n_right + extra :]
    outs, (ordered, *wide) = rest[: 2 * len(sides)], rest[2 * len(sides) :]
    step = pl.program_id(0)
    blocks = lefts[0].shape[0] // rows
    half = blocks // 2 * rows

    @pl.when(step == 0)
    def _():
        start = 0
        for left in lefts:
            source, size = left, left.shape[1]
            if wide:
                source = wide[0].at[:, pl.ds(0, size)]
                source[...] = left[...].astype(jnp.float32)
            for side, order in enumerate(sides):
                bit = 1 - order
                for i in range(blocks):
                    low, high = i % (1 << bit), (i % (blocks // 2)) >> bit
                    mine = ids[2 - order] if i < blocks // 2 else 1 - ids[2 - order]
                    place = (high << (bit + 1)) + (mine << bit) + low
                    taken = source[pl.ds(pl.multiple_of(place * rows, rows), rows), :]
                    ordered[side, i * rows : (i + 1) * rows, start : start + size] = taken.astype(jnp.bfloat16)
            start += size

    steps = sum(s[-1] for s in spans)
    first = 0
    for mine, other, tokens, which, _, count in spans:
        for side in range(len(sides)):
            keep, send = outs[2 * side : 2 * side + 2]
            low = max(first, side * steps // len(sides))
            high = min(first + count, (side + 1) * steps // len(sides))
            if low >= high:
                continue

            @pl.when((step >= low) & (step < high))
            def _(mine=mine, other=other, tokens=tokens, which=which, side=side, keep=keep, send=send):
                total = dot(
                    ordered[side, :, mine : mine + tokens], rights[2 * which][:tokens, :], (1, 0)
                ) + dot(
                    ordered[side, :, other : other + tokens], rights[2 * which + 1][:tokens, :], (1, 0)
                )
                keep[...] = total[:half].astype(jnp.bfloat16)
                send[...] = total[half:].astype(jnp.bfloat16)

        first += count


def products(ids, lefts, rights, spans, rows, chunk, sides=(0, 1), after=()):
    height = lefts[0][0].shape[0]
    columns = sum(s[-1] for s in spans)
    steps = columns // chunk
    spans = [(*s[:-1], s[-1] // chunk) for s in spans]
    count = len(sides)
    part = jax.ShapeDtypeStruct((height // 2, columns // count), jnp.bfloat16)
    blocks = [
        pl.BlockSpec(
            (height // 2, chunk),
            lambda j, side=side: (0, jnp.clip(j - side * steps // count, 0, steps // count - 1)),
        )
        for side in range(count)
        for _ in range(2)
    ]
    tokens = sum(x[1] for x in lefts)
    wide = [pltpu.VMEM((height, max(x[1] for x in lefts)), jnp.float32)] if rows % 16 else []
    taken = [pl.BlockSpec((height, size), lambda j, place=place: (0, place)) for _, size, place in lefts]

    def place_of(which):
        def index(j):
            first, found = 0, []
            for _, _, _, w, row, count in spans:
                if w == which:
                    found.append((first, first + count, row))
                first += count
            first, end, row = found[-1]
            at_row, at_column = row, jnp.clip(j - first, 0, end - first - 1)
            for first, end, row in found[-2::-1]:
                at_row = jnp.where(j < end, row, at_row)
                at_column = jnp.where(j < end, jnp.clip(j - first, 0, end - first - 1), at_column)
            return at_row, at_column

        return index

    strips = [
        pl.BlockSpec((block, chunk), place_of(i)) for i, (_, _, block) in enumerate(rights) for _ in range(2)
    ]
    return pl.pallas_call(
        functools.partial(
            product_kernel,
            spans=spans,
            n_left=len(lefts),
            n_right=len(rights),
            rows=rows,
            chunk=chunk,
            extra=len(after),
            sides=sides,
        ),
        grid=(steps,),
        out_shape=(part,) * (2 * count),
        in_specs=[smem] + taken + strips + [anywhere] * len(after),
        out_specs=blocks,
        scratch_shapes=[pltpu.VMEM((count, height, tokens), jnp.bfloat16)] + wide,
        compiler_params=kernel_params(48),
        cost_estimate=cost(2.5 * height * tokens * columns / len(lefts), 20),
    )(ids, *[x[0] for x in lefts], *[x for right in rights for x in right[:2]], *after)


def exchange(values, bit):
    count = lax.axis_size(AXES)
    return lax.ppermute(values, AXES, [(i, i ^ (1 << bit)) for i in range(count)])


def place_kernel(*refs, slots, rows):
    me = lax.axis_index(AXES)
    pieces, out, sems = refs[: len(slots)], refs[-2], refs[-1]
    copies = []
    for piece, (start, order) in zip(pieces, slots):
        columns = pl.ds(start, piece.shape[-1])
        for i, slot in enumerate(order):
            place = pl.ds(pl.multiple_of((me ^ slot) * rows, rows), rows)
            copies.append(
                pltpu.make_async_copy(piece.at[i], out.at[place, columns], sems.at[len(copies)])
            )
    for copy in copies:
        copy.start()
    for copy in copies:
        copy.wait()


def join_kernel(*refs, count, split):
    parts, outs = refs[: 2 * count], refs[-(2 if split else count) :]
    for i in range(count):
        first = 0
        for part in parts[2 * i : 2 * i + 2]:
            rows = slice(first, first + part.shape[0])
            if split:
                outs[0][rows] = part[:, :, :split]
                outs[1][rows] = part[:, :, split:]
            else:
                outs[i][rows] = part[...]
            first += part.shape[0]


def pack_kernel(w_in, w_out, *refs):
    out = refs[-1]
    rows, width = w_in.shape[0], out.shape[1]
    count = w_in.shape[1] // width
    for i in range(count):
        out[i * rows : (i + 1) * rows, :] = w_in[:, i * width : (i + 1) * width]
    out[count * rows :, :] = w_out[...]


def pack_ffn(w_in, w_out, after):
    return pl.pallas_call(
        pack_kernel,
        out_shape=jax.ShapeDtypeStruct((2 * w_out.shape[0], w_out.shape[1]), jnp.bfloat16),
        in_specs=[vmem] * 2 + [anywhere] * len(after),
        out_specs=vmem,
        compiler_params=kernel_params(16),
        cost_estimate=cost(0, 1),
    )(w_in, w_out, *after)


class Gather:
    def __init__(self, local):
        self.rows, self.width = local.shape
        bits = lax.axis_size(AXES).bit_length() - 1
        self.half = self.width // 256 * 128
        high = [(b,) for b in range(bits - 1, 2, -1)]
        self.bits = high + [(2, 1), (1, 2), (0, 0)]
        self.count = len(high)
        self.values, self.order, self.stage = [local[None]], [[0]], 0
        self.send()

    def send(self):
        self.arrived = [exchange(v, b) for v, b in zip(self.values, self.bits[self.stage])]

    def step(self, after=()):
        self.order = [
            order + [i ^ (1 << b) for i in order] for order, b in zip(self.order, self.bits[self.stage])
        ]
        self.stage += 1
        split = self.half if self.stage == self.count else 0
        slots, columns = 2 * self.values[0].shape[0], [v.shape[-1] for v in self.values]
        if split:
            self.order = self.order * 2
            columns = [split, self.width - split]
        parts = [x for pair in zip(self.values, self.arrived) for x in pair]
        self.values = pl.pallas_call(
            functools.partial(join_kernel, count=len(self.values), split=split),
            out_shape=[jax.ShapeDtypeStruct((slots, self.rows, n), jnp.bfloat16) for n in columns],
            in_specs=[vmem] * len(parts) + [anywhere] * len(after),
            out_specs=[vmem] * len(columns),
            compiler_params=kernel_params(32),
            cost_estimate=cost(0, 4 * slots * self.rows * self.width / 2**20),
        )(*parts, *after)
        self.send()
        return self.values[:1]

    def place(self, after=()):
        pieces = [x for pair in zip(self.values, self.arrived) for x in pair]
        slots = []
        for start, order in zip((0, self.half), self.order):
            slots += [(start, order), (start, [i ^ 1 for i in order])]
        count = lax.axis_size(AXES)
        return pl.pallas_call(
            functools.partial(place_kernel, slots=slots, rows=self.rows),
            out_shape=jax.ShapeDtypeStruct((count * self.rows, self.width), jnp.bfloat16),
            in_specs=[anywhere] * (len(pieces) + len(after)),
            out_specs=anywhere,
            scratch_shapes=[pltpu.SemaphoreType.DMA((2 * count,))],
            compiler_params=kernel_params(16),
            cost_estimate=cost(0, 4 * count * self.rows * self.width / 2**20),
        )(*pieces, *after)


def stage_kernel(ids, *refs, groups, extra):
    inputs = refs[: 2 * sum(count for _, count in groups)]
    outputs = refs[len(inputs) + extra :]
    for g, (bit, count) in enumerate(groups):
        send, keep = outputs[2 * g : 2 * g + 2]
        mine, rows = ids[bit], send.shape[1]
        start = 0
        for _ in range(count):
            left, right, *inputs = inputs
            for j in range(left.shape[2] // rows):
                columns, block = slice(start, start + left.shape[-1]), slice(j * rows, (j + 1) * rows)
                for i in range(left.shape[0]):
                    for out, b in ((send, 1 - mine), (keep, mine)):
                        total = left[i, b, block].astype(jnp.float32) + right[i, b, block].astype(jnp.float32)
                        out[i, :, columns] = total.astype(jnp.bfloat16)
                start += left.shape[-1]


class Chain:
    def __init__(self, ids, parts, rows, sides=(0, 1)):
        self.ids, self.rows = ids, rows
        self.rest = list(range(3, ids.shape[0]))
        self.sends = parts[1::2]
        self.next = [(1, 2)[side] for side in sides]
        self.groups = [
            [(keep, exchange(send, (2, 1)[side]), rows)]
            for keep, send, side in zip(parts[::2], parts[1::2], sides)
        ]

    def arrived(self):
        return [part[1] for group in self.groups for part in group]

    def advance(self, groups, bits, after):
        shaped, shapes = [], []
        for group in groups:
            columns = 0
            for keep, arrived, rows in group:
                shaped += [x.reshape(-1, 2, rows, x.shape[-1]) for x in (keep, arrived)]
                columns += keep.shape[-1] * rows // self.rows
            shapes += [jax.ShapeDtypeStruct((shaped[-1].shape[0], self.rows, columns), jnp.bfloat16)] * 2
        outs = pl.pallas_call(
            functools.partial(
                stage_kernel, groups=[(b, len(g)) for b, g in zip(bits, groups)], extra=len(after)
            ),
            out_shape=shapes,
            in_specs=[smem] + [vmem] * len(shaped) + [anywhere] * len(after),
            out_specs=[vmem] * len(shapes),
            compiler_params=kernel_params(32),
            cost_estimate=cost(0, sum(3 * x.size for x in shaped) / 2**20),
        )(self.ids, *shaped, *after)
        self.groups = [
            [(keep, exchange(send, b), self.rows)] for send, keep, b in zip(outs[::2], outs[1::2], bits)
        ]
        return outs[1::2]

    def join(self, other):
        self.rows = other.rows
        self.groups = [[part for chain in (self, other) for group in chain.groups for part in group]]

    def second(self, after=()):
        return self.advance(self.groups, self.next, after)

    def third(self, after=()):
        self.groups = [[part for group in self.groups for part in group]]
        return self.advance(self.groups, [self.rest.pop(0)], after)

    def finish(self):
        [[(keep, arrived, _)]] = self.groups
        return (keep.astype(jnp.float32) + arrived.astype(jnp.float32))[0]


def small_kernel(*refs, rows, count, owned):
    sums, bias, out = refs[:count], refs[count], refs[-1]
    lines = [sums[i][row : row + 1] for i, row in rows]
    lines += [jnp.zeros_like(lines[0])] * (128 - len(lines))
    out[:, :128] = jnp.concatenate(lines, axis=0).T
    out[:, 128:] = jnp.zeros((out.shape[0], 128), jnp.float32)
    for i in range(bias.shape[0]):
        out[i * owned : i * owned + 1, 128:] = bias[i : i + 1]


def small_block(lines, sums, bias, owned, after):
    width = sums[0].shape[1]
    devices = width // owned
    bias = bias.reshape(devices, -1)
    bias = jnp.pad(bias, ((0, 0), (0, 128 - bias.shape[1])))
    places = [([i for i, x in enumerate(sums) if x is s][0], row) for s, row in lines]
    block = pl.pallas_call(
        functools.partial(small_kernel, rows=places, count=len(sums), owned=owned),
        out_shape=jax.ShapeDtypeStruct((width, 256), jnp.float32),
        in_specs=[vmem] * (len(sums) + 1) + [anywhere] * len(after),
        out_specs=vmem,
        compiler_params=kernel_params(16),
        cost_estimate=cost(0, 2),
    )(*sums, bias, *after)
    return block.astype(jnp.bfloat16)


def add_product_kernel(*refs, count, base, extra):
    out = refs[-1]
    total = refs[2 * count][...] if base else jnp.zeros(out.shape, jnp.float32)
    for left, right in zip(refs[:count], refs[count : 2 * count]):
        total += dot(left[...], right[...], (1, 1))
    out[...] = total


def add_product(stack, places, weights, columns, rows, chunk, base=None, after=()):
    width = stack.shape[1]
    count = len(places)
    bases = [] if base is None else [base]
    block = pl.BlockSpec((chunk, width), lambda i: (i, 0))
    return pl.pallas_call(
        functools.partial(add_product_kernel, count=count, base=len(bases), extra=len(after)),
        grid=(rows // chunk,),
        out_shape=jax.ShapeDtypeStruct((rows, width), jnp.float32),
        in_specs=[pl.BlockSpec((chunk, width), lambda i, p=p: (p // chunk + i, 0)) for p in places]
        + [pl.BlockSpec((width, width), lambda i, c=c: (0, c)) for c in columns]
        + [block] * len(bases)
        + [anywhere] * len(after),
        out_specs=block,
        compiler_params=kernel_params(40),
        cost_estimate=cost(0, 0.001),
    )(*[stack] * count, *[weights] * count, *bases, *after)


def body(
    target_in,
    memory,
    block_rows,
    pad_rows,
    seq_lengths,
    self_qkv,
    self_out,
    cross_query,
    cross_kv,
    cross_out,
    ffn_in,
    ffn_out,
    norm_scale,
    small_bias,
    ffn_bias,
    cotangent,
):
    width = target_in.shape[1]
    owned = self_qkv.shape[0]
    me = lax.axis_index(AXES)
    core = (me & 1).reshape(1)
    ids = (me >> jnp.arange(lax.axis_size(AXES).bit_length() - 1)) & 1
    tokens, mems = target_in.shape[0], memory.shape[0]

    def turned(*arrays, after=()):
        keep, send = turn(core, arrays, owned, after)
        return keep, exchange(send, 0)

    pack = jnp.concatenate([norm_scale.T, small_bias.T, ffn_bias.reshape(owned, -1)], axis=1)
    small_cols = pack.shape[1]
    pack = jnp.pad(pack, ((0, 0), (0, -small_cols % 128)))
    early = Gather(jnp.concatenate([self_qkv, self_out, cross_query, pack], axis=1))
    late = Gather(jnp.concatenate([cross_kv, cross_out], axis=1))
    memory_turned = turned(memory)
    target_turned = turned(target_in, after=memory_turned[:1])
    last = target_turned[:1]
    for _ in range(early.count + 2):
        last = early.step(last)
        if early.stage == early.count:
            packed = lax.all_gather(pack_ffn(ffn_in, ffn_out, last), AXES)
        if early.stage < early.count + 2:
            last = late.step(last)
    early = early.place(last)

    w_qkv, w_self, w_query = early[:, : 3 * width], early[:, 3 * width : 4 * width], early[:, 4 * width : 5 * width]
    small = early[:, 5 * width : 5 * width + small_cols].astype(jnp.float32)
    gains = small[:, :3].T
    biases = small[:, 3:13].T
    in_bias = small[:, 13:].reshape(1, -1)

    bound = memory_bounds(block_rows[0], pad_rows[0])
    lengths = seq_lengths[0]
    zeros = jnp.zeros((width,), jnp.float32)
    qkv = (matmul(target_in, w_qkv) + jnp.concatenate([biases[0], zeros, biases[1]])).astype(
        jnp.bfloat16
    )
    self_context, self_summary = self_forward(lengths, qkv)
    first, first_unit, first_inverse = normalize(
        target_in.astype(jnp.float32) + matmul(self_context, w_self) + biases[2],
        gains[0],
        biases[7],
    )
    first_low = first.astype(jnp.bfloat16)
    self_turned = turned(self_context, first_low)
    cross_q = (matmul(first_low, w_query) + biases[3]).astype(jnp.bfloat16)
    late.step((cross_q, self_turned[0]))
    late = late.place()
    w_pairs, w_cross = late[:, : 2 * width], late[:, 2 * width :]
    cross_pairs = (matmul(memory, w_pairs) + jnp.concatenate([zeros, biases[4]])).astype(
        jnp.bfloat16
    )
    cross_context, cross_summary = cross_forward(bound, cross_q, cross_pairs)
    second, second_unit, second_inverse = normalize(
        first + matmul(cross_context, w_cross) + biases[5], gains[1], biases[8]
    )

    cross_turned = turned(cross_context, second)
    vectors = jnp.concatenate([biases[6:7], gains[2:3], biases[9:10], jnp.zeros((5, width), jnp.float32)])
    hidden, hidden_send, slope, block_out, third_grad, out_grad, third_sums = ffn_forward(
        core,
        second,
        packed,
        in_bias,
        cotangent,
        vectors,
        ffn_out.shape[0],
        after=(memory_turned[1], target_turned[1]),
    )
    hidden_other, out_grad_other = exchange(hidden_send, 0), exchange(out_grad, 0)
    pre_grad, ffn_bias_grad, second_grad, cross_branch, second_sums = ffn_backward(
        packed, slope, third_grad, out_grad, second_unit, second_inverse, gains[1:2], (cross_turned[1], out_grad_other)
    )
    pre_grad_other = exchange(pre_grad, 0)
    parts = products(
        ids,
        [(hidden, tokens, 0), (hidden_other, tokens, 0)],
        [(out_grad, out_grad_other, tokens)],
        [(0, tokens, tokens, 0, 0, width)],
        ffn_out.shape[0],
        512,
        sides=(0,),
        after=(pre_grad,),
    )
    out_chain = Chain(ids, parts, ffn_out.shape[0], sides=(0,))
    parts = products(
        ids,
        [(x, tokens, 1) for x in cross_turned],
        [(pre_grad, pre_grad_other, tokens)],
        [(0, tokens, tokens, 0, 0, ffn_in.shape[1])],
        owned,
        1024,
        sides=(1,),
        after=out_chain.sends,
    )
    in_chain = Chain(ids, parts, owned, sides=(1,))

    cross_delta, cross_sums = cross_backward(
        bound, cross_q, cross_pairs, cross_summary, cross_branch, late, 2, after=in_chain.sends
    )
    cross_other = exchange(cross_delta, 0)
    self_delta, self_sums, first_grad = self_backward(
        lengths,
        qkv,
        self_summary,
        second_grad,
        cross_delta,
        early,
        first_unit,
        first_inverse,
        gains[0:1],
    )
    self_other = exchange(self_delta, 0)
    small_grad = small_block(
        [
            (self_sums, 3),
            (second_sums, 0),
            (third_sums, 0),
            (self_sums, 0),
            (self_sums, 1),
            (self_sums, 2),
            (cross_sums, 0),
            (cross_sums, 1),
            (second_sums, 2),
            (third_sums, 2),
            (self_sums, 4),
            (second_sums, 1),
            (third_sums, 1),
        ],
        [self_sums, cross_sums, second_sums, third_sums],
        ffn_bias_grad,
        owned,
        (self_sums,),
    )
    bits = list(range(lax.axis_size(AXES).bit_length() - 1))[::-1]
    small_part = small_grad.reshape((2,) * len(bits) + (owned, -1))
    for bit in (0, 1):
        mine = (me >> bit) & 1
        small_keep, small_send = [
            lax.dynamic_index_in_dim(small_part, i, bits.index(bit), keepdims=False)
            for i in (mine, 1 - mine)
        ]
        small_other = exchange(small_send, bit)
        small_part = (small_keep.astype(jnp.float32) + small_other.astype(jnp.float32)).astype(jnp.bfloat16)
        bits.remove(bit)
    beyond = mems + 2 * tokens
    parts = products(
        ids,
        [
            part
            for i in range(2)
            for part in (
                (memory_turned[i], mems, 0),
                (self_turned[i], tokens, 1),
                (cross_turned[i], tokens, 0),
            )
        ],
        [(cross_delta, cross_other, mems), (cross_delta, cross_other, mems // 2)],
        [
            (mems, beyond + mems, tokens, 1, 4, width),
            (0, beyond, mems, 0, 0, width),
            (0, beyond, mems, 0, 1, width),
            (mems + tokens, beyond + mems + tokens, tokens, 1, 5, width),
        ],
        owned,
        1024,
        after=in_chain.second(after=out_chain.second(after=(small_grad,))),
    )
    cross_chain = Chain(ids, parts, owned)
    parts = products(
        ids,
        [part for i in range(2) for part in ((target_turned[i], tokens, 0), (self_turned[i], tokens, 0))],
        [(self_delta, self_other, tokens)],
        [(0, 2 * tokens, tokens, 0, i, width) for i in range(3)]
        + [(tokens, 3 * tokens, tokens, 0, 3, width)],
        owned,
        1024,
        after=(parts[0], small_other),
    )
    self_chain = Chain(ids, parts, owned)
    self_chain.groups[1].append((small_keep, small_other, owned))
    out_chain.join(in_chain)
    last = out_chain.third(after=parts[:1])
    last = cross_chain.second(after=last)
    memory_grad = add_product(cross_delta, [0, mems], late, [0, 1], mems, 512, after=last)
    last = (memory_grad,)
    while out_chain.rest:
        last = out_chain.third(after=last)
    last = self_chain.second(after=last)
    target_grad = add_product(
        self_delta,
        [0, tokens, 2 * tokens],
        early,
        [0, 1, 2],
        tokens,
        tokens,
        first_grad,
        after=last,
    )
    last = (target_grad,)
    last = cross_chain.third(after=last)
    last = self_chain.third(after=last)
    while self_chain.rest:
        last = cross_chain.third(after=last)
        last = self_chain.third(after=last)
    ffn_shard = out_chain.finish()
    size = ffn_in.shape[1]
    ffn_out_shard = ffn_shard[:, :size].reshape(owned, -1, width).swapaxes(0, 1).reshape(ffn_out.shape)
    ffn_in_shard = ffn_shard[:, size:]
    cross_shard = cross_chain.finish()
    self_shard = self_chain.finish()
    small_shard = self_shard[:, 4 * width :]
    return (
        block_out,
        target_grad,
        memory_grad,
        self_shard[:, : 3 * width],
        self_shard[:, 3 * width : 4 * width],
        cross_shard[:, :width],
        cross_shard[:, width : 3 * width],
        cross_shard[:, 3 * width :],
        ffn_in_shard,
        ffn_out_shard,
        small_shard[:, :3].T,
        small_shard[:, 3:13].T,
        small_shard[0, 128 : 128 + ffn_bias.shape[0]],
    )


def solution(mesh):
    in_specs = (
        P(("wide", "narrow"), None),
        P(("wide", "narrow"), None),
        P(("wide", "narrow"), None),
        P(("wide", "narrow"), None),
        P(("wide", "narrow"), None),
        P(("wide", "narrow"), None),
        P(("wide", "narrow"), None),
        P(("wide", "narrow"), None),
        P(("wide", "narrow"), None),
        P(("wide", "narrow"), None),
        P(("wide", "narrow"), None),
        P(("wide", "narrow"), None),
        P(None, ("wide", "narrow")),
        P(None, ("wide", "narrow")),
        P(("wide", "narrow")),
        P(("wide", "narrow"), None),
    )
    out_specs = (
        P(("wide", "narrow"), None),
        P(("wide", "narrow"), None),
        P(("wide", "narrow"), None),
        P(("wide", "narrow"), None),
        P(("wide", "narrow"), None),
        P(("wide", "narrow"), None),
        P(("wide", "narrow"), None),
        P(("wide", "narrow"), None),
        P(("wide", "narrow"), None),
        P(("wide", "narrow"), None),
        P(None, ("wide", "narrow")),
        P(None, ("wide", "narrow")),
        P(("wide", "narrow")),
    )
    return jax.shard_map(body, mesh=mesh, in_specs=in_specs, out_specs=out_specs, check_vma=False)
```
